256 devices in a mesh: cell: 8 (over x, z_hi), dom: 32 (over y, z_lo, core).
Axes of the slice: x: 4, y: 4, z: 8 (z_hi: 2, z_lo: 4; z = z_hi * 4 + z_lo), core: 2. Of those that a mesh axis runs over, the one named last changes fastest.
Arguments:
- feats: bfloat16 [8, 4096, 128], P('cell', 'dom'), may hold values from -6 to 6
- positions: float32 [8, 3, 4096], P('cell', None, 'dom'), may hold values from 0 to 1
- species: int32 [8, 4096], P('cell', 'dom'), may hold values from 0 to 7
- wave_vectors: int32 [3, 2048], replicated, may hold values from -8 to 8, as said below
- smearing: float32 [128], replicated, may hold values from 0.001 to 0.03
- species_gain: float32 [8, 128], replicated, may hold values from 0.5 to 1.5
- w_charge: bfloat16 [128, 128], replicated, may hold values from -0.5 to 0.5
- w_message: bfloat16 [128, 128], replicated, may hold values from -0.5 to 0.5
- w_radial: float32 [8, 128], replicated, may hold values from -2 to 2
- w_out: bfloat16 [128, 128], replicated, may hold values from -0.5 to 0.5
- edge_sender: int32 [8, 393216], P('cell', 'dom'), may hold values from 0 to 191
- edge_receiver: int32 [8, 393216], P('cell', 'dom'), may hold values from 0 to 127
- edge_mask: int32 [8, 393216], P('cell', 'dom'), may hold values 0 or 1
- edge_length: float32 [8, 393216], P('cell', 'dom'), may hold values from 0.8 to 5.8
- ghost_down: int32 [8, 1024], P('cell', 'dom'), may hold values from 0 to 127
- ghost_up: int32 [8, 1024], P('cell', 'dom'), may hold values from 0 to 127
- cotangent: bfloat16 [8, 4096, 128], P('cell', 'dom'), may hold values from -6 to 6
Outputs:
- updated: bfloat16 [8, 4096, 128], P('cell', 'dom')
- feat_grad: bfloat16 [8, 4096, 128], P('cell', 'dom')
- grad_charge: float32 [128, 128], replicated
- grad_message: float32 [128, 128], replicated
- grad_radial: float32 [8, 128], replicated
- grad_out: float32 [128, 128], replicated
The draws below stay inside these ranges and needn't reach their ends.
Inputs may be any that keep to these rules, and one draw needn't show every extreme that they name: `wave_vectors`: every column is a nonzero integer triple. `edge_sender`: rows below 128 are the domain's own atoms, then 32 rows from below, then 32 from above. `edge_receiver`: local row within the domain. `ghost_down`: local row within the sending domain; rows may repeat. `ghost_up`: local row within the sending domain; rows may repeat.
All inputs are finite; a program needn't handle non-finite values. No bound on the sum of `edge_mask` on one device may be relied on, other than what follows from the above.
Results may differ from the reference program's by a relative error of at most 0.01.
Values may be sent and summed in bfloat16 or wider, within the bound.
No kernel may reach another device: no remote copies, remote signals or barrier semaphores. Data moves between devices by JAX's collectives and lax.ppermute only.
A program may use at most 64 MiB of HBM per device.

```python
import math
import jax
import jax.numpy as jnp
from jax import lax

C = 128
K = 2048
NB = 8
SPECIES = 8
ATOMS_DEV = 128
GHOST = 32
EDGES_DEV = 12288
ATOMS = 4096
GHOSTS = 1024
EDGES = 393216
CELLS = 8
N_DOM = 32


def draw_wave_vectors(key, part):
    key = jax.random.fold_in(key, 11)
    lattice = jax.random.randint(key, (3, K), -8, 9)
    vanish = jnp.all(lattice == 0, axis=0)
    first = jnp.where(vanish, 1, lattice[0])
    return lattice.at[0].set(first).astype(jnp.int32)


def set_ends(values, key, smallest, largest):
    place = [jax.random.randint(jax.random.fold_in(key, axis), (), 0, length) for axis, length in enumerate(values.shape)]
    main_axis = values.shape.index(max(values.shape))
    beside = place[:main_axis] + [(place[main_axis] + 1) % values.shape[main_axis]] + place[main_axis + 1:]
    return values.at[tuple(place)].set(smallest).at[tuple(beside)].set(largest)


def block_levels(own_key, extent, pieces, low, high):
    loudness = 1.0
    for axis_at, parts in pieces:
        draws = jax.random.uniform(jax.random.fold_in(jax.random.fold_in(own_key, 6), axis_at), (parts,), jnp.float32, low / len(pieces), high / len(pieces))
        loudness = loudness * jnp.repeat(jnp.exp(draws), extent[axis_at] // parts).reshape((-1,) + (1,) * (len(extent) - 1 - axis_at))
    return loudness


def scatter_about(own_key, extent, deviation, bound, shards=(), kind=jnp.bfloat16):
    drawn = jax.random.normal(own_key, extent, jnp.float32) * deviation
    if len(shards) > 0:
        drawn = block_levels(own_key, extent, shards, -0.22, 0.18) * drawn
    return jnp.clip(drawn, min=-bound, max=bound).astype(kind)


def setup_inputs(seed: int = 0) -> dict:
    key_of = jax.random.split(jax.random.key(seed), 18)
    return {
        "feats": scatter_about(key_of[0], (CELLS, ATOMS, C), 1.0, 6.0, ((0, 8), (1, 32))),
        "positions": jnp.clip(1.0 * jax.random.uniform(key_of[1], (CELLS, 3, ATOMS), jnp.float32) ** block_levels(key_of[1], (CELLS, 3, ATOMS), ((0, 8), (2, 32)), -0.2, 0.2), 0.0, 1.0),
        "species": set_ends(jax.random.randint(key_of[2], (CELLS, ATOMS), 0, SPECIES), jax.random.fold_in(key_of[2], 1), 0, SPECIES - 1).astype(jnp.int32),
        "wave_vectors": draw_wave_vectors(jax.random.fold_in(key_of[17], 71), 0),
        "smearing": jnp.clip(jnp.exp(jax.random.uniform(key_of[4], (C,), jnp.float32, math.log(0.001), math.log(0.03))), 0.001, 0.03),
        "species_gain": jnp.clip(jax.random.uniform(key_of[5], (SPECIES, C), jnp.float32, 0.5, 1.5), 0.5, 1.5),
        "w_charge": scatter_about(key_of[6], (C, C), C ** -0.5, 0.5),
        "w_message": scatter_about(key_of[7], (C, C), C ** -0.5, 0.5),
        "w_radial": scatter_about(key_of[8], (NB, C), NB ** -0.5, 2.0, (), jnp.float32),
        "w_out": scatter_about(key_of[9], (C, C), C ** -0.5, 0.5),
        "edge_sender": set_ends(jax.random.randint(key_of[10], (CELLS, EDGES), 0, ATOMS_DEV + 2 * GHOST), jax.random.fold_in(key_of[10], 1), 0, (ATOMS_DEV + 2 * GHOST) - 1).astype(jnp.int32),
        "edge_receiver": set_ends(jax.random.randint(key_of[11], (CELLS, EDGES), 0, ATOMS_DEV), jax.random.fold_in(key_of[11], 1), 0, ATOMS_DEV - 1).astype(jnp.int32),
        "edge_mask": set_ends((jax.random.randint(key_of[12], (CELLS, EDGES), 0, 8) < 7).astype(jnp.int32), jax.random.fold_in(key_of[12], 1), 0, 1),
        "edge_length": jnp.clip(0.8 + 5 * jax.random.uniform(key_of[13], (CELLS, EDGES), jnp.float32) ** block_levels(key_of[13], (CELLS, EDGES), ((0, 8), (1, 32)), -0.2, 0.2), 0.8, 5.8),
        "ghost_down": set_ends(jax.random.randint(key_of[14], (CELLS, GHOSTS), 0, ATOMS_DEV), jax.random.fold_in(key_of[14], 1), 0, ATOMS_DEV - 1).astype(jnp.int32),
        "ghost_up": set_ends(jax.random.randint(key_of[15], (CELLS, GHOSTS), 0, ATOMS_DEV), jax.random.fold_in(key_of[15], 1), 0, ATOMS_DEV - 1).astype(jnp.int32),
        "cotangent": scatter_about(key_of[16], (CELLS, ATOMS, C), 1.0, 6.0, ((0, 8), (1, 32))),
    }


cutoff_radius = 6.0
basis_width = 0.75
edge_scale = 0.25
filter_factor = 12.0

def phase_tables(coords, wave_vectors):
    waves = wave_vectors.astype(jnp.float32)
    theta = coords[0][:, None] * waves[0][None, :] + coords[1][:, None] * waves[1][None, :] + coords[2][:, None] * waves[2][None, :]
    theta = 2.0 * math.pi * theta
    return (jnp.cos(theta).astype(jnp.bfloat16), jnp.sin(theta).astype(jnp.bfloat16))

def filter_table(wave_vectors, smearing):
    waves = wave_vectors.astype(jnp.float32)
    squared = lax.optimization_barrier(jnp.sum(waves * waves, axis=0))
    return filter_factor * jnp.exp(-squared[:, None] * smearing[None, :]) / jnp.sqrt(squared)[:, None]

def radial_terms(lengths, w_radial):
    centers = 0.5 + basis_width * jnp.arange(w_radial.shape[0]).astype(jnp.float32)
    basis = jnp.exp(-jnp.square((lengths[:, None] - centers[None, :]) / basis_width))
    envelope = 0.5 * (jnp.cos(math.pi * lengths / cutoff_radius) + 1.0)
    radial = envelope[:, None] * jnp.dot(basis, w_radial, precision=lax.Precision.HIGHEST)
    return (basis, envelope, radial)

def reference(feats, positions, species, wave_vectors, smearing, species_gain, w_charge, w_message, w_radial, w_out, edge_sender, edge_receiver, edge_mask, edge_length, ghost_down, ghost_up, cotangent):
    inv_atoms = 1.0 / math.sqrt(ATOMS)
    inv_waves = 1.0 / math.sqrt(K)
    filt = filter_table(wave_vectors, smearing)

    def take_rows(rows, index):
        return rows[index]

    def one_cell(packed):
        cell_feats, coords, kinds, senders, receivers, masks, lengths, downs, ups, cell_cot = packed
        gain = species_gain[kinds]
        charges = (jnp.dot(cell_feats, w_charge, preferred_element_type=jnp.float32) * gain).astype(jnp.bfloat16)
        coord_blocks = coords.reshape(3, N_DOM, ATOMS_DEV).transpose(1, 0, 2)
        charge_blocks = charges.reshape(N_DOM, ATOMS_DEV, C)

        def structure_block(block):
            coord, values = block
            cos_table, sin_table = phase_tables(coord, wave_vectors)
            return (jnp.dot(cos_table.T, values, preferred_element_type=jnp.float32), jnp.dot(sin_table.T, values, preferred_element_type=jnp.float32))
        parts_re, parts_im = lax.map(structure_block, (coord_blocks, charge_blocks))
        field_re = (filt * lax.optimization_barrier(jnp.sum(parts_re, axis=0)) * inv_atoms).astype(jnp.bfloat16)
        field_im = (filt * lax.optimization_barrier(jnp.sum(parts_im, axis=0)) * inv_atoms).astype(jnp.bfloat16)

        def potential_block(coord):
            cos_table, sin_table = phase_tables(coord, wave_vectors)
            total = jnp.dot(cos_table, field_re, preferred_element_type=jnp.float32) + jnp.dot(sin_table, field_im, preferred_element_type=jnp.float32)
            return total * inv_waves
        potential = lax.map(potential_block, coord_blocks).reshape(ATOMS, C)
        feat_blocks = cell_feats.reshape(N_DOM, ATOMS_DEV, C)
        down_blocks = downs.reshape(N_DOM, GHOST)
        up_blocks = ups.reshape(N_DOM, GHOST)
        sent_down = jax.vmap(take_rows)(feat_blocks, down_blocks)
        sent_up = jax.vmap(take_rows)(feat_blocks, up_blocks)
        from_below = jnp.roll(sent_up, 1, axis=0)
        from_above = jnp.roll(sent_down, -1, axis=0)
        extended = jnp.concatenate([feat_blocks, from_below, from_above], axis=1)
        edge_blocks = (extended, senders.reshape(N_DOM, EDGES_DEV), receivers.reshape(N_DOM, EDGES_DEV), masks.reshape(N_DOM, EDGES_DEV), lengths.reshape(N_DOM, EDGES_DEV))

        def edge_block(block):
            rows, send, recv, live, length = block
            message_rows = jnp.dot(rows, w_message, preferred_element_type=jnp.float32).astype(jnp.bfloat16)
            basis, envelope, radial = radial_terms(length, w_radial)
            picked = message_rows[send].astype(jnp.float32)
            messages = live.astype(jnp.float32)[:, None] * radial * picked
            return jnp.zeros((ATOMS_DEV, C), jnp.float32).at[recv].add(messages) * edge_scale
        aggregate = lax.map(edge_block, edge_blocks).reshape(ATOMS, C)
        preact = aggregate + potential
        act = jax.nn.silu(preact).astype(jnp.bfloat16)
        updated = (cell_feats.astype(jnp.float32) + jnp.dot(act, w_out, preferred_element_type=jnp.float32)).astype(jnp.bfloat16)
        grad_act = jnp.dot(cell_cot, w_out.T, preferred_element_type=jnp.float32)
        sig = jax.nn.sigmoid(preact)
        grad_pre = grad_act * sig * (1.0 + preact * (1.0 - sig))
        grad_pre_b = grad_pre.astype(jnp.bfloat16)
        grad_out = jnp.dot(act.T, cell_cot, preferred_element_type=jnp.float32)
        back_re, back_im = lax.map(structure_block, (coord_blocks, grad_pre_b.reshape(N_DOM, ATOMS_DEV, C)))
        dfield_re = (filt * lax.optimization_barrier(jnp.sum(back_re, axis=0)) * (inv_waves * inv_atoms)).astype(jnp.bfloat16)
        dfield_im = (filt * lax.optimization_barrier(jnp.sum(back_im, axis=0)) * (inv_waves * inv_atoms)).astype(jnp.bfloat16)

        def charge_block(coord):
            cos_table, sin_table = phase_tables(coord, wave_vectors)
            return jnp.dot(cos_table, dfield_re, preferred_element_type=jnp.float32) + jnp.dot(sin_table, dfield_im, preferred_element_type=jnp.float32)
        grad_charges = lax.map(charge_block, coord_blocks).reshape(ATOMS, C)
        grad_raw = (grad_charges * gain).astype(jnp.bfloat16)
        grad_charge = jnp.dot(cell_feats.T, grad_raw, preferred_element_type=jnp.float32)
        feat_from_charge = jnp.dot(grad_raw, w_charge.T, preferred_element_type=jnp.float32)

        def edge_back(block):
            rows, send, recv, live, length, upper = block
            message_rows = jnp.dot(rows, w_message, preferred_element_type=jnp.float32).astype(jnp.bfloat16)
            basis, envelope, radial = radial_terms(length, w_radial)
            picked = message_rows[send].astype(jnp.float32)
            livef = live.astype(jnp.float32)[:, None]
            upstream = upper[recv] * edge_scale
            grad_picked = livef * radial * upstream
            grad_radial_edge = livef * picked * upstream
            grad_msg = jnp.zeros((ATOMS_DEV + 2 * GHOST, C), jnp.float32).at[send].add(grad_picked).astype(jnp.bfloat16)
            part_message = jnp.dot(rows.T, grad_msg, preferred_element_type=jnp.float32)
            grad_rows = jnp.dot(grad_msg, w_message.T, preferred_element_type=jnp.float32)
            part_radial = jnp.dot(basis.T, envelope[:, None] * grad_radial_edge, precision=lax.Precision.HIGHEST)
            return (grad_rows, part_message, part_radial)
        grad_rows, parts_message, parts_radial = lax.map(edge_back, edge_blocks + (grad_pre.reshape(N_DOM, ATOMS_DEV, C),))
        back_below = grad_rows[:, ATOMS_DEV:ATOMS_DEV + GHOST]
        back_above = grad_rows[:, ATOMS_DEV + GHOST:]
        to_down = jnp.roll(back_above, 1, axis=0)
        to_up = jnp.roll(back_below, -1, axis=0)
        own_total = (cell_cot.astype(jnp.float32) + feat_from_charge).reshape(N_DOM, ATOMS_DEV, C) + grad_rows[:, :ATOMS_DEV]

        def add_back(total, down_index, up_index, down_rows, up_rows):
            return total.at[down_index].add(down_rows).at[up_index].add(up_rows)
        own_total = jax.vmap(add_back)(own_total, down_blocks, up_blocks, to_down, to_up)
        feat_grad = own_total.reshape(ATOMS, C).astype(jnp.bfloat16)
        return (updated, feat_grad, grad_charge, lax.optimization_barrier(jnp.sum(parts_message, axis=0)), lax.optimization_barrier(jnp.sum(parts_radial, axis=0)), grad_out)
    results = lax.map(one_cell, (feats, positions, species, edge_sender, edge_receiver, edge_mask, edge_length, ghost_down, ghost_up, cotangent))
    scale = 1.0 / math.sqrt(CELLS * ATOMS)
    return (results[0], results[1], lax.optimization_barrier(jnp.sum(results[2], axis=0)) * scale, lax.optimization_barrier(jnp.sum(results[3], axis=0)) * scale, lax.optimization_barrier(jnp.sum(results[4], axis=0)) * scale, lax.optimization_barrier(jnp.sum(results[5], axis=0)) * scale)
```

```python
import functools
import math

import jax
import jax.numpy as jnp
from jax import lax
from jax.experimental import pallas as pl
from jax.experimental.pallas import tpu as pltpu
from jax.sharding import PartitionSpec as P

bf16 = jnp.bfloat16
f32 = jnp.float32

C = 128
K = 2048
NB = 8
ATOMS = 128
GHOST = 32
EXT = ATOMS + 2 * GHOST
EDGES = 12288
DOMS = 32
CELLS = 8
ROW = 8
KB = K // ROW
PACK = ATOMS + 16
GROWS = 3 * C + 16
CHUNK = 1024

cutoff_radius = 6.0
basis_width = 0.75
edge_scale = 0.25
filter_factor = 12.0
inv_waves = 1.0 / math.sqrt(K)
inv_atoms = 1.0 / math.sqrt(ATOMS * DOMS)
grad_scale = 1.0 / math.sqrt(CELLS * ATOMS * DOMS)

COS_TURN = (
    0.9999999890754399,
    -19.73920450099313,
    64.93911749956553,
    -85.45013994347214,
    60.16763282514798,
    -25.967602441408868,
    6.528658639370483,
)
SIN_TURN = (
    6.283184916984331,
    -41.34158926418157,
    81.59994386455666,
    -76.61447586020026,
    41.342889428722025,
    -12.471244745942547,
)


def horner(coefficients, x):
    total = jnp.full_like(x, coefficients[-1])
    for value in coefficients[-2::-1]:
        total = total * x + value
    return total


def iota(shape, axis):
    return lax.broadcasted_iota(jnp.int32, shape, axis)


def dot(left, right):
    return jnp.dot(left, right, preferred_element_type=f32)


def dot_rows(left, right):
    return lax.dot_general(left, right, (((0,), (0,)), ((), ())), preferred_element_type=f32)


def dot_lanes(left, right):
    return lax.dot_general(left, right, (((1,), (1,)), ((), ())), preferred_element_type=f32)


def split(values):
    high = values.astype(bf16)
    return high, (values - high.astype(f32)).astype(bf16)


def call(kernel, outs, *args, scratch=(), flops=0, grid=None, in_specs=None, out_specs=None, name=None):
    more = {}
    if grid is not None:
        more = {"grid": grid, "in_specs": in_specs, "out_specs": out_specs}
    return pl.pallas_call(
        kernel,
        out_shape=[jax.ShapeDtypeStruct(shape, dtype) for shape, dtype in outs],
        scratch_shapes=list(scratch),
        compiler_params=pltpu.CompilerParams(vmem_limit_bytes=40 * 1024 * 1024),
        name=name,
        **more,
    )(*args)


def pack_kernel(feats, coords, kinds, downs, ups, packed, sent_up, sent_down):
    rows = feats[...]
    packed[0:ATOMS, :] = rows
    place = coords[...]
    high = place.astype(bf16).astype(f32)
    rest = place - high
    middle = rest.astype(bf16).astype(f32)
    low = rest - middle
    at = iota((16, ATOMS), 0)
    tail = jnp.zeros((16, ATOMS), f32)
    for part, values in enumerate((high, middle, low)):
        for axis in range(3):
            tail = jnp.where(at == 3 * part + axis, values[axis : axis + 1, :], tail)
    tail = jnp.where(at == 9, kinds[...].astype(f32), tail)
    packed[ATOMS:PACK, :] = tail.astype(bf16)
    atom = iota((ATOMS, GHOST), 0)
    sent_up[...] = dot_rows((atom == ups[...]).astype(f32).astype(bf16), rows).astype(bf16)
    sent_down[...] = dot_rows((atom == downs[...]).astype(f32).astype(bf16), rows).astype(bf16)


def structure_kernel(packed, waves, smearing, species_gain, w_charge, table, sums, filt, gain, charges):
    block = lax.rem(lax.axis_index("dom"), ROW)
    mine = waves[:, pl.ds(pl.multiple_of(block * KB, KB), KB)].astype(f32)
    at = iota((16, KB), 0)
    stacked = jnp.zeros((16, KB), f32)
    for axis in range(3):
        stacked = jnp.where(at == axis, mine[axis : axis + 1, :], stacked)
    stacked = stacked.astype(bf16)
    axis_at = iota((16, C), 0)
    lanes = [
        dot_rows(stacked, (axis_at == axis).astype(f32).astype(bf16)) for axis in range(3)
    ]
    squared = lanes[0] * lanes[0] + lanes[1] * lanes[1] + lanes[2] * lanes[2]
    filt[...] = filter_factor * jnp.exp(-squared * smearing[...]) / jnp.sqrt(squared)
    kind_at = iota((8, ATOMS), 0).astype(f32)
    for j in range(ROW):
        rows = packed[PACK * j : PACK * j + ATOMS, :]
        tail = packed[PACK * j + ATOMS : PACK * (j + 1), :].astype(f32)
        onehot = (tail[9:10, :] == kind_at).astype(f32)
        own_gain = lax.dot_general(
            onehot,
            species_gain[...],
            (((0,), (0,)), ((), ())),
            precision=lax.Precision.HIGHEST,
            preferred_element_type=f32,
        )
        span = slice(ATOMS * j, ATOMS * (j + 1))
        gain[span, :] = own_gain
        charges[span, :] = (dot(rows, w_charge[...]) * own_gain).astype(bf16)
        turns = jnp.zeros((KB, ATOMS), f32)
        for axis in range(3):
            place = tail[axis : axis + 1, :] + tail[axis + 3 : axis + 4, :] + tail[axis + 6 : axis + 7, :]
            turns = turns + place * lanes[axis]
        turns = turns - jnp.round(turns)
        square = turns * turns
        table[0:KB, span] = horner(COS_TURN, square).astype(bf16)
        table[KB : 2 * KB, span] = (turns * horner(SIN_TURN, square)).astype(bf16)
    sums[...] = dot(table[...], charges[...]).astype(bf16)


def field_of(parts, filt, scale):
    total = parts[0][...].astype(f32)
    for part in parts[1:]:
        total = total + part[...].astype(f32)
    weight = filt[...]
    return jnp.concatenate(
        [
            (weight * total[0:KB] * scale).astype(bf16),
            (weight * total[KB : 2 * KB] * scale).astype(bf16),
        ],
        axis=0,
    )


def potential_kernel(s0, s1, s2, s3, filt, table, send, keep):
    field = field_of((s0, s1, s2, s3), filt, inv_atoms)
    values = dot_rows(table[...], field) * inv_waves
    half = ROW * ATOMS // 2
    keep[...] = values[:half]
    send[...] = values[half:].astype(bf16)


def halve_kernel(held, received, send, keep):
    half = keep.shape[0]
    keep[...] = held[0:half, :] + received[0:half, :].astype(f32)
    send[...] = (held[half : 2 * half, :] + received[half : 2 * half, :].astype(f32)).astype(bf16)


def edge_kernel(senders, receivers, live, lengths, total, left, right):
    step = pl.program_id(0)
    reach = lengths[...]
    turn = reach * (0.5 / cutoff_radius)
    envelope = 0.5 * (horner(COS_TURN, turn * turn) + 1.0) * live[...].astype(f32)
    centers = 0.5 + basis_width * iota((NB, CHUNK), 0).astype(f32)
    offset = (reach - centers) * (1.0 / basis_width)
    weights = (jnp.exp(-offset * offset) * envelope).astype(bf16)
    atom = iota((ATOMS, CHUNK), 0)
    onehot = (atom == receivers[...]).astype(f32).astype(bf16)
    for b in range(NB):
        left[ATOMS * b : ATOMS * (b + 1), :] = onehot * weights[b : b + 1, :]
    source = iota((EXT, CHUNK), 0)
    right[...] = (source == senders[...]).astype(f32).astype(bf16)

    @pl.when(step == 0)
    def _():
        total[...] = jnp.zeros_like(total)

    total[...] += dot_lanes(left[...], right[...])


def aggregate_kernel(feats, below, above, w_message, operator, w_radial, aggregate, radial_rows):
    extended = jnp.concatenate([feats[...], below[...], above[...]], axis=0)
    rows = dot(extended, w_message[...]).astype(bf16)
    high, low = split(operator[...])
    products = dot(high, rows) + dot(low, rows)
    radial_rows[...] = products
    total = jnp.zeros((ATOMS, C), f32)
    for b in range(NB):
        total = total + w_radial[b : b + 1, :] * products[ATOMS * b : ATOMS * (b + 1)]
    aggregate[...] = total * edge_scale


def update_kernel(held, received, aggregate, feats, cotangent, w_out, updated, act_out, grad_pre, grad_pre_b):
    preact = aggregate[...] + held[...] + received[...].astype(f32)
    sig = jax.nn.sigmoid(preact)
    grad_act = dot_lanes(cotangent[...], w_out[...])
    grad = grad_act * sig * (1.0 + preact * (1.0 - sig))
    grad_pre[...] = grad
    grad_pre_b[...] = grad.astype(bf16)
    act = (preact * sig).astype(bf16)
    act_out[...] = act
    updated[...] = (feats[...].astype(f32) + dot(act, w_out[...])).astype(bf16)


def message_back_kernel(
    grad_pre, act, cotangent, feats, below, above, w_message, operator, radial_rows, w_radial,
    own, back_below, back_above, grads,
):
    grad = grad_pre[...] * edge_scale
    stacked = jnp.concatenate([w_radial[b : b + 1, :] * grad for b in range(NB)], axis=0).astype(bf16)
    high, low = split(operator[...])
    grad_msg = (dot_rows(high, stacked) + dot_rows(low, stacked)).astype(bf16)
    grad_rows = dot_lanes(grad_msg, w_message[...])
    own[...] = cotangent[...].astype(f32) + grad_rows[:ATOMS]
    back_below[...] = grad_rows[ATOMS : ATOMS + GHOST]
    back_above[...] = grad_rows[ATOMS + GHOST :]
    extended = jnp.concatenate([feats[...], below[...], above[...]], axis=0)
    grads[0:C, :] = dot_rows(extended, grad_msg).astype(bf16)
    grads[C : 2 * C, :] = dot_rows(act[...], cotangent[...]).astype(bf16)
    at = iota((16, C), 0)
    tail = jnp.zeros((16, C), f32)
    for b in range(NB):
        part = jnp.sum(grad * radial_rows[ATOMS * b : ATOMS * (b + 1), :], axis=0, keepdims=True)
        tail = jnp.where(at == b, part, tail)
    grads[2 * C :, :] = tail.astype(bf16)


def back_structure_kernel(table, grad_pre_b, sums):
    sums[...] = dot(table[...], grad_pre_b[...]).astype(bf16)


def charge_back_kernel(s0, s1, s2, s3, filt, table, gain, packed, grads, send, keep, partial, rounded):
    field = field_of((s0, s1, s2, s3), filt, inv_waves * inv_atoms)
    half = ROW * ATOMS // 2
    values = dot_rows(table[...], field) * gain[...]
    rounded[...] = values.astype(bf16)
    keep[...] = values[:half]
    send[0:half, :] = rounded[half:, :]
    total = jnp.zeros((C, C), f32)
    for j in range(ROW):
        total = total + dot_rows(
            packed[PACK * j : PACK * j + ATOMS, :], rounded[ATOMS * j : ATOMS * (j + 1), :]
        )
    partial[0:C, :] = total.astype(bf16)
    partial[C:, :] = grads[...]
    send[half:, :] = partial[...]


def tail_kernel(held, held_grads, received, send, keep, partial):
    whole = held.shape[0]
    half = whole // 2
    values = held[...] + received[0:whole, :].astype(f32)
    total = (held_grads[...].astype(f32) + received[whole:, :].astype(f32)).astype(bf16)
    keep[...] = values[:half]
    partial[...] = total
    send[0:half, :] = values[half:].astype(bf16)
    send[half:, :] = total


def raw_kernel(held, held_grads, received, raw, partial):
    raw[...] = (held[...] + received[0:ATOMS, :].astype(f32)).astype(bf16)
    partial[...] = (held_grads[...].astype(f32) + received[ATOMS:, :].astype(f32)).astype(bf16)


def feature_kernel(raw, w_charge, own, downs, ups, back_down, back_up, out):
    total = own[...] + dot_lanes(raw[...], w_charge[...])
    atom = iota((ATOMS, GHOST), 0)
    for index, rows in ((downs, back_down), (ups, back_up)):
        onehot = (atom == index[...]).astype(f32).astype(bf16)
        high, low = split(rows[...])
        total = total + dot(onehot, high) + dot(onehot, low)
    out[...] = total.astype(bf16)


def add_kernel(held, received, out):
    out[...] = (held[...].astype(f32) + received[...].astype(f32)).astype(bf16)


def weights_kernel(held, received, charge, message, radial, out):
    total = (held[...].astype(f32) + received[...].astype(f32)) * grad_scale
    charge[...] = total[0:C]
    message[...] = total[C : 2 * C]
    out[...] = total[2 * C : 3 * C]
    radial[...] = total[3 * C : 3 * C + NB]


def swap(values, axis, mask):
    count = lax.axis_size(axis)
    return lax.ppermute(values, axis, [(i, i ^ mask) for i in range(count)])


def shift(values, by):
    return lax.ppermute(values, "dom", [(i, (i + by) % DOMS) for i in range(DOMS)])


def gather_row(values):
    for mask in (4, 2, 1):
        values = jnp.concatenate([values, swap(values, "dom", mask)], axis=0)
    return values


def column_parts(values):
    return [values] + [swap(values, "dom", mask) for mask in (8, 16, 24)]


def per_device(
    feats,
    positions,
    species,
    wave_vectors,
    smearing,
    species_gain,
    w_charge,
    w_message,
    w_radial,
    w_out,
    edge_sender,
    edge_receiver,
    edge_mask,
    edge_length,
    ghost_down,
    ghost_up,
    cotangent,
):
    own_rows = feats[0]
    cot = cotangent[0]
    packed, sent_up, sent_down = call(
        pack_kernel,
        [((PACK, C), bf16), ((GHOST, C), bf16), ((GHOST, C), bf16)],
        own_rows, positions[0], species, ghost_down, ghost_up,
        name="pack",
    )
    gathered = gather_row(packed)
    below = shift(sent_up, 1)
    above = shift(sent_down, -1)

    edge_spec = pl.BlockSpec((1, CHUNK), lambda e: (0, e))
    (operator,) = call(
        edge_kernel,
        [((NB * ATOMS, EXT), f32)],
        edge_sender, edge_receiver, edge_mask, edge_length,
        scratch=[pltpu.VMEM((NB * ATOMS, CHUNK), bf16), pltpu.VMEM((EXT, CHUNK), bf16)],
        grid=(EDGES // CHUNK,),
        in_specs=[edge_spec] * 4,
        out_specs=[pl.BlockSpec((NB * ATOMS, EXT), lambda e: (0, 0))],
        name="edges",
    )
    table, sums, filt, gain = call(
        structure_kernel,
        [((2 * KB, ROW * ATOMS), bf16), ((2 * KB, C), bf16), ((KB, C), f32), ((ROW * ATOMS, C), f32)],
        gathered, wave_vectors, smearing[None], species_gain, w_charge,
        scratch=[pltpu.VMEM((ROW * ATOMS, C), bf16)],
        name="structure",
    )
    parts = column_parts(sums)
    half = ROW * ATOMS // 2
    send, keep = call(
        potential_kernel, [((half, C), bf16), ((half, C), f32)], *parts, filt, table, name="potential"
    )
    for mask in (1, 2):
        received = swap(send, "dom", mask)
        half //= 2
        send, keep = call(
            halve_kernel, [((half, C), bf16), ((half, C), f32)], keep, received, name="halve"
        )
    received = swap(send, "dom", 4)
    aggregate, radial_rows = call(
        aggregate_kernel,
        [((ATOMS, C), f32), ((NB * ATOMS, C), f32)],
        own_rows, below, above, w_message, operator, w_radial,
        name="aggregate",
    )
    updated, act, grad_pre, grad_pre_b = call(
        update_kernel,
        [((ATOMS, C), bf16), ((ATOMS, C), bf16), ((ATOMS, C), f32), ((ATOMS, C), bf16)],
        keep, received, aggregate, own_rows, cot, w_out,
        name="update",
    )
    all_grad_pre = gather_row(grad_pre_b)
    own, back_below, back_above, grads = call(
        message_back_kernel,
        [((ATOMS, C), f32), ((GHOST, C), f32), ((GHOST, C), f32), ((2 * C + 16, C), bf16)],
        grad_pre, act, cot, own_rows, below, above, w_message, operator, radial_rows, w_radial,
        name="message_back",
    )
    back_down = shift(back_above, 1)
    back_up = shift(back_below, -1)
    (back_sums,) = call(
        back_structure_kernel, [((2 * KB, C), bf16)], table, all_grad_pre, name="back_structure"
    )
    parts = column_parts(back_sums)
    half = ROW * ATOMS // 2
    send, keep, partial = call(
        charge_back_kernel,
        [((half + GROWS, C), bf16), ((half, C), f32), ((GROWS, C), bf16)],
        *parts, filt, table, gain, gathered, grads,
        scratch=[pltpu.VMEM((ROW * ATOMS, C), bf16)],
        name="charge_back",
    )
    for mask in (1, 2):
        received = swap(send, "dom", mask)
        half //= 2
        send, keep, partial = call(
            tail_kernel,
            [((half + GROWS, C), bf16), ((half, C), f32), ((GROWS, C), bf16)],
            keep, partial, received,
            name="tail",
        )
    received = swap(send, "dom", 4)
    raw, partial = call(
        raw_kernel, [((ATOMS, C), bf16), ((GROWS, C), bf16)], keep, partial, received, name="raw"
    )
    for axis, mask in (("dom", 8), ("dom", 24), ("cell", 2), ("cell", 6)):
        received = swap(partial, axis, mask)
        (partial,) = call(add_kernel, [((GROWS, C), bf16)], partial, received, name="add")
    received = swap(partial, "cell", 1)
    (feat_grad,) = call(
        feature_kernel,
        [((ATOMS, C), bf16)],
        raw, w_charge, own, ghost_down, ghost_up, back_down, back_up,
        name="feature",
    )
    charge, message, radial, out = call(
        weights_kernel,
        [((C, C), f32), ((C, C), f32), ((NB, C), f32), ((C, C), f32)],
        partial, received,
        name="weights",
    )
    return updated[None], feat_grad[None], charge, message, radial, out


def solution(mesh):
    placed = (
        P("cell", "dom", None),
        P("cell", None, "dom"),
        P("cell", "dom"),
        P(),
        P(),
        P(),
        P(),
        P(),
        P(),
        P(),
        P("cell", "dom"),
        P("cell", "dom"),
        P("cell", "dom"),
        P("cell", "dom"),
        P("cell", "dom"),
        P("cell", "dom"),
        P("cell", "dom", None),
    )
    return jax.shard_map(
        per_device,
        mesh=mesh,
        in_specs=placed,
        out_specs=(P("cell", "dom", None), P("cell", "dom", None), P(), P(), P(), P()),
        check_vma=False,
    )
```

```python
import math

import jax
import jax.numpy as jnp
from jax import lax
from jax.experimental import pallas as pl
from jax.experimental.pallas import tpu as pltpu
from jax.sharding import PartitionSpec as P

bf16 = jnp.bfloat16
f32 = jnp.float32

C = 128
K = 2048
NB = 8
ATOMS = 128
GHOST = 32
EXT = ATOMS + 2 * GHOST
EDGES = 12288
DOMS = 32
CELLS = 8
ROW = 8
KB = K // ROW
PACK = ATOMS + 16
QUARTER = 80
HALF = ROW * ATOMS // 2
CHUNK = 1024
EDGE_STEPS = (3, 5, 1, 3)

cutoff_radius = 6.0
basis_width = 0.75
edge_scale = 0.25
filter_factor = 12.0
inv_waves = 1.0 / math.sqrt(K)
inv_atoms = 1.0 / math.sqrt(ATOMS * DOMS)
grad_scale = 1.0 / math.sqrt(CELLS * ATOMS * DOMS)

COS_TURN = (
    0.9999999890754399,
    -19.73920450099313,
    64.93911749956553,
    -85.45013994347214,
    60.16763282514798,
    -25.967602441408868,
    6.528658639370483,
)
SIN_TURN = (
    6.283184916984331,
    -41.34158926418157,
    81.59994386455666,
    -76.61447586020026,
    41.342889428722025,
    -12.471244745942547,
)


def horner(coefficients, x):
    total = jnp.full_like(x, coefficients[-1])
    for value in coefficients[-2::-1]:
        total = total * x + value
    return total


def iota(shape, axis):
    return lax.broadcasted_iota(jnp.int32, shape, axis)


def dot(left, right):
    return jnp.dot(left, right, preferred_element_type=f32)


def dot_rows(left, right):
    return lax.dot_general(left, right, (((0,), (0,)), ((), ())), preferred_element_type=f32)


def dot_lanes(left, right):
    return lax.dot_general(left, right, (((1,), (1,)), ((), ())), preferred_element_type=f32)


def split(values):
    high = values.astype(bf16)
    return high, (values - high.astype(f32)).astype(bf16)


def call(kernel, outs, *args, scratch=(), flops=0, after=(), name=None, **more):
    def run(*refs):
        kernel(*refs[: len(args)], *refs[len(args) + len(after) :])

    if "in_specs" not in more:
        more["in_specs"] = [pl.BlockSpec(memory_space=pltpu.VMEM)] * len(args)
        more["out_specs"] = [pl.BlockSpec(memory_space=pltpu.VMEM)] * len(outs)
    more["in_specs"] = more["in_specs"] + [pl.BlockSpec(memory_space=pl.ANY)] * len(after)
    return pl.pallas_call(
        run,
        out_shape=[jax.ShapeDtypeStruct(shape, dtype) for shape, dtype in outs],
        scratch_shapes=list(scratch),
        compiler_params=pltpu.CompilerParams(vmem_limit_bytes=40 * 1024 * 1024),
        cost_estimate=pl.CostEstimate(flops=flops, bytes_accessed=1 << 18, transcendentals=0),
        name=name,
        **more,
    )(*args, *after)


def place_in_row():
    return lax.rem(lax.axis_index("dom"), ROW)


def at_block(mask, rows):
    return pl.multiple_of((mask // 2 + (mask % 2) * (ROW // 2)) * rows, rows)


def quarter_at(part):
    return pl.ds(pl.multiple_of(((place_in_row() // 2) ^ part) * QUARTER, QUARTER), QUARTER)


def pack_kernel(feats, coords, kinds, downs, ups, packed, tail):
    packed[0:ATOMS, :] = feats[...]
    place = coords[...]
    high = place.astype(bf16).astype(f32)
    rest = place - high
    middle = rest.astype(bf16).astype(f32)
    low = rest - middle
    at = iota((16, ATOMS), 0)
    values = jnp.zeros((16, ATOMS), f32)
    for part, piece in enumerate((high, middle, low)):
        for axis in range(3):
            values = jnp.where(at == 3 * part + axis, piece[axis : axis + 1, :], values)
    tail[...] = jnp.where(at == 9, kinds[...].astype(f32), values)
    tail[10:11, 0:GHOST] = ups[...].astype(f32)
    tail[11:12, 0:GHOST] = downs[...].astype(f32)
    packed[ATOMS:PACK, :] = tail[...].astype(bf16)


def wave_lanes(waves):
    mine = waves[:, pl.ds(pl.multiple_of(place_in_row() * KB, KB), KB)].astype(f32)
    at = iota((16, KB), 0)
    stacked = jnp.zeros((16, KB), f32)
    for axis in range(3):
        stacked = jnp.where(at == axis, mine[axis : axis + 1, :], stacked)
    stacked = stacked.astype(bf16)
    axis_at = iota((16, C), 0)
    return [dot_rows(stacked, (axis_at == axis).astype(f32).astype(bf16)) for axis in range(3)]


def tables_of(packed, lanes, species_gain, w_charge, table, gain, charges):
    kind_at = iota((8, ATOMS), 0).astype(f32)
    for j in range(ROW // 2):
        rows = packed[PACK * j : PACK * j + ATOMS, :]
        tail = packed[PACK * j + ATOMS : PACK * (j + 1), :].astype(f32)
        onehot = (tail[9:10, :] == kind_at).astype(f32)
        own_gain = lax.dot_general(
            onehot,
            species_gain[...],
            (((0,), (0,)), ((), ())),
            precision=lax.Precision.HIGHEST,
            preferred_element_type=f32,
        )
        span = slice(ATOMS * j, ATOMS * (j + 1))
        gain[span, :] = own_gain
        charges[span, :] = (dot(rows, w_charge[...]) * own_gain).astype(bf16)
        turns = jnp.zeros((KB, ATOMS), f32)
        for axis in range(3):
            place = tail[axis : axis + 1, :] + tail[axis + 3 : axis + 4, :] + tail[axis + 6 : axis + 7, :]
            turns = turns + place * lanes[axis]
        turns = turns - jnp.round(turns)
        square = turns * turns
        table[0:KB, span] = horner(COS_TURN, square).astype(bf16)
        table[KB : 2 * KB, span] = (turns * horner(SIN_TURN, square)).astype(bf16)


def structure_near_kernel(packed, waves, smearing, species_gain, w_charge, table, sums, filt, gain, charges):
    lanes = wave_lanes(waves)
    squared = lanes[0] * lanes[0] + lanes[1] * lanes[1] + lanes[2] * lanes[2]
    filt[...] = filter_factor * jnp.exp(-squared * smearing[...]) / jnp.sqrt(squared)
    tables_of(packed, lanes, species_gain, w_charge, table, gain, charges)
    sums[...] = dot(table[...], charges[...])


def structure_far_kernel(
    packed, near, near_sums, waves, species_gain, w_charge,
    table, sums, message, gain, below, above, charges, joined,
):
    tables_of(packed, wave_lanes(waves), species_gain, w_charge, table, gain, charges)
    total = (near_sums[...] + dot(table[...], charges[...])).astype(bf16)
    sums[...] = total
    message[0 : 2 * KB, :] = total
    joined[0 : PACK * ROW // 2, :] = near[...]
    joined[PACK * ROW // 2 :, :] = packed[...]
    place = place_in_row()
    atom = iota((ATOMS, GHOST), 0).astype(f32)

    def ghosts(owner, row):
        start = at_block(place ^ owner, PACK)
        rows = joined[pl.ds(start, ATOMS), :]
        tail = joined[pl.ds(pl.multiple_of(start + ATOMS, 16), 16), :].astype(f32)
        return dot_rows((atom == tail[row : row + 1, 0:GHOST]).astype(f32).astype(bf16), rows).astype(bf16)

    below[...] = ghosts((place + ROW - 1) % ROW, 10)
    above[...] = ghosts((place + 1) % ROW, 11)
    message[2 * KB : 2 * KB + GHOST, :] = ghosts(ROW - 1, 10)
    message[2 * KB + GHOST :, :] = ghosts(0, 11)


def column_sum(own, up, down, over, span):
    return (own[span, :].astype(f32) + over[span, :].astype(f32)) + (
        up[span, :].astype(f32) + down[span, :].astype(f32)
    )


def field_of(sums, filt, scale):
    weight = filt[...] * scale
    return jnp.concatenate(
        [(weight * sums[0:KB]).astype(bf16), (weight * sums[KB : 2 * KB]).astype(bf16)], axis=0
    )


def potential_kernel(own, up, down, over, filt, near, far, send, keep):
    field = field_of(column_sum(own, up, down, over, slice(0, 2 * KB)), filt, inv_atoms)
    send[...] = (dot_rows(far[...], field) * inv_waves).astype(bf16)
    keep[...] = dot_rows(near[...], field) * inv_waves


def spread_kernel(held, received, own, *sends):
    values = held[...] + received[...].astype(f32)
    own[...] = values[0:ATOMS]
    for part, send in enumerate(sends):
        send[...] = values[ATOMS * (part + 1) : ATOMS * (part + 2)].astype(bf16)


def edge_kernel(first, *refs):
    senders, receivers, live, lengths = refs[:4]
    total, left, right = refs[-3:]
    step = pl.program_id(0)
    reach = lengths[...]
    turn = reach * (0.5 / cutoff_radius)
    envelope = 0.5 * (horner(COS_TURN, turn * turn) + 1.0) * live[...].astype(f32)
    centers = 0.5 + basis_width * iota((NB, CHUNK), 0).astype(f32)
    offset = (reach - centers) * (1.0 / basis_width)
    weights = (jnp.exp(-offset * offset) * envelope).astype(bf16)
    atom = iota((ATOMS, CHUNK), 0)
    onehot = (atom == receivers[...]).astype(f32).astype(bf16)
    for b in range(NB):
        left[ATOMS * b : ATOMS * (b + 1), :] = onehot * weights[b : b + 1, :]
    source = iota((EXT, CHUNK), 0)
    right[...] = (source == senders[...]).astype(f32).astype(bf16)

    @pl.when(step == 0)
    def _():
        total[...] = jnp.zeros_like(total) if first else refs[4][...]

    total[...] += dot_lanes(left[...], right[...])


def aggregate_kernel(feats, below, above, up, down, w_message, operator, w_radial, aggregate, radial_rows, extended):
    place = place_in_row()
    extended[0:ATOMS, :] = feats[...]
    first, last = 2 * KB, 2 * KB + GHOST
    extended[ATOMS : ATOMS + GHOST, :] = jnp.where(place == 0, up[first:last, :], below[...])
    extended[ATOMS + GHOST :, :] = jnp.where(place == ROW - 1, down[last:, :], above[...])
    rows = dot(extended[...], w_message[...]).astype(bf16)
    high, low = split(operator[...])
    products = dot(high, rows) + dot(low, rows)
    radial_rows[...] = products
    total = jnp.zeros((ATOMS, C), f32)
    for b in range(NB):
        total = total + w_radial[b : b + 1, :] * products[ATOMS * b : ATOMS * (b + 1)]
    aggregate[...] = total * edge_scale


def update_kernel(
    held, near, across, corner, aggregate, feats, cotangent, w_out, extended, w_message, operator, radial_rows,
    w_radial, updated, own_total, own_rows, own_quarter, send_near, send_across, send_corner, grads,
):
    preact = aggregate[...] + (
        (held[...] + near[...].astype(f32)) + (across[...].astype(f32) + corner[...].astype(f32))
    )
    sig = jax.nn.sigmoid(preact)
    grad_act = dot_lanes(cotangent[...], w_out[...])
    grad = grad_act * sig * (1.0 + preact * (1.0 - sig))
    rounded = grad.astype(bf16)
    grad = grad * edge_scale
    stacked = jnp.concatenate([w_radial[b : b + 1, :] * grad for b in range(NB)], axis=0).astype(bf16)
    high, low = split(operator[...])
    grad_msg = (dot_rows(high, stacked) + dot_rows(low, stacked)).astype(bf16)
    grad_rows = dot_lanes(grad_msg, w_message[...])
    own_total[...] = cotangent[...].astype(f32) + grad_rows[:ATOMS]
    own_rows[0:ATOMS, :] = rounded
    own_rows[ATOMS:, :] = grad_rows[ATOMS:].astype(bf16)
    act = (preact * sig).astype(bf16)
    updated[...] = (feats[...].astype(f32) + dot(act, w_out[...])).astype(bf16)
    grads[0:C, :] = dot_rows(extended[...], grad_msg)
    grads[C : 2 * C, :] = dot_rows(act, cotangent[...])
    at = iota((4 * QUARTER - 2 * C, C), 0)
    tail = jnp.zeros((4 * QUARTER - 2 * C, C), f32)
    for b in range(NB):
        part = jnp.sum(grad * radial_rows[ATOMS * b : ATOMS * (b + 1), :], axis=0, keepdims=True)
        tail = jnp.where(at == b, part, tail)
    grads[2 * C :, :] = tail
    own_quarter[...] = grads[quarter_at(0), :]
    for part, send in ((1, send_near), (2, send_across), (3, send_corner)):
        send[0:EXT, :] = own_rows[...]
        send[EXT:, :] = grads[quarter_at(part), :].astype(bf16)


def join_kernel(own_rows, own_quarter, near, across, corner, joined):
    quarter = own_quarter[...]
    for part, rows in enumerate((own_rows, near, across, corner)):
        joined[ATOMS * part : ATOMS * (part + 1), :] = rows[0:ATOMS, :]
        start = HALF + 2 * GHOST * part
        joined[start : start + 2 * GHOST, :] = rows[ATOMS:EXT, :]
        if part:
            quarter = quarter + rows[EXT:, :].astype(f32)
    joined[HALF + 8 * GHOST :, :] = quarter.astype(bf16)


def back_near_kernel(table, joined, sums):
    sums[...] = dot(table[...], joined[0:HALF, :])


def back_far_kernel(table, received, joined, near_sums, message, over, back_down, back_up, ghosts):
    total = (near_sums[...] + dot(table[...], received[0:HALF, :])).astype(bf16)
    ends = HALF + 8 * GHOST
    quarter = (joined[ends:, :].astype(f32) + received[ends:, :].astype(f32)).astype(bf16)
    for target in (message, over):
        target[0 : 2 * KB, :] = total
        target[2 * KB : 2 * KB + QUARTER, :] = quarter
    ghosts[0 : 8 * GHOST, :] = joined[HALF:ends, :]
    ghosts[8 * GHOST :, :] = received[HALF:ends, :]
    place = place_in_row()

    def returned(owner, above):
        start = at_block(place ^ owner, 2 * GHOST) + above * GHOST
        return ghosts[pl.ds(pl.multiple_of(start, GHOST), GHOST), :]

    back_down[...] = returned((place + ROW - 1) % ROW, 1)
    back_up[...] = returned((place + 1) % ROW, 0)
    message[2 * KB + QUARTER : 2 * KB + QUARTER + GHOST, :] = returned(ROW - 1, 1)
    message[2 * KB + QUARTER + GHOST :, :] = returned(0, 0)


def charge_back_kernel(
    own, up, down, over, filt, near, far, near_gain, far_gain, near_rows, far_rows,
    send, keep, charge, quarter, rounded,
):
    field = field_of(column_sum(own, up, down, over, slice(0, 2 * KB)), filt, inv_waves * inv_atoms)
    quarter[...] = column_sum(own, up, down, over, slice(2 * KB, 2 * KB + QUARTER)).astype(bf16)
    send[0:HALF, :] = (dot_rows(far[...], field) * far_gain[...]).astype(bf16)
    values = dot_rows(near[...], field) * near_gain[...]
    keep[...] = values
    rounded[...] = values.astype(bf16)
    total = jnp.zeros((C, C), f32)
    for j in range(ROW // 2):
        rows, atoms = slice(PACK * j, PACK * j + ATOMS), slice(ATOMS * j, ATOMS * (j + 1))
        total = total + dot_rows(near_rows[rows, :], rounded[atoms, :])
        total = total + dot_rows(far_rows[rows, :], send[atoms, :])
    charge[...] = total.astype(bf16)
    send[HALF:, :] = charge[...]


def tail_spread_kernel(held, charge, quarter, received, own, charge_out, *sends):
    values = held[...] + received[0:HALF, :].astype(f32)
    total = (charge[...].astype(f32) + received[HALF:, :].astype(f32)).astype(bf16)
    own[...] = values[0:ATOMS]
    charge_out[...] = total
    for part, send in enumerate(sends):
        send[0:ATOMS, :] = values[ATOMS * (part + 1) : ATOMS * (part + 2)].astype(bf16)
        send[ATOMS : ATOMS + C, :] = total
        send[ATOMS + C :, :] = quarter[...]


def raw_kernel(held, charge, quarter, near, across, corner, raw, charge_out, grads):
    rows = slice(0, ATOMS)
    raw[...] = (
        (held[...] + near[rows, :].astype(f32)) + (across[rows, :].astype(f32) + corner[rows, :].astype(f32))
    ).astype(bf16)
    rows = slice(ATOMS, ATOMS + C)
    charge_out[...] = (
        (charge[...].astype(f32) + near[rows, :].astype(f32))
        + (across[rows, :].astype(f32) + corner[rows, :].astype(f32))
    ).astype(bf16)
    grads[quarter_at(0), :] = quarter[...]
    for part, received in ((1, near), (2, across), (3, corner)):
        grads[quarter_at(part), :] = received[ATOMS + C :, :]


def charge_sum_kernel(own, up, down, over, grads, out):
    out[0:C, :] = column_sum(own, up, down, over, slice(0, C)).astype(bf16)
    out[C:, :] = grads[...]


def cell_sum_kernel(own, near, across, corner, out):
    out[...] = (
        (own[...].astype(f32) + near[...].astype(f32)) + (across[...].astype(f32) + corner[...].astype(f32))
    ).astype(bf16)


def feature_kernel(raw, w_charge, own, downs, ups, back_down, back_up, up, down, out):
    place = place_in_row()
    first, last = 2 * KB + QUARTER, 2 * KB + QUARTER + GHOST
    returned = jnp.where(place == 0, up[first:last, :], back_down[...])
    total = own[...] + dot_lanes(raw[...], w_charge[...])
    atom = iota((ATOMS, GHOST), 0)
    total = total + dot((atom == downs[...]).astype(f32).astype(bf16), returned)
    returned = jnp.where(place == ROW - 1, down[last:, :], back_up[...])
    total = total + dot((atom == ups[...]).astype(f32).astype(bf16), returned)
    out[...] = total.astype(bf16)


def weights_kernel(held, received, charge, message, radial, out):
    total = (held[...].astype(f32) + received[...].astype(f32)) * grad_scale
    charge[...] = total[0:C]
    message[...] = total[C : 2 * C]
    out[...] = total[2 * C : 3 * C]
    radial[...] = total[3 * C : 3 * C + NB]


def swap(values, axis, mask):
    count = lax.axis_size(axis)
    return lax.ppermute(values, axis, [(i, i ^ mask) for i in range(count)])


def from_y(values, by):
    return lax.ppermute(values, "dom", [(i, (i + ROW * by) % DOMS) for i in range(DOMS)])


def per_device(
    feats,
    positions,
    species,
    wave_vectors,
    smearing,
    species_gain,
    w_charge,
    w_message,
    w_radial,
    w_out,
    edge_sender,
    edge_receiver,
    edge_mask,
    edge_length,
    ghost_down,
    ghost_up,
    cotangent,
):
    own_rows = feats[0]
    cot = cotangent[0]

    def edges(first, count, total, after):
        spec = pl.BlockSpec((1, CHUNK), lambda e: (0, first + e))
        whole = pl.BlockSpec((NB * ATOMS, EXT), lambda e: (0, 0))
        held = [] if total is None else [total]
        (out,) = call(
            lambda *refs: edge_kernel(total is None, *refs),
            [((NB * ATOMS, EXT), f32)],
            edge_sender, edge_receiver, edge_mask, edge_length, *held,
            scratch=[pltpu.VMEM((NB * ATOMS, CHUNK), bf16), pltpu.VMEM((EXT, CHUNK), bf16)],
            flops=count * 2 * NB * ATOMS * CHUNK * 256,
            grid=(count,),
            in_specs=[spec] * 4 + [whole] * len(held),
            out_specs=[whole],
            after=after,
            name="edges",
        )
        return out

    (packed,) = call(
        pack_kernel,
        [((PACK, C), bf16)],
        own_rows, positions[0], species, ghost_down, ghost_up,
        scratch=[pltpu.VMEM((16, C), f32)],
        name="pack",
    )
    operator = edges(0, EDGE_STEPS[0], None, [packed])
    near_rows = jnp.concatenate([packed] + [swap(packed, "dom", mask) for mask in (2, 4, 6)], axis=0)
    far_rows = swap(near_rows, "dom", 1)
    near, near_sums, filt, near_gain = call(
        structure_near_kernel,
        [((2 * KB, HALF), bf16), ((2 * KB, C), f32), ((KB, C), f32), ((HALF, C), f32)],
        near_rows, wave_vectors, smearing[None], species_gain, w_charge,
        scratch=[pltpu.VMEM((HALF, C), bf16)],
        after=[operator],
        name="structure_near",
    )
    far, sums, message, far_gain, below, above = call(
        structure_far_kernel,
        [
            ((2 * KB, HALF), bf16), ((2 * KB, C), bf16), ((2 * KB + 2 * GHOST, C), bf16), ((HALF, C), f32),
            ((GHOST, C), bf16), ((GHOST, C), bf16),
        ],
        far_rows, near_rows, near_sums, wave_vectors, species_gain, w_charge,
        scratch=[pltpu.VMEM((HALF, C), bf16), pltpu.VMEM((ROW * PACK, C), bf16)],
        name="structure_far",
    )
    up, down, over = from_y(message, 1), from_y(message, -1), from_y(sums, 2)
    operator = edges(EDGE_STEPS[0], EDGE_STEPS[1], operator, [message])
    send, keep = call(
        potential_kernel,
        [((HALF, C), bf16), ((HALF, C), f32)],
        sums, up, down, over, filt, near, far,
        after=[operator],
        name="potential",
    )
    received = swap(send, "dom", 1)
    operator = edges(EDGE_STEPS[0] + EDGE_STEPS[1], EDGE_STEPS[2], operator, [send])
    held, *sends = call(
        spread_kernel, [((ATOMS, C), f32)] + [((ATOMS, C), bf16)] * 3, keep, received, after=[operator], name="spread"
    )
    parts = [swap(values, "dom", 2 * (part + 1)) for part, values in enumerate(sends)]
    operator = edges(sum(EDGE_STEPS[:3]), EDGE_STEPS[3], operator, [held])
    aggregate, radial_rows, extended = call(
        aggregate_kernel,
        [((ATOMS, C), f32), ((NB * ATOMS, C), f32), ((EXT, C), bf16)],
        own_rows, below, above, up, down, w_message, operator, w_radial,
        name="aggregate",
    )
    updated, own_total, back_rows, quarter, *sends = call(
        update_kernel,
        [((ATOMS, C), bf16), ((ATOMS, C), f32), ((EXT, C), bf16), ((QUARTER, C), f32)]
        + [((EXT + QUARTER, C), bf16)] * 3,
        held, *parts, aggregate, own_rows, cot, w_out, extended, w_message, operator, radial_rows, w_radial,
        scratch=[pltpu.VMEM((4 * QUARTER, C), f32)],
        name="update",
    )
    parts = [swap(values, "dom", 2 * (part + 1)) for part, values in enumerate(sends)]
    (joined,) = call(
        join_kernel, [((HALF + 8 * GHOST + QUARTER, C), bf16)], back_rows, quarter, *parts, name="join"
    )
    received = swap(joined, "dom", 1)
    (near_sums,) = call(back_near_kernel, [((2 * KB, C), f32)], near, joined, name="back_near")
    message, over, back_down, back_up = call(
        back_far_kernel,
        [
            ((2 * KB + QUARTER + 2 * GHOST, C), bf16), ((2 * KB + QUARTER, C), bf16),
            ((GHOST, C), bf16), ((GHOST, C), bf16),
        ],
        far, received, joined, near_sums,
        scratch=[pltpu.VMEM((16 * GHOST, C), bf16)],
        name="back_far",
    )
    up, down, over = from_y(message, 1), from_y(message, -1), from_y(over, 2)
    send, keep, charge, quarter = call(
        charge_back_kernel,
        [((HALF + C, C), bf16), ((HALF, C), f32), ((C, C), bf16), ((QUARTER, C), bf16)],
        message, up, down, over, filt, near, far, near_gain, far_gain, near_rows, far_rows,
        scratch=[pltpu.VMEM((HALF, C), bf16)],
        name="charge_back",
    )
    received = swap(send, "dom", 1)
    held, charge, *sends = call(
        tail_spread_kernel,
        [((ATOMS, C), f32), ((C, C), bf16)] + [((ATOMS + C + QUARTER, C), bf16)] * 3,
        keep, charge, quarter, received,
        name="tail_spread",
    )
    parts = [swap(values, "dom", 2 * (part + 1)) for part, values in enumerate(sends)]
    raw, charge, grads = call(
        raw_kernel,
        [((ATOMS, C), bf16), ((C, C), bf16), ((4 * QUARTER, C), bf16)],
        held, charge, quarter, *parts,
        name="raw",
    )
    parts = [from_y(charge, by) for by in (1, -1, 2)]
    (feat_grad,) = call(
        feature_kernel,
        [((ATOMS, C), bf16)],
        raw, w_charge, own_total, ghost_down, ghost_up, back_down, back_up, up, down,
        name="feature",
    )
    (total,) = call(
        charge_sum_kernel, [((C + 4 * QUARTER, C), bf16)], charge, *parts, grads, after=[feat_grad], name="charge_sum"
    )
    parts = [swap(total, "cell", mask) for mask in (2, 4, 6)]
    (total,) = call(cell_sum_kernel, [((C + 4 * QUARTER, C), bf16)], total, *parts, name="cell_sum")
    received = swap(total, "cell", 1)
    charge, message, radial, out = call(
        weights_kernel,
        [((C, C), f32), ((C, C), f32), ((NB, C), f32), ((C, C), f32)],
        total, received,
        name="weights",
    )
    return updated[None], feat_grad[None], charge, message, radial, out


def solution(mesh):
    placed = (
        P("cell", "dom", None),
        P("cell", None, "dom"),
        P("cell", "dom"),
        P(),
        P(),
        P(),
        P(),
        P(),
        P(),
        P(),
        P("cell", "dom"),
        P("cell", "dom"),
        P("cell", "dom"),
        P("cell", "dom"),
        P("cell", "dom"),
        P("cell", "dom"),
        P("cell", "dom", None),
    )
    return jax.shard_map(
        per_device,
        mesh=mesh,
        in_specs=placed,
        out_specs=(P("cell", "dom", None), P("cell", "dom", None), P(), P(), P(), P()),
        check_vma=False,
    )
```

```python
import math

import jax
import jax.numpy as jnp
from jax import lax
from jax.experimental import pallas as pl
from jax.experimental.pallas import tpu as pltpu
from jax.sharding import PartitionSpec as P

bf16 = jnp.bfloat16
f32 = jnp.float32

C = 128
K = 2048
NB = 8
ATOMS = 128
GHOST = 32
EXT = ATOMS + 2 * GHOST
EDGES = 12288
DOMS = 32
CELLS = 8
ROW = 8
KB = K // ROW
PACK = ATOMS + 16
QUARTER = 64
PART = QUARTER // 2
LOW = C // 2
HALF = ROW * ATOMS // 2
CHUNK = 1024
EDGE_STEPS = (3, 6, 1, 2)

cutoff_radius = 6.0
basis_width = 0.75
edge_scale = 0.25
filter_factor = 12.0
inv_waves = 1.0 / math.sqrt(K)
inv_atoms = 1.0 / math.sqrt(ATOMS * DOMS)
grad_scale = 1.0 / math.sqrt(CELLS * ATOMS * DOMS)

COS_TURN = (
    0.9999999890754399,
    -19.73920450099313,
    64.93911749956553,
    -85.45013994347214,
    60.16763282514798,
    -25.967602441408868,
    6.528658639370483,
)
SIN_TURN = (
    6.283184916984331,
    -41.34158926418157,
    81.59994386455666,
    -76.61447586020026,
    41.342889428722025,
    -12.471244745942547,
)


def horner(coefficients, x):
    total = jnp.full_like(x, coefficients[-1])
    for value in coefficients[-2::-1]:
        total = total * x + value
    return total


def iota(shape, axis):
    return lax.broadcasted_iota(jnp.int32, shape, axis)


def dot(left, right):
    return jnp.dot(left, right, preferred_element_type=f32)


def dot_rows(left, right):
    return lax.dot_general(left, right, (((0,), (0,)), ((), ())), preferred_element_type=f32)


def dot_lanes(left, right):
    return lax.dot_general(left, right, (((1,), (1,)), ((), ())), preferred_element_type=f32)


def split(values):
    high = values.astype(bf16)
    return high, (values - high.astype(f32)).astype(bf16)


def call(kernel, outs, *args, scratch=(), flops=0, after=(), name=None, **more):
    def run(*refs):
        kernel(*refs[: len(args)], *refs[len(args) + len(after) :])

    if "in_specs" not in more:
        more["in_specs"] = [pl.BlockSpec(memory_space=pltpu.VMEM)] * len(args)
        more["out_specs"] = [pl.BlockSpec(memory_space=pltpu.VMEM)] * len(outs)
    more["in_specs"] = more["in_specs"] + [pl.BlockSpec(memory_space=pl.ANY)] * len(after)
    return pl.pallas_call(
        run,
        out_shape=[jax.ShapeDtypeStruct(shape, dtype) for shape, dtype in outs],
        scratch_shapes=list(scratch),
        compiler_params=pltpu.CompilerParams(vmem_limit_bytes=40 * 1024 * 1024),
        cost_estimate=pl.CostEstimate(flops=flops, bytes_accessed=1 << 18, transcendentals=0),
        name=name,
        **more,
    )(*args, *after)


def place_in_row():
    return lax.rem(lax.axis_index("dom"), ROW)


def at_block(mask, rows):
    return pl.multiple_of((mask // 2 + (mask % 2) * (ROW // 2)) * rows, rows)


def rows_at(index, count):
    return pl.ds(pl.multiple_of(index * count, count), count)


def z_at(part, count):
    return rows_at((place_in_row() // 2) ^ part, count)


def core():
    return lax.rem(lax.axis_index("dom"), 2)


def tree(own, near, across, corner):
    return (own.astype(f32) + near.astype(f32)) + (across.astype(f32) + corner.astype(f32))


def pack_kernel(
    feats, coords, kinds, downs, ups, sent, got, live, reach,
    packed, senders, receivers, mask, lengths, tail, whole, places, labels, indices, sems,
):
    near = [(feats, whole), (coords, places), (kinds, labels), (ups, indices.at[0]), (downs, indices.at[1])]
    edges = [(sent, senders), (got, receivers), (live, mask), (reach, lengths)]
    copies = [
        pltpu.make_async_copy(source, target, sems.at[i]) for i, (source, target) in enumerate(near + edges)
    ]
    for copy in copies:
        copy.start()
    for copy in copies:
        copy.wait()
    packed[0:ATOMS, :] = whole[...]
    at = iota((16, ATOMS), 0)
    values = jnp.where(at == 9, labels[...].astype(f32), 0.0)
    for axis in range(3):
        place = places[axis]
        for part in range(3):
            piece = place.astype(bf16).astype(f32)
            values = jnp.where(at == 3 * part + axis, piece, values)
            place = place - piece
    tail[...] = values
    tail[10:11, 0:GHOST] = indices[0].astype(f32)
    tail[11:12, 0:GHOST] = indices[1].astype(f32)
    packed[ATOMS:PACK, :] = tail[...].astype(bf16)


def gather_kernel(own, near, across, corner, out):
    for part, rows in enumerate((own, near, across, corner)):
        out[PACK * part : PACK * (part + 1), :] = rows[...]


def wave_lanes(waves):
    mine = waves[:, pl.ds(pl.multiple_of(place_in_row() * KB, KB), KB)].astype(f32)
    at = iota((16, KB), 0)
    stacked = jnp.zeros((16, KB), f32)
    for axis in range(3):
        stacked = jnp.where(at == axis, mine[axis : axis + 1, :], stacked)
    stacked = stacked.astype(bf16)
    axis_at = iota((16, C), 0)
    return [dot_rows(stacked, (axis_at == axis).astype(f32).astype(bf16)) for axis in range(3)]


def tables_of(packed, lanes, species_gain, w_charge, table, gain, charges):
    kind_at = iota((8, ATOMS), 0).astype(f32)
    for j in range(ROW // 2):
        rows = packed[PACK * j : PACK * j + ATOMS, :]
        tail = packed[PACK * j + ATOMS : PACK * (j + 1), :].astype(f32)
        onehot = (tail[9:10, :] == kind_at).astype(f32)
        own_gain = lax.dot_general(
            onehot,
            species_gain[...],
            (((0,), (0,)), ((), ())),
            precision=lax.Precision.HIGHEST,
            preferred_element_type=f32,
        )
        span = slice(ATOMS * j, ATOMS * (j + 1))
        gain[span, :] = own_gain
        charges[span, :] = (dot(rows, w_charge[...]) * own_gain).astype(bf16)
        turns = jnp.zeros((KB, ATOMS), f32)
        for axis in range(3):
            place = tail[axis : axis + 1, :] + tail[axis + 3 : axis + 4, :] + tail[axis + 6 : axis + 7, :]
            turns = turns + place * lanes[axis]
        turns = turns - jnp.round(turns)
        square = turns * turns
        table[0:KB, span] = horner(COS_TURN, square).astype(bf16)
        table[KB : 2 * KB, span] = (turns * horner(SIN_TURN, square)).astype(bf16)


def structure_near_kernel(packed, waves, smearing, species_gain, w_charge, table, sums, filt, gain, charges):
    lanes = wave_lanes(waves)
    squared = lanes[0] * lanes[0] + lanes[1] * lanes[1] + lanes[2] * lanes[2]
    filt[...] = filter_factor * jnp.exp(-squared * smearing[...]) / jnp.sqrt(squared)
    tables_of(packed, lanes, species_gain, w_charge, table, gain, charges)
    sums[...] = dot(table[...], charges[...])


def structure_far_kernel(
    packed, near, near_sums, waves, species_gain, w_charge,
    table, sums, message, gain, below, above, charges, joined,
):
    tables_of(packed, wave_lanes(waves), species_gain, w_charge, table, gain, charges)
    total = (near_sums[...] + dot(table[...], charges[...])).astype(bf16)
    sums[...] = total
    message[0 : 2 * KB, :] = total
    joined[0 : PACK * ROW // 2, :] = near[...]
    joined[PACK * ROW // 2 :, :] = packed[...]
    place = place_in_row()
    atom = iota((ATOMS, GHOST), 0).astype(f32)

    def ghosts(owner, row):
        start = at_block(place ^ owner, PACK)
        rows = joined[pl.ds(start, ATOMS), :]
        tail = joined[pl.ds(pl.multiple_of(start + ATOMS, 16), 16), :].astype(f32)
        return dot_rows((atom == tail[row : row + 1, 0:GHOST]).astype(f32).astype(bf16), rows).astype(bf16)

    below[...] = ghosts((place + ROW - 1) % ROW, 10)
    above[...] = ghosts((place + 1) % ROW, 11)
    message[2 * KB : 2 * KB + GHOST, :] = ghosts(ROW - 1, 10)
    message[2 * KB + GHOST :, :] = ghosts(0, 11)


def column_sum(own, up, down, over, span):
    return tree(own[span, :], over[span, :], up[span, :], down[span, :])


def field_of(sums, filt, scale):
    weight = filt[...] * scale
    return jnp.concatenate(
        [(weight * sums[0:KB]).astype(bf16), (weight * sums[KB : 2 * KB]).astype(bf16)], axis=0
    )


def potential_kernel(own, up, down, over, filt, near, far, send, keep):
    field = field_of(column_sum(own, up, down, over, slice(0, 2 * KB)), filt, inv_atoms)
    send[...] = (dot_rows(far[...], field) * inv_waves).astype(bf16)
    keep[...] = dot_rows(near[...], field) * inv_waves


def spread_kernel(held, received, own, *sends):
    values = held[...] + received[...].astype(f32)
    own[...] = values[0:ATOMS]
    for part, send in enumerate(sends):
        send[...] = values[ATOMS * (part + 1) : ATOMS * (part + 2)].astype(bf16)


def edge_kernel(first, *refs):
    senders, receivers, live, lengths = refs[:4]
    total, left, right = refs[-3:]
    step = pl.program_id(0)
    reach = lengths[...]
    turn = reach * (0.5 / cutoff_radius)
    envelope = 0.5 * (horner(COS_TURN, turn * turn) + 1.0) * live[...].astype(f32)
    centers = 0.5 + basis_width * iota((NB, CHUNK), 0).astype(f32)
    offset = (reach - centers) * (1.0 / basis_width)
    weights = (jnp.exp(-offset * offset) * envelope).astype(bf16)
    atom = iota((ATOMS, CHUNK), 0)
    onehot = (atom == receivers[...]).astype(f32).astype(bf16)
    for b in range(NB):
        left[ATOMS * b : ATOMS * (b + 1), :] = onehot * weights[b : b + 1, :]
    source = iota((EXT, CHUNK), 0)
    right[...] = (source == senders[...]).astype(f32).astype(bf16)

    @pl.when(step == 0)
    def _():
        total[...] = jnp.zeros_like(total) if first else refs[4][...]

    total[...] += dot_lanes(left[...], right[...])


def aggregate_kernel(feats, below, above, up, down, w_message, operator, w_radial, aggregate, radial_rows, extended):
    place = place_in_row()
    extended[0:ATOMS, :] = feats[...]
    first, last = 2 * KB, 2 * KB + GHOST
    extended[ATOMS : ATOMS + GHOST, :] = jnp.where(place == 0, up[first:last, :], below[...])
    extended[ATOMS + GHOST :, :] = jnp.where(place == ROW - 1, down[last:, :], above[...])
    rows = dot(extended[...], w_message[...]).astype(bf16)
    high, low = split(operator[...])
    products = dot(high, rows) + dot(low, rows)
    radial_rows[...] = products
    total = jnp.zeros((ATOMS, C), f32)
    for b in range(NB):
        total = total + w_radial[b : b + 1, :] * products[ATOMS * b : ATOMS * (b + 1)]
    aggregate[...] = total * edge_scale


def update_kernel(
    held, near, across, corner, aggregate, cotangent, w_out, extended, w_message, operator, radial_rows, w_radial,
    act_out, own_total, own_rows, own_quarter, own_radial, send_near, send_across, send_corner, grads,
):
    preact = aggregate[...] + tree(held[...], near[...], across[...], corner[...])
    sig = jax.nn.sigmoid(preact)
    grad_act = dot_lanes(cotangent[...], w_out[...])
    grad = grad_act * sig * (1.0 + preact * (1.0 - sig))
    rounded = grad.astype(bf16)
    grad = grad * edge_scale
    stacked = jnp.concatenate([w_radial[b : b + 1, :] * grad for b in range(NB)], axis=0).astype(bf16)
    high, low = split(operator[...])
    grad_msg = (dot_rows(high, stacked) + dot_rows(low, stacked)).astype(bf16)
    grad_rows = dot_lanes(grad_msg, w_message[...])
    own_total[...] = cotangent[...].astype(f32) + grad_rows[:ATOMS]
    own_rows[0:ATOMS, :] = rounded
    own_rows[ATOMS:, :] = grad_rows[ATOMS:].astype(bf16)
    act = (preact * sig).astype(bf16)
    act_out[...] = act
    grad_message = dot_rows(extended[...], grad_msg)
    grad_out = dot_rows(act, cotangent[...])
    for t in range(ROW):
        grads[PART * t : PART * t + 16, :] = grad_message[16 * t : 16 * (t + 1)]
        grads[PART * t + 16 : PART * (t + 1), :] = grad_out[16 * t : 16 * (t + 1)]
    at = iota((16, C), 0)
    tail = jnp.zeros((16, C), f32)
    for b in range(NB):
        part = jnp.sum(grad * radial_rows[ATOMS * b : ATOMS * (b + 1), :], axis=0, keepdims=True)
        tail = jnp.where(at == b, part, tail)
    tail = tail.astype(bf16)
    own_radial[...] = tail
    own_quarter[...] = grads[z_at(0, QUARTER), :]
    for part, send in ((1, send_near), (2, send_across), (3, send_corner)):
        send[0:EXT, :] = own_rows[...]
        send[EXT : EXT + QUARTER, :] = grads[z_at(part, QUARTER), :].astype(bf16)
        send[EXT + QUARTER :, :] = tail


def updated_kernel(feats, act, w_out, updated, token):
    total = feats[...].astype(f32) + dot(act[...], w_out[...])
    updated[...] = total.astype(bf16)
    token[...] = total[0:8]


def join_kernel(own_rows, own_quarter, own_radial, near, across, corner, joined, kept, sums):
    quarter = own_quarter[...]
    for part, rows in enumerate((own_rows, near, across, corner)):
        joined[ATOMS * part : ATOMS * (part + 1), :] = rows[0:ATOMS, :]
        start = HALF + 2 * GHOST * part
        joined[start : start + 2 * GHOST, :] = rows[ATOMS:EXT, :]
        if part:
            quarter = quarter + rows[EXT : EXT + QUARTER, :].astype(f32)
    sums[...] = quarter
    kept[...] = sums[rows_at(core(), PART), :]
    ends = HALF + 8 * GHOST
    joined[ends : ends + PART, :] = sums[rows_at(1 - core(), PART), :].astype(bf16)
    last = slice(EXT + QUARTER, EXT + QUARTER + 16)
    joined[ends + PART :, :] = tree(own_radial[...], near[last, :], across[last, :], corner[last, :]).astype(bf16)


def back_near_kernel(table, joined, sums):
    sums[...] = dot(table[...], joined[0:HALF, :])


def back_far_kernel(table, received, joined, kept, near_sums, message, over, back_down, back_up, ghosts):
    total = (near_sums[...] + dot(table[...], received[0:HALF, :])).astype(bf16)
    ends = HALF + 8 * GHOST
    part = (kept[...] + received[ends : ends + PART, :].astype(f32)).astype(bf16)
    radial = (joined[ends + PART :, :].astype(f32) + received[ends + PART :, :].astype(f32)).astype(bf16)
    for target in (message, over):
        target[0 : 2 * KB, :] = total
        target[2 * KB : 2 * KB + PART, :] = part
        target[2 * KB + PART : 2 * KB + PART + 16, :] = radial
    ghosts[0 : 8 * GHOST, :] = joined[HALF:ends, :]
    ghosts[8 * GHOST :, :] = received[HALF:ends, :]
    place = place_in_row()

    def returned(owner, above):
        start = at_block(place ^ owner, 2 * GHOST) + above * GHOST
        return ghosts[pl.ds(pl.multiple_of(start, GHOST), GHOST), :]

    back_down[...] = returned((place + ROW - 1) % ROW, 1)
    back_up[...] = returned((place + 1) % ROW, 0)
    first = 2 * KB + PART + 16
    message[first : first + GHOST, :] = returned(ROW - 1, 1)
    message[first + GHOST :, :] = returned(0, 0)


def charge_back_kernel(
    own, up, down, over, filt, near, far, near_gain, far_gain, near_rows, far_rows,
    send, keep, charge, early, rounded, sums,
):
    field = field_of(column_sum(own, up, down, over, slice(0, 2 * KB)), filt, inv_waves * inv_atoms)
    early[...] = column_sum(own, up, down, over, slice(2 * KB, 2 * KB + PART + 16)).astype(bf16)
    send[0:HALF, :] = (dot_rows(far[...], field) * far_gain[...]).astype(bf16)
    values = dot_rows(near[...], field) * near_gain[...]
    keep[...] = values
    rounded[...] = values.astype(bf16)
    total = jnp.zeros((C, C), f32)
    for j in range(ROW // 2):
        rows, atoms = slice(PACK * j, PACK * j + ATOMS), slice(ATOMS * j, ATOMS * (j + 1))
        total = total + dot_rows(near_rows[rows, :], rounded[atoms, :])
        total = total + dot_rows(far_rows[rows, :], send[atoms, :])
    sums[...] = total
    charge[...] = sums[rows_at(core(), LOW), :]
    send[HALF:, :] = sums[rows_at(1 - core(), LOW), :].astype(bf16)


def tail_spread_kernel(held, charge, early, received, own, charge_out, *sends):
    values = held[...] + received[0:HALF, :].astype(f32)
    total = (charge[...] + received[HALF:, :].astype(f32)).astype(bf16)
    own[...] = values[0:ATOMS]
    charge_out[...] = total
    for part, send in enumerate(sends):
        send[0:ATOMS, :] = values[ATOMS * (part + 1) : ATOMS * (part + 2)].astype(bf16)
        send[ATOMS : ATOMS + LOW, :] = total
        send[ATOMS + LOW :, :] = early[0:PART, :]


def raw_kernel(held, charge, early, near, across, corner, raw, charge_out, grads):
    rows = slice(0, ATOMS)
    raw[...] = tree(held[...], near[rows, :], across[rows, :], corner[rows, :]).astype(bf16)
    rows = slice(ATOMS, ATOMS + LOW)
    charge_out[...] = tree(charge[...], near[rows, :], across[rows, :], corner[rows, :]).astype(bf16)
    grads[z_at(0, PART), :] = early[0:PART, :]
    for part, received in ((1, near), (2, across), (3, corner)):
        grads[z_at(part, PART), :] = received[ATOMS + LOW :, :]


def charge_sum_kernel(own, up, down, over, grads, early, out):
    out[0:LOW, :] = column_sum(own, up, down, over, slice(0, LOW)).astype(bf16)
    out[LOW : LOW + C, :] = grads[...]
    out[LOW + C :, :] = early[PART:, :]


def cell_sum_kernel(own, near, across, corner, out):
    out[...] = tree(own[...], near[...], across[...], corner[...]).astype(bf16)


def feature_kernel(raw, w_charge, own, downs, ups, back_down, back_up, up, down, out, token):
    place = place_in_row()
    first, last = 2 * KB + PART + 16, 2 * KB + PART + 16 + GHOST
    returned = jnp.where(place == 0, up[first:last, :], back_down[...])
    total = own[...] + dot_lanes(raw[...], w_charge[...])
    atom = iota((ATOMS, GHOST), 0)
    total = total + dot((atom == downs[...]).astype(f32).astype(bf16), returned)
    returned = jnp.where(place == ROW - 1, down[last:, :], back_up[...])
    total = total + dot((atom == ups[...]).astype(f32).astype(bf16), returned)
    out[...] = total.astype(bf16)
    token[...] = total[0:8]


def weights_kernel(own, other, own_cell, other_cell, charge, message, radial, out):
    for first, second, at in ((own, own_cell, core()), (other, other_cell, 1 - core())):
        total = (first[...].astype(f32) + second[...].astype(f32)) * grad_scale
        charge[rows_at(at, LOW), :] = total[0:LOW]
        for z in range(4):
            start = LOW + PART * z
            message[rows_at(2 * z + at, 16), :] = total[start : start + 16]
            out[rows_at(2 * z + at, 16), :] = total[start + 16 : start + PART]
        radial[...] = total[LOW + C : LOW + C + NB]


def swap(values, axis, mask):
    count = lax.axis_size(axis)
    return lax.ppermute(values, axis, [(i, i ^ mask) for i in range(count)])


def from_y(values, by):
    return lax.ppermute(values, "dom", [(i, (i + ROW * by) % DOMS) for i in range(DOMS)])


def per_device(
    feats,
    positions,
    species,
    wave_vectors,
    smearing,
    species_gain,
    w_charge,
    w_message,
    w_radial,
    w_out,
    edge_sender,
    edge_receiver,
    edge_mask,
    edge_length,
    ghost_down,
    ghost_up,
    cotangent,
):
    own_rows = feats[0]
    cot = cotangent[0]

    def edges(first, count, total, after):
        spec = pl.BlockSpec((1, CHUNK), lambda e: (0, first + e))
        whole = pl.BlockSpec((NB * ATOMS, EXT), lambda e: (0, 0))
        held = [] if total is None else [total]
        (out,) = call(
            lambda *refs: edge_kernel(total is None, *refs),
            [((NB * ATOMS, EXT), f32)],
            *edge_arrays, *held,
            scratch=[pltpu.VMEM((NB * ATOMS, CHUNK), bf16), pltpu.VMEM((EXT, CHUNK), bf16)],
            flops=count * 2 * NB * ATOMS * CHUNK * 256,
            grid=(count,),
            in_specs=[spec] * 4 + [whole] * len(held),
            out_specs=[whole],
            after=after,
            name="edges",
        )
        return out

    in_place = pl.BlockSpec(memory_space=pltpu.HBM)
    arrays = (
        own_rows, positions.transpose(1, 0, 2), species, ghost_down, ghost_up,
        edge_sender, edge_receiver, edge_mask, edge_length,
    )
    packed, *edge_arrays = call(
        pack_kernel,
        [((PACK, C), bf16)] + [((1, EDGES), jnp.int32)] * 3 + [((1, EDGES), f32)],
        *[pltpu.with_memory_space_constraint(values, pltpu.HBM) for values in arrays],
        scratch=[
            pltpu.VMEM((16, C), f32), pltpu.VMEM((ATOMS, C), bf16), pltpu.VMEM((3, 1, ATOMS), f32),
            pltpu.VMEM((1, ATOMS), jnp.int32), pltpu.VMEM((2, 1, GHOST), jnp.int32), pltpu.SemaphoreType.DMA((9,)),
        ],
        in_specs=[in_place] * 9,
        out_specs=[pl.BlockSpec(memory_space=pltpu.VMEM)] * 5,
        name="pack",
    )
    operator = edges(0, EDGE_STEPS[0], None, [packed])
    (near_rows,) = call(
        gather_kernel,
        [((ROW // 2 * PACK, C), bf16)],
        packed, *[swap(packed, "dom", mask) for mask in (2, 4, 6)],
        after=[operator],
        name="gather",
    )
    far_rows = swap(near_rows, "dom", 1)
    near, near_sums, filt, near_gain = call(
        structure_near_kernel,
        [((2 * KB, HALF), bf16), ((2 * KB, C), f32), ((KB, C), f32), ((HALF, C), f32)],
        near_rows, wave_vectors, smearing[None], species_gain, w_charge,
        scratch=[pltpu.VMEM((HALF, C), bf16)],
        name="structure_near",
    )
    far, sums, message, far_gain, below, above = call(
        structure_far_kernel,
        [
            ((2 * KB, HALF), bf16), ((2 * KB, C), bf16), ((2 * KB + 2 * GHOST, C), bf16), ((HALF, C), f32),
            ((GHOST, C), bf16), ((GHOST, C), bf16),
        ],
        far_rows, near_rows, near_sums, wave_vectors, species_gain, w_charge,
        scratch=[pltpu.VMEM((HALF, C), bf16), pltpu.VMEM((ROW * PACK, C), bf16)],
        name="structure_far",
    )
    up, down, over = from_y(message, 1), from_y(message, -1), from_y(sums, 2)
    operator = edges(EDGE_STEPS[0], EDGE_STEPS[1], operator, [message])
    send, keep = call(
        potential_kernel,
        [((HALF, C), bf16), ((HALF, C), f32)],
        sums, up, down, over, filt, near, far,
        after=[operator],
        name="potential",
    )
    received = swap(send, "dom", 1)
    operator = edges(EDGE_STEPS[0] + EDGE_STEPS[1], EDGE_STEPS[2], operator, [send])
    held, *sends = call(
        spread_kernel, [((ATOMS, C), f32)] + [((ATOMS, C), bf16)] * 3, keep, received, after=[operator], name="spread"
    )
    parts = [swap(values, "dom", 2 * (part + 1)) for part, values in enumerate(sends)]
    operator = edges(sum(EDGE_STEPS[:3]), EDGE_STEPS[3], operator, [held])
    aggregate, radial_rows, extended = call(
        aggregate_kernel,
        [((ATOMS, C), f32), ((NB * ATOMS, C), f32), ((EXT, C), bf16)],
        own_rows, below, above, up, down, w_message, operator, w_radial,
        name="aggregate",
    )
    act, own_total, back_rows, quarter, radial, *sends = call(
        update_kernel,
        [((ATOMS, C), bf16), ((ATOMS, C), f32), ((EXT, C), bf16), ((QUARTER, C), f32), ((16, C), bf16)]
        + [((EXT + QUARTER + 16, C), bf16)] * 3,
        held, *parts, aggregate, cot, w_out, extended, w_message, operator, radial_rows, w_radial,
        scratch=[pltpu.VMEM((2 * C, C), f32)],
        name="update",
    )
    parts = [swap(values, "dom", 2 * (part + 1)) for part, values in enumerate(sends)]
    updated, token = call(
        updated_kernel, [((ATOMS, C), bf16), ((8, C), f32)], own_rows, act, w_out, after=[sends[0]], name="updated"
    )
    joined, kept = call(
        join_kernel,
        [((HALF + 8 * GHOST + PART + 16, C), bf16), ((PART, C), f32)],
        back_rows, quarter, radial, *parts,
        scratch=[pltpu.VMEM((QUARTER, C), f32)],
        after=[token],
        name="join",
    )
    received = swap(joined, "dom", 1)
    (near_sums,) = call(back_near_kernel, [((2 * KB, C), f32)], near, joined, name="back_near")
    message, over, back_down, back_up = call(
        back_far_kernel,
        [
            ((2 * KB + PART + 16 + 2 * GHOST, C), bf16), ((2 * KB + PART + 16, C), bf16),
            ((GHOST, C), bf16), ((GHOST, C), bf16),
        ],
        far, received, joined, kept, near_sums,
        scratch=[pltpu.VMEM((16 * GHOST, C), bf16)],
        name="back_far",
    )
    up, down, over = from_y(message, 1), from_y(message, -1), from_y(over, 2)
    send, keep, charge, early = call(
        charge_back_kernel,
        [((HALF + LOW, C), bf16), ((HALF, C), f32), ((LOW, C), f32), ((PART + 16, C), bf16)],
        message, up, down, over, filt, near, far, near_gain, far_gain, near_rows, far_rows,
        scratch=[pltpu.VMEM((HALF, C), bf16), pltpu.VMEM((C, C), f32)],
        name="charge_back",
    )
    received = swap(send, "dom", 1)
    held, charge, *sends = call(
        tail_spread_kernel,
        [((ATOMS, C), f32), ((LOW, C), bf16)] + [((ATOMS + LOW + PART, C), bf16)] * 3,
        keep, charge, early, received,
        name="tail_spread",
    )
    parts = [swap(values, "dom", 2 * (part + 1)) for part, values in enumerate(sends)]
    raw, charge, grads = call(
        raw_kernel,
        [((ATOMS, C), bf16), ((LOW, C), bf16), ((C, C), bf16)],
        held, charge, early, *parts,
        name="raw",
    )
    parts = [from_y(charge, by) for by in (1, -1, 2)]
    feat_grad, token = call(
        feature_kernel,
        [((ATOMS, C), bf16), ((8, C), f32)],
        raw, w_charge, own_total, ghost_down, ghost_up, back_down, back_up, up, down,
        name="feature",
    )
    (total,) = call(
        charge_sum_kernel, [((LOW + C + 16, C), bf16)], charge, *parts, grads, early, after=[token], name="charge_sum"
    )
    parts = [swap(total, "cell", mask) for mask in (2, 4, 6)]
    (total,) = call(cell_sum_kernel, [((LOW + C + 16, C), bf16)], total, *parts, name="cell_sum")
    parts = [swap(total, "dom", 1)] + [swap(total, ("cell", "dom"), DOMS + mask) for mask in (6, 7)]
    charge, message, radial, out = call(
        weights_kernel,
        [((C, C), f32), ((C, C), f32), ((NB, C), f32), ((C, C), f32)],
        total, *parts,
        name="weights",
    )
    return updated[None], feat_grad[None], charge, message, radial, out


def solution(mesh):
    placed = (
        P("cell", "dom", None),
        P("cell", None, "dom"),
        P("cell", "dom"),
        P(),
        P(),
        P(),
        P(),
        P(),
        P(),
        P(),
        P("cell", "dom"),
        P("cell", "dom"),
        P("cell", "dom"),
        P("cell", "dom"),
        P("cell", "dom"),
        P("cell", "dom"),
        P("cell", "dom", None),
    )
    return jax.shard_map(
        per_device,
        mesh=mesh,
        in_specs=placed,
        out_specs=(P("cell", "dom", None), P("cell", "dom", None), P(), P(), P(), P()),
        check_vma=False,
    )
```

```python
import math

import jax
import jax.numpy as jnp
from jax import lax
from jax.experimental import pallas as pl
from jax.experimental.pallas import tpu as pltpu
from jax.sharding import PartitionSpec as P

bf16 = jnp.bfloat16
f32 = jnp.float32

C = 128
K = 2048
NB = 8
ATOMS = 128
GHOST = 32
EXT = ATOMS + 2 * GHOST
EDGES = 12288
DOMS = 32
CELLS = 8
ROW = 8
KB = K // ROW
PACK = ATOMS + 16
QUARTER = 64
PART = QUARTER // 2
LOW = C // 2
HALF = ROW * ATOMS // 2
CHUNK = 1024
EDGE_STEPS = (5, 7)

cutoff_radius = 6.0
basis_width = 0.75
edge_scale = 0.25
filter_factor = 12.0
inv_waves = 1.0 / math.sqrt(K)
inv_atoms = 1.0 / math.sqrt(ATOMS * DOMS)
grad_scale = 1.0 / math.sqrt(CELLS * ATOMS * DOMS)

COS_TURN = (
    0.9999999890754399,
    -19.73920450099313,
    64.93911749956553,
    -85.45013994347214,
    60.16763282514798,
    -25.967602441408868,
    6.528658639370483,
)
SIN_TURN = (
    6.283184916984331,
    -41.34158926418157,
    81.59994386455666,
    -76.61447586020026,
    41.342889428722025,
    -12.471244745942547,
)


def horner(coefficients, x):
    total = jnp.full_like(x, coefficients[-1])
    for value in coefficients[-2::-1]:
        total = total * x + value
    return total


def iota(shape, axis):
    return lax.broadcasted_iota(jnp.int32, shape, axis)


def dot(left, right):
    return jnp.dot(left, right, preferred_element_type=f32)


def dot_rows(left, right):
    return lax.dot_general(left, right, (((0,), (0,)), ((), ())), preferred_element_type=f32)


def dot_lanes(left, right):
    return lax.dot_general(left, right, (((1,), (1,)), ((), ())), preferred_element_type=f32)


def split(values):
    high = values.astype(bf16)
    return high, (values - high.astype(f32)).astype(bf16)


def call(kernel, outs, *args, scratch=(), flops=0, after=(), name=None, **more):
    def run(*refs):
        kernel(*refs[: len(args)], *refs[len(args) + len(after) :])

    if "in_specs" not in more:
        more["in_specs"] = [pl.BlockSpec(memory_space=pltpu.VMEM)] * len(args)
        more["out_specs"] = [pl.BlockSpec(memory_space=pltpu.VMEM)] * len(outs)
    more["in_specs"] = more["in_specs"] + [pl.BlockSpec(memory_space=pl.ANY)] * len(after)
    return pl.pallas_call(
        run,
        out_shape=[jax.ShapeDtypeStruct(shape, dtype) for shape, dtype in outs],
        scratch_shapes=list(scratch),
        compiler_params=pltpu.CompilerParams(vmem_limit_bytes=40 * 1024 * 1024),
        cost_estimate=pl.CostEstimate(flops=flops, bytes_accessed=1 << 18, transcendentals=0),
        name=name,
        **more,
    )(*args, *after)


def place_in_row():
    return lax.rem(lax.axis_index("dom"), ROW)


def at_block(mask, rows):
    return pl.multiple_of((mask // 2 + (mask % 2) * (ROW // 2)) * rows, rows)


def rows_at(index, count):
    return pl.ds(pl.multiple_of(index * count, count), count)


def z_at(part, count):
    return rows_at((place_in_row() // 2) ^ part, count)


def core():
    return lax.rem(lax.axis_index("dom"), 2)


def tree(own, near, across, corner):
    return (own.astype(f32) + near.astype(f32)) + (across.astype(f32) + corner.astype(f32))


def pack_kernel(
    feats, coords, kinds, downs, ups, sent, got, live, reach,
    packed, senders, receivers, mask, lengths, tail, whole, places, labels, indices, sems,
):
    near = [(feats, whole), (coords, places), (kinds, labels), (ups, indices.at[0]), (downs, indices.at[1])]
    edges = [(sent, senders), (got, receivers), (live, mask), (reach, lengths)]
    copies = [
        pltpu.make_async_copy(source, target, sems.at[i]) for i, (source, target) in enumerate(near + edges)
    ]
    for copy in copies:
        copy.start()
    for copy in copies:
        copy.wait()
    packed[0:ATOMS, :] = whole[...]
    at = iota((16, ATOMS), 0)
    values = jnp.where(at == 9, labels[...].astype(f32), 0.0)
    for axis in range(3):
        place = places[axis]
        for part in range(3):
            piece = place.astype(bf16).astype(f32)
            values = jnp.where(at == 3 * part + axis, piece, values)
            place = place - piece
    tail[...] = values
    tail[10:11, 0:GHOST] = indices[0].astype(f32)
    tail[11:12, 0:GHOST] = indices[1].astype(f32)
    packed[ATOMS:PACK, :] = tail[...].astype(bf16)


def gather_kernel(own, near, across, corner, out):
    for part, rows in enumerate((own, near, across, corner)):
        out[PACK * part : PACK * (part + 1), :] = rows[...]


def wave_lanes(waves):
    mine = waves[:, pl.ds(pl.multiple_of(place_in_row() * KB, KB), KB)].astype(f32)
    at = iota((16, KB), 0)
    stacked = jnp.zeros((16, KB), f32)
    for axis in range(3):
        stacked = jnp.where(at == axis, mine[axis : axis + 1, :], stacked)
    stacked = stacked.astype(bf16)
    axis_at = iota((16, C), 0)
    return [dot_rows(stacked, (axis_at == axis).astype(f32).astype(bf16)) for axis in range(3)]


def tables_of(packed, lanes, species_gain, w_charge, table, gain, charges):
    kind_at = iota((8, ATOMS), 0).astype(f32)
    for j in range(ROW // 2):
        rows = packed[PACK * j : PACK * j + ATOMS, :]
        tail = packed[PACK * j + ATOMS : PACK * (j + 1), :].astype(f32)
        onehot = (tail[9:10, :] == kind_at).astype(f32)
        own_gain = lax.dot_general(
            onehot,
            species_gain[...],
            (((0,), (0,)), ((), ())),
            precision=lax.Precision.HIGHEST,
            preferred_element_type=f32,
        )
        span = slice(ATOMS * j, ATOMS * (j + 1))
        gain[span, :] = own_gain
        charges[span, :] = (dot(rows, w_charge[...]) * own_gain).astype(bf16)
        turns = jnp.zeros((KB, ATOMS), f32)
        for axis in range(3):
            place = tail[axis : axis + 1, :] + tail[axis + 3 : axis + 4, :] + tail[axis + 6 : axis + 7, :]
            turns = turns + place * lanes[axis]
        turns = turns - jnp.round(turns)
        square = turns * turns
        table[0:KB, span] = horner(COS_TURN, square).astype(bf16)
        table[KB : 2 * KB, span] = (turns * horner(SIN_TURN, square)).astype(bf16)


def structure_near_kernel(packed, waves, smearing, species_gain, w_charge, table, sums, filt, gain, charges):
    lanes = wave_lanes(waves)
    squared = lanes[0] * lanes[0] + lanes[1] * lanes[1] + lanes[2] * lanes[2]
    filt[...] = filter_factor * jnp.exp(-squared * smearing[...]) / jnp.sqrt(squared)
    tables_of(packed, lanes, species_gain, w_charge, table, gain, charges)
    sums[...] = dot(table[...], charges[...])


def structure_far_kernel(
    packed, near, near_sums, waves, species_gain, w_charge,
    table, sums, message, gain, below, above, charges, joined,
):
    tables_of(packed, wave_lanes(waves), species_gain, w_charge, table, gain, charges)
    total = (near_sums[...] + dot(table[...], charges[...])).astype(bf16)
    sums[...] = total
    message[0 : 2 * KB, :] = total
    joined[0 : PACK * ROW // 2, :] = near[...]
    joined[PACK * ROW // 2 :, :] = packed[...]
    place = place_in_row()
    atom = iota((ATOMS, GHOST), 0).astype(f32)

    def ghosts(owner, row):
        start = at_block(place ^ owner, PACK)
        rows = joined[pl.ds(start, ATOMS), :]
        tail = joined[pl.ds(pl.multiple_of(start + ATOMS, 16), 16), :].astype(f32)
        return dot_rows((atom == tail[row : row + 1, 0:GHOST]).astype(f32).astype(bf16), rows).astype(bf16)

    below[...] = ghosts((place + ROW - 1) % ROW, 10)
    above[...] = ghosts((place + 1) % ROW, 11)
    message[2 * KB : 2 * KB + GHOST, :] = ghosts(ROW - 1, 10)
    message[2 * KB + GHOST :, :] = ghosts(0, 11)


def column_sum(own, up, down, over, span):
    return tree(own[span, :], over[span, :], up[span, :], down[span, :])


def field_of(sums, filt, scale):
    weight = filt[...] * scale
    return jnp.concatenate(
        [(weight * sums[0:KB]).astype(bf16), (weight * sums[KB : 2 * KB]).astype(bf16)], axis=0
    )


def potential_kernel(own, up, down, over, filt, near, far, send, keep):
    field = field_of(column_sum(own, up, down, over, slice(0, 2 * KB)), filt, inv_atoms)
    send[...] = (dot_rows(far[...], field) * inv_waves).astype(bf16)
    keep[...] = dot_rows(near[...], field) * inv_waves


def spread_kernel(held, received, own, *sends):
    values = held[...] + received[...].astype(f32)
    own[...] = values[0:ATOMS]
    for part, send in enumerate(sends):
        send[...] = values[ATOMS * (part + 1) : ATOMS * (part + 2)].astype(bf16)


def edge_kernel(first, count, *refs):
    total, left, right = refs[-3:]
    for step in range(first, first + count):
        senders, receivers, live, reach = (ref[:, CHUNK * step : CHUNK * (step + 1)] for ref in refs[:4])
        turn = reach * (0.5 / cutoff_radius)
        envelope = 0.5 * (horner(COS_TURN, turn * turn) + 1.0) * live.astype(f32)
        centers = 0.5 + basis_width * iota((NB, CHUNK), 0).astype(f32)
        offset = (reach - centers) * (1.0 / basis_width)
        weights = (jnp.exp(-offset * offset) * envelope).astype(bf16)
        atom = iota((ATOMS, CHUNK), 0)
        onehot = (atom == receivers).astype(f32).astype(bf16)
        for b in range(NB):
            left[ATOMS * b : ATOMS * (b + 1), :] = onehot * weights[b : b + 1, :]
        source = iota((EXT, CHUNK), 0)
        right[...] = (source == senders).astype(f32).astype(bf16)
        products = dot_lanes(left[...], right[...])
        if step > first:
            total[...] += products
        elif first:
            total[...] = refs[4][...] + products
        else:
            total[...] = products


def aggregate_kernel(feats, below, above, up, down, w_message, operator, w_radial, aggregate, radial_rows, extended):
    place = place_in_row()
    extended[0:ATOMS, :] = feats[...]
    first, last = 2 * KB, 2 * KB + GHOST
    extended[ATOMS : ATOMS + GHOST, :] = jnp.where(place == 0, up[first:last, :], below[...])
    extended[ATOMS + GHOST :, :] = jnp.where(place == ROW - 1, down[last:, :], above[...])
    rows = dot(extended[...], w_message[...]).astype(bf16)
    high, low = split(operator[...])
    products = dot(high, rows) + dot(low, rows)
    radial_rows[...] = products
    total = jnp.zeros((ATOMS, C), f32)
    for b in range(NB):
        total = total + w_radial[b : b + 1, :] * products[ATOMS * b : ATOMS * (b + 1)]
    aggregate[...] = total * edge_scale


def update_kernel(
    held, near, across, corner, aggregate, cotangent, w_out, extended, w_message, operator, radial_rows, w_radial,
    act_out, own_total, own_rows, own_quarter, own_radial, send_near, send_across, send_corner, grads,
):
    preact = aggregate[...] + tree(held[...], near[...], across[...], corner[...])
    sig = jax.nn.sigmoid(preact)
    grad_act = dot_lanes(cotangent[...], w_out[...])
    grad = grad_act * sig * (1.0 + preact * (1.0 - sig))
    rounded = grad.astype(bf16)
    grad = grad * edge_scale
    stacked = jnp.concatenate([w_radial[b : b + 1, :] * grad for b in range(NB)], axis=0).astype(bf16)
    high, low = split(operator[...])
    grad_msg = (dot_rows(high, stacked) + dot_rows(low, stacked)).astype(bf16)
    grad_rows = dot_lanes(grad_msg, w_message[...])
    own_total[...] = cotangent[...].astype(f32) + grad_rows[:ATOMS]
    own_rows[0:ATOMS, :] = rounded
    own_rows[ATOMS:, :] = grad_rows[ATOMS:].astype(bf16)
    act = (preact * sig).astype(bf16)
    act_out[...] = act
    grad_message = dot_rows(extended[...], grad_msg)
    grad_out = dot_rows(act, cotangent[...])
    for t in range(ROW):
        grads[PART * t : PART * t + 16, :] = grad_message[16 * t : 16 * (t + 1)]
        grads[PART * t + 16 : PART * (t + 1), :] = grad_out[16 * t : 16 * (t + 1)]
    at = iota((16, C), 0)
    tail = jnp.zeros((16, C), f32)
    for b in range(NB):
        part = jnp.sum(grad * radial_rows[ATOMS * b : ATOMS * (b + 1), :], axis=0, keepdims=True)
        tail = jnp.where(at == b, part, tail)
    tail = tail.astype(bf16)
    own_radial[...] = tail
    own_quarter[...] = grads[z_at(0, QUARTER), :]
    for part, send in ((1, send_near), (2, send_across), (3, send_corner)):
        send[0:EXT, :] = own_rows[...]
        send[EXT : EXT + QUARTER, :] = grads[z_at(part, QUARTER), :].astype(bf16)
        send[EXT + QUARTER :, :] = tail


def updated_kernel(feats, act, w_out, updated, token):
    total = feats[...].astype(f32) + dot(act[...], w_out[...])
    updated[...] = total.astype(bf16)
    token[...] = total[0:8]


def join_kernel(own_rows, own_quarter, own_radial, near, across, corner, joined, kept, sums):
    quarter = own_quarter[...]
    for part, rows in enumerate((own_rows, near, across, corner)):
        joined[ATOMS * part : ATOMS * (part + 1), :] = rows[0:ATOMS, :]
        start = HALF + 2 * GHOST * part
        joined[start : start + 2 * GHOST, :] = rows[ATOMS:EXT, :]
        if part:
            quarter = quarter + rows[EXT : EXT + QUARTER, :].astype(f32)
    sums[...] = quarter
    kept[...] = sums[rows_at(core(), PART), :]
    ends = HALF + 8 * GHOST
    joined[ends : ends + PART, :] = sums[rows_at(1 - core(), PART), :].astype(bf16)
    last = slice(EXT + QUARTER, EXT + QUARTER + 16)
    joined[ends + PART :, :] = tree(own_radial[...], near[last, :], across[last, :], corner[last, :]).astype(bf16)


def back_near_kernel(table, joined, sums):
    sums[...] = dot(table[...], joined[0:HALF, :])


def back_far_kernel(table, received, joined, kept, near_sums, message, over, back_down, back_up, ghosts):
    total = (near_sums[...] + dot(table[...], received[0:HALF, :])).astype(bf16)
    ends = HALF + 8 * GHOST
    part = (kept[...] + received[ends : ends + PART, :].astype(f32)).astype(bf16)
    radial = (joined[ends + PART :, :].astype(f32) + received[ends + PART :, :].astype(f32)).astype(bf16)
    for target in (message, over):
        target[0 : 2 * KB, :] = total
        target[2 * KB : 2 * KB + PART, :] = part
        target[2 * KB + PART : 2 * KB + PART + 16, :] = radial
    ghosts[0 : 8 * GHOST, :] = joined[HALF:ends, :]
    ghosts[8 * GHOST :, :] = received[HALF:ends, :]
    place = place_in_row()

    def returned(owner, above):
        start = at_block(place ^ owner, 2 * GHOST) + above * GHOST
        return ghosts[pl.ds(pl.multiple_of(start, GHOST), GHOST), :]

    back_down[...] = returned((place + ROW - 1) % ROW, 1)
    back_up[...] = returned((place + 1) % ROW, 0)
    first = 2 * KB + PART + 16
    message[first : first + GHOST, :] = returned(ROW - 1, 1)
    message[first + GHOST :, :] = returned(0, 0)


def charge_back_kernel(
    own, up, down, over, filt, near, far, near_gain, far_gain, near_rows, far_rows,
    send, keep, charge, early, rounded, sums,
):
    field = field_of(column_sum(own, up, down, over, slice(0, 2 * KB)), filt, inv_waves * inv_atoms)
    early[...] = column_sum(own, up, down, over, slice(2 * KB, 2 * KB + PART + 16)).astype(bf16)
    send[0:HALF, :] = (dot_rows(far[...], field) * far_gain[...]).astype(bf16)
    values = dot_rows(near[...], field) * near_gain[...]
    keep[...] = values
    rounded[...] = values.astype(bf16)
    total = jnp.zeros((C, C), f32)
    for j in range(ROW // 2):
        rows, atoms = slice(PACK * j, PACK * j + ATOMS), slice(ATOMS * j, ATOMS * (j + 1))
        total = total + dot_rows(near_rows[rows, :], rounded[atoms, :])
        total = total + dot_rows(far_rows[rows, :], send[atoms, :])
    sums[...] = total
    charge[...] = sums[rows_at(core(), LOW), :]
    send[HALF:, :] = sums[rows_at(1 - core(), LOW), :].astype(bf16)


def tail_spread_kernel(held, charge, early, received, own, charge_out, *sends):
    values = held[...] + received[0:HALF, :].astype(f32)
    total = (charge[...] + received[HALF:, :].astype(f32)).astype(bf16)
    own[...] = values[0:ATOMS]
    charge_out[...] = total
    for part, send in enumerate(sends):
        send[0:ATOMS, :] = values[ATOMS * (part + 1) : ATOMS * (part + 2)].astype(bf16)
        send[ATOMS : ATOMS + LOW, :] = total
        send[ATOMS + LOW :, :] = early[0:PART, :]


def raw_kernel(held, charge, early, near, across, corner, raw, charge_out, grads):
    rows = slice(0, ATOMS)
    raw[...] = tree(held[...], near[rows, :], across[rows, :], corner[rows, :]).astype(bf16)
    rows = slice(ATOMS, ATOMS + LOW)
    charge_out[...] = tree(charge[...], near[rows, :], across[rows, :], corner[rows, :]).astype(bf16)
    grads[z_at(0, PART), :] = early[0:PART, :]
    for part, received in ((1, near), (2, across), (3, corner)):
        grads[z_at(part, PART), :] = received[ATOMS + LOW :, :]


def charge_sum_kernel(own, up, down, over, grads, early, out):
    out[0:LOW, :] = column_sum(own, up, down, over, slice(0, LOW)).astype(bf16)
    out[LOW : LOW + C, :] = grads[...]
    out[LOW + C :, :] = early[PART:, :]


def cell_sum_kernel(own, near, across, corner, out):
    out[...] = tree(own[...], near[...], across[...], corner[...]).astype(bf16)


def feature_kernel(raw, w_charge, own, downs, ups, back_down, back_up, up, down, out, token):
    place = place_in_row()
    first, last = 2 * KB + PART + 16, 2 * KB + PART + 16 + GHOST
    returned = jnp.where(place == 0, up[first:last, :], back_down[...])
    total = own[...] + dot_lanes(raw[...], w_charge[...])
    atom = iota((ATOMS, GHOST), 0)
    total = total + dot((atom == downs[...]).astype(f32).astype(bf16), returned)
    returned = jnp.where(place == ROW - 1, down[last:, :], back_up[...])
    total = total + dot((atom == ups[...]).astype(f32).astype(bf16), returned)
    out[...] = total.astype(bf16)
    token[...] = total[0:8]


def total_kernel(own, other_cell, total):
    total[...] = (own[...].astype(f32) + other_cell[...].astype(f32)) * grad_scale


def weights_kernel(own, other, charge, message, radial, out):
    for total, at in ((own, core()), (other, 1 - core())):
        charge[rows_at(at, LOW), :] = total[0:LOW, :]
        for z in range(4):
            start = LOW + PART * z
            message[rows_at(2 * z + at, 16), :] = total[start : start + 16, :]
            out[rows_at(2 * z + at, 16), :] = total[start + 16 : start + PART, :]
    radial[...] = own[LOW + C : LOW + C + NB, :]


def swap(values, axis, mask):
    count = lax.axis_size(axis)
    return lax.ppermute(values, axis, [(i, i ^ mask) for i in range(count)])


def from_y(values, by):
    return lax.ppermute(values, "dom", [(i, (i + ROW * by) % DOMS) for i in range(DOMS)])


def per_device(
    feats,
    positions,
    species,
    wave_vectors,
    smearing,
    species_gain,
    w_charge,
    w_message,
    w_radial,
    w_out,
    edge_sender,
    edge_receiver,
    edge_mask,
    edge_length,
    ghost_down,
    ghost_up,
    cotangent,
):
    own_rows = feats[0]
    cot = cotangent[0]

    def edges(first, count, total, after):
        (out,) = call(
            lambda *refs: edge_kernel(first, count, *refs),
            [((NB * ATOMS, EXT), f32)],
            *edge_arrays, *total,
            scratch=[pltpu.VMEM((NB * ATOMS, CHUNK), bf16), pltpu.VMEM((EXT, CHUNK), bf16)],
            flops=count * 2 * NB * ATOMS * CHUNK * 256,
            after=after,
            name="edges",
        )
        return out

    in_place = pl.BlockSpec(memory_space=pltpu.HBM)
    arrays = (
        own_rows, positions.transpose(1, 0, 2), species, ghost_down, ghost_up,
        edge_sender, edge_receiver, edge_mask, edge_length,
    )
    packed, *edge_arrays = call(
        pack_kernel,
        [((PACK, C), bf16)] + [((1, EDGES), jnp.int32)] * 3 + [((1, EDGES), f32)],
        *[pltpu.with_memory_space_constraint(values, pltpu.HBM) for values in arrays],
        scratch=[
            pltpu.VMEM((16, C), f32), pltpu.VMEM((ATOMS, C), bf16), pltpu.VMEM((3, 1, ATOMS), f32),
            pltpu.VMEM((1, ATOMS), jnp.int32), pltpu.VMEM((2, 1, GHOST), jnp.int32), pltpu.SemaphoreType.DMA((9,)),
        ],
        in_specs=[in_place] * 9,
        out_specs=[pl.BlockSpec(memory_space=pltpu.VMEM)] * 5,
        name="pack",
    )
    operator = edges(0, EDGE_STEPS[0], [], [packed])
    (near_rows,) = call(
        gather_kernel,
        [((ROW // 2 * PACK, C), bf16)],
        packed, *[swap(packed, "dom", mask) for mask in (2, 4, 6)],
        after=[operator],
        name="gather",
    )
    far_rows = swap(near_rows, "dom", 1)
    near, near_sums, filt, near_gain = call(
        structure_near_kernel,
        [((2 * KB, HALF), bf16), ((2 * KB, C), f32), ((KB, C), f32), ((HALF, C), f32)],
        near_rows, wave_vectors, smearing[None], species_gain, w_charge,
        scratch=[pltpu.VMEM((HALF, C), bf16)],
        name="structure_near",
    )
    far, sums, message, far_gain, below, above = call(
        structure_far_kernel,
        [
            ((2 * KB, HALF), bf16), ((2 * KB, C), bf16), ((2 * KB + 2 * GHOST, C), bf16), ((HALF, C), f32),
            ((GHOST, C), bf16), ((GHOST, C), bf16),
        ],
        far_rows, near_rows, near_sums, wave_vectors, species_gain, w_charge,
        scratch=[pltpu.VMEM((HALF, C), bf16), pltpu.VMEM((ROW * PACK, C), bf16)],
        name="structure_far",
    )
    up, down, over = from_y(message, 1), from_y(message, -1), from_y(sums, 2)
    operator = edges(EDGE_STEPS[0], EDGE_STEPS[1], [operator], [message])
    send, keep = call(
        potential_kernel,
        [((HALF, C), bf16), ((HALF, C), f32)],
        sums, up, down, over, filt, near, far,
        after=[operator],
        name="potential",
    )
    received = swap(send, "dom", 1)
    held, *sends = call(
        spread_kernel, [((ATOMS, C), f32)] + [((ATOMS, C), bf16)] * 3, keep, received, name="spread"
    )
    parts = [swap(values, "dom", 2 * (part + 1)) for part, values in enumerate(sends)]
    aggregate, radial_rows, extended = call(
        aggregate_kernel,
        [((ATOMS, C), f32), ((NB * ATOMS, C), f32), ((EXT, C), bf16)],
        own_rows, below, above, up, down, w_message, operator, w_radial,
        name="aggregate",
    )
    act, own_total, back_rows, quarter, radial, *sends = call(
        update_kernel,
        [((ATOMS, C), bf16), ((ATOMS, C), f32), ((EXT, C), bf16), ((QUARTER, C), f32), ((16, C), bf16)]
        + [((EXT + QUARTER + 16, C), bf16)] * 3,
        held, *parts, aggregate, cot, w_out, extended, w_message, operator, radial_rows, w_radial,
        scratch=[pltpu.VMEM((2 * C, C), f32)],
        name="update",
    )
    parts = [swap(values, "dom", 2 * (part + 1)) for part, values in enumerate(sends)]
    updated, token = call(
        updated_kernel, [((ATOMS, C), bf16), ((8, C), f32)], own_rows, act, w_out, after=[sends[0]], name="updated"
    )
    joined, kept = call(
        join_kernel,
        [((HALF + 8 * GHOST + PART + 16, C), bf16), ((PART, C), f32)],
        back_rows, quarter, radial, *parts,
        scratch=[pltpu.VMEM((QUARTER, C), f32)],
        after=[token],
        name="join",
    )
    received = swap(joined, "dom", 1)
    (near_sums,) = call(back_near_kernel, [((2 * KB, C), f32)], near, joined, name="back_near")
    message, over, back_down, back_up = call(
        back_far_kernel,
        [
            ((2 * KB + PART + 16 + 2 * GHOST, C), bf16), ((2 * KB + PART + 16, C), bf16),
            ((GHOST, C), bf16), ((GHOST, C), bf16),
        ],
        far, received, joined, kept, near_sums,
        scratch=[pltpu.VMEM((16 * GHOST, C), bf16)],
        name="back_far",
    )
    up, down, over = from_y(message, 1), from_y(message, -1), from_y(over, 2)
    send, keep, charge, early = call(
        charge_back_kernel,
        [((HALF + LOW, C), bf16), ((HALF, C), f32), ((LOW, C), f32), ((PART + 16, C), bf16)],
        message, up, down, over, filt, near, far, near_gain, far_gain, near_rows, far_rows,
        scratch=[pltpu.VMEM((HALF, C), bf16), pltpu.VMEM((C, C), f32)],
        name="charge_back",
    )
    received = swap(send, "dom", 1)
    held, charge, *sends = call(
        tail_spread_kernel,
        [((ATOMS, C), f32), ((LOW, C), bf16)] + [((ATOMS + LOW + PART, C), bf16)] * 3,
        keep, charge, early, received,
        name="tail_spread",
    )
    parts = [swap(values, "dom", 2 * (part + 1)) for part, values in enumerate(sends)]
    raw, charge, grads = call(
        raw_kernel,
        [((ATOMS, C), bf16), ((LOW, C), bf16), ((C, C), bf16)],
        held, charge, early, *parts,
        name="raw",
    )
    parts = [from_y(charge, by) for by in (1, -1, 2)]
    feat_grad, token = call(
        feature_kernel,
        [((ATOMS, C), bf16), ((8, C), f32)],
        raw, w_charge, own_total, ghost_down, ghost_up, back_down, back_up, up, down,
        name="feature",
    )
    (total,) = call(
        charge_sum_kernel, [((LOW + C + 16, C), bf16)], charge, *parts, grads, early, after=[token], name="charge_sum"
    )
    parts = [swap(total, "cell", mask) for mask in (2, 4, 6)]
    (total,) = call(cell_sum_kernel, [((LOW + C + 16, C), bf16)], total, *parts, name="cell_sum")
    received = swap(total, ("cell", "dom"), DOMS + 6)
    (total,) = call(total_kernel, [((LOW + C + 16, C), f32)], total, received, name="total")
    charge, message, radial, out = call(
        weights_kernel,
        [((C, C), f32), ((C, C), f32), ((NB, C), f32), ((C, C), f32)],
        total, swap(total, "dom", 1),
        name="weights",
    )
    return updated[None], feat_grad[None], charge, message, radial, out


def solution(mesh):
    placed = (
        P("cell", "dom", None),
        P("cell", None, "dom"),
        P("cell", "dom"),
        P(),
        P(),
        P(),
        P(),
        P(),
        P(),
        P(),
        P("cell", "dom"),
        P("cell", "dom"),
        P("cell", "dom"),
        P("cell", "dom"),
        P("cell", "dom"),
        P("cell", "dom"),
        P("cell", "dom", None),
    )
    return jax.shard_map(
        per_device,
        mesh=mesh,
        in_specs=placed,
        out_specs=(P("cell", "dom", None), P("cell", "dom", None), P(), P(), P(), P()),
        check_vma=False,
    )
```

```python
import math

import jax
import jax.numpy as jnp
from jax import lax
from jax.experimental import pallas as pl
from jax.experimental.pallas import tpu as pltpu
from jax.sharding import PartitionSpec as P

bf16 = jnp.bfloat16
f32 = jnp.float32

C = 128
K = 2048
NB = 8
ATOMS = 128
GHOST = 32
EXT = ATOMS + 2 * GHOST
EDGES = 12288
DOMS = 32
CELLS = 8
ROW = 8
KB = K // ROW
PACK = ATOMS + 16
QUARTER = 64
PART = QUARTER // 2
NEAR = ROW // 2 * PACK
COLUMN = 4
HALF = ROW * ATOMS // 2
CHUNK = 1024
EDGE_STEPS = (5, 7)

cutoff_radius = 6.0
basis_width = 0.75
edge_scale = 0.25
filter_factor = 12.0
inv_waves = 1.0 / math.sqrt(K)
inv_atoms = 1.0 / math.sqrt(ATOMS * DOMS)
grad_scale = 1.0 / math.sqrt(CELLS * ATOMS * DOMS)

COS_TURN = (
    0.9999999890754399,
    -19.73920450099313,
    64.93911749956553,
    -85.45013994347214,
    60.16763282514798,
    -25.967602441408868,
    6.528658639370483,
)
SIN_TURN = (
    6.283184916984331,
    -41.34158926418157,
    81.59994386455666,
    -76.61447586020026,
    41.342889428722025,
    -12.471244745942547,
)


def horner(coefficients, x):
    total = jnp.full_like(x, coefficients[-1])
    for value in coefficients[-2::-1]:
        total = total * x + value
    return total


def iota(shape, axis):
    return lax.broadcasted_iota(jnp.int32, shape, axis)


def dot(left, right):
    return jnp.dot(left, right, preferred_element_type=f32)


def dot_rows(left, right):
    return lax.dot_general(left, right, (((0,), (0,)), ((), ())), preferred_element_type=f32)


def dot_lanes(left, right):
    return lax.dot_general(left, right, (((1,), (1,)), ((), ())), preferred_element_type=f32)


def split(values):
    high = values.astype(bf16)
    return high, (values - high.astype(f32)).astype(bf16)


def call(kernel, outs, *args, scratch=(), flops=0, after=(), name=None, **more):
    def run(*refs):
        kernel(*refs[: len(args)], *refs[len(args) + len(after) :])

    if "in_specs" not in more:
        more["in_specs"] = [pl.BlockSpec(memory_space=pltpu.VMEM)] * len(args)
        more["out_specs"] = [pl.BlockSpec(memory_space=pltpu.VMEM)] * len(outs)
    more["in_specs"] = more["in_specs"] + [pl.BlockSpec(memory_space=pl.ANY)] * len(after)
    return pl.pallas_call(
        run,
        out_shape=[jax.ShapeDtypeStruct(shape, dtype) for shape, dtype in outs],
        scratch_shapes=list(scratch),
        compiler_params=pltpu.CompilerParams(vmem_limit_bytes=40 * 1024 * 1024),
        cost_estimate=pl.CostEstimate(flops=flops, bytes_accessed=1 << 18, transcendentals=0),
        name=name,
        **more,
    )(*args, *after)


def place_in_row():
    return lax.rem(lax.axis_index("dom"), ROW)


def at_block(mask, rows):
    return pl.multiple_of((mask // 2 + (mask % 2) * (ROW // 2)) * rows, rows)


def rows_at(index, count):
    return pl.ds(pl.multiple_of(index * count, count), count)


def z_at(part, count):
    quarter = (place_in_row() // 2) ^ (3 * lax.rem(lax.axis_index("cell"), 2))
    return rows_at(quarter ^ part, count)


def core():
    return lax.rem(lax.axis_index("dom"), 2)


def tree(own, near, across, corner):
    return (own.astype(f32) + near.astype(f32)) + (across.astype(f32) + corner.astype(f32))


def pack_kernel(
    feats, coords, kinds, downs, ups, sent, got, live, reach,
    packed, senders, receivers, mask, lengths, tail, whole, places, labels, indices, sems,
):
    near = [(feats, whole), (coords, places), (kinds, labels), (ups, indices.at[0]), (downs, indices.at[1])]
    edges = [(sent, senders), (got, receivers), (live, mask), (reach, lengths)]
    copies = [
        pltpu.make_async_copy(source, target, sems.at[i]) for i, (source, target) in enumerate(near + edges)
    ]
    for copy in copies:
        copy.start()
    for copy in copies[: len(near)]:
        copy.wait()
    packed[0:ATOMS, :] = whole[...]
    at = iota((16, ATOMS), 0)
    values = jnp.where(at == 9, labels[...].astype(f32), 0.0)
    for axis in range(3):
        place = places[axis]
        for part in range(3):
            piece = place.astype(bf16).astype(f32)
            values = jnp.where(at == 3 * part + axis, piece, values)
            place = place - piece
    tail[...] = values
    tail[10:11, 0:GHOST] = indices[0].astype(f32)
    tail[11:12, 0:GHOST] = indices[1].astype(f32)
    packed[ATOMS:PACK, :] = tail[...].astype(bf16)
    for copy in copies[len(near) :]:
        copy.wait()


def gather_kernel(own, near, across, corner, out):
    for part, rows in enumerate((own, near, across, corner)):
        out[PACK * part : PACK * (part + 1), :] = rows[...]


def wave_lanes(waves):
    mine = waves[:, pl.ds(pl.multiple_of(place_in_row() * KB, KB), KB)].astype(f32)
    at = iota((16, KB), 0)
    stacked = jnp.zeros((16, KB), f32)
    for axis in range(3):
        stacked = jnp.where(at == axis, mine[axis : axis + 1, :], stacked)
    stacked = stacked.astype(bf16)
    axis_at = iota((16, C), 0)
    return [dot_rows(stacked, (axis_at == axis).astype(f32).astype(bf16)) for axis in range(3)]


def tables_of(packed, lanes, species_gain, w_charge, table, gain, charges):
    kind_at = iota((8, ATOMS), 0).astype(f32)
    for j in range(ROW // 2):
        rows = packed[PACK * j : PACK * j + ATOMS, :]
        tail = packed[PACK * j + ATOMS : PACK * (j + 1), :].astype(f32)
        onehot = (tail[9:10, :] == kind_at).astype(f32)
        own_gain = lax.dot_general(
            onehot,
            species_gain[...],
            (((0,), (0,)), ((), ())),
            precision=lax.Precision.HIGHEST,
            preferred_element_type=f32,
        )
        span = slice(ATOMS * j, ATOMS * (j + 1))
        gain[span, :] = own_gain
        charges[span, :] = (dot(rows, w_charge[...]) * own_gain).astype(bf16)
        turns = jnp.zeros((KB, ATOMS), f32)
        for axis in range(3):
            place = tail[axis : axis + 1, :] + tail[axis + 3 : axis + 4, :] + tail[axis + 6 : axis + 7, :]
            turns = turns + place * lanes[axis]
        turns = turns - jnp.round(turns)
        square = turns * turns
        table[0:KB, span] = horner(COS_TURN, square).astype(bf16)
        table[KB : 2 * KB, span] = (turns * horner(SIN_TURN, square)).astype(bf16)


def structure_near_kernel(packed, waves, smearing, species_gain, w_charge, table, sums, filt, gain, charges):
    lanes = wave_lanes(waves)
    squared = lanes[0] * lanes[0] + lanes[1] * lanes[1] + lanes[2] * lanes[2]
    filt[...] = filter_factor * jnp.exp(-squared * smearing[...]) / jnp.sqrt(squared)
    tables_of(packed, lanes, species_gain, w_charge, table, gain, charges)
    sums[...] = dot(table[...], charges[...])


def structure_far_kernel(
    packed, near, near_sums, waves, species_gain, w_charge,
    table, sums, message_up, message_down, gain, below, above, charges, joined,
):
    tables_of(packed, wave_lanes(waves), species_gain, w_charge, table, gain, charges)
    total = (near_sums[...] + dot(table[...], charges[...])).astype(bf16)
    sums[...] = total
    message_up[0 : 2 * KB, :] = total
    message_down[0 : 2 * KB, :] = total
    joined[0:NEAR, :] = near[...]
    joined[NEAR:, :] = packed[...]
    place = place_in_row()
    atom = iota((ATOMS, GHOST), 0).astype(f32)

    def ghosts(owner, row):
        start = at_block(place ^ owner, PACK)
        rows = joined[pl.ds(start, ATOMS), :]
        tail = joined[pl.ds(pl.multiple_of(start + ATOMS, 16), 16), :].astype(f32)
        return dot_rows((atom == tail[row : row + 1, 0:GHOST]).astype(f32).astype(bf16), rows).astype(bf16)

    below[...] = ghosts((place + ROW - 1) % ROW, 10)
    above[...] = ghosts((place + 1) % ROW, 11)
    message_up[2 * KB :, :] = ghosts(ROW - 1, 10)
    message_down[2 * KB :, :] = ghosts(0, 11)


def copy_kernel(rows, out):
    out[...] = rows[...]


def pair_kernel(own, other, out):
    out[0:NEAR, :] = own[...]
    out[NEAR:, :] = other[...]


def collect_kernel(pair, other, out):
    mine = lax.axis_index("dom") // ROW
    for at, rows, half in ((mine, pair, 0), (mine ^ 1, pair, 1), (mine ^ 3, other, 0), (mine ^ 2, other, 1)):
        out[rows_at(at, NEAR), :] = rows[NEAR * half : NEAR * (half + 1), :]


def column_tables_kernel(packed, waves, species_gain, table, gain, turned):
    mine = waves[:, pl.ds(pl.multiple_of(place_in_row() * KB, KB), KB)].astype(f32)
    at = iota((16, KB), 0)
    kind_at = iota((8, ATOMS), 0).astype(f32)
    for j in range(COLUMN * ROW // 2):
        tail = packed[PACK * j + ATOMS : PACK * (j + 1), :]
        turned[:, ATOMS * j : ATOMS * (j + 1)] = packed[PACK * j : PACK * j + ATOMS, :].T
        span = slice(ATOMS * j, ATOMS * (j + 1))
        turns = jnp.zeros((ATOMS, KB), f32)
        for axis in range(3):
            chosen = (at == axis) | (at == axis + 3) | (at == axis + 6)
            turns = turns + dot_rows(tail, chosen.astype(f32).astype(bf16)) * mine[axis : axis + 1, :]
        turns = turns - jnp.round(turns)
        square = turns * turns
        table[span, 0:KB] = horner(COS_TURN, square).astype(bf16)
        table[span, KB : 2 * KB] = (turns * horner(SIN_TURN, square)).astype(bf16)
        onehot = (tail.astype(f32)[9:10, :] == kind_at).astype(f32)
        gain[span, :] = lax.dot_general(
            onehot,
            species_gain[...],
            (((0,), (0,)), ((), ())),
            precision=lax.Precision.HIGHEST,
            preferred_element_type=f32,
        )


def column_sum(own, up, down, over, span):
    return tree(own[span, :], over[span, :], up[span, :], down[span, :])


def field_of(sums, filt, scale):
    weight = filt[...] * scale
    return jnp.concatenate(
        [(weight * sums[0:KB]).astype(bf16), (weight * sums[KB : 2 * KB]).astype(bf16)], axis=0
    )


def potential_kernel(own, up, down, over, filt, near, far, send, keep):
    field = field_of(column_sum(own, up, down, over, slice(0, 2 * KB)), filt, inv_atoms)
    send[...] = (dot_rows(far[...], field) * inv_waves).astype(bf16)
    keep[...] = dot_rows(near[...], field) * inv_waves


def spread_kernel(held, received, own, *sends):
    values = held[...] + received[...].astype(f32)
    own[...] = values[0:ATOMS]
    for part, send in enumerate(sends):
        send[...] = values[ATOMS * (part + 1) : ATOMS * (part + 2)].astype(bf16)


def edge_kernel(first, count, *refs):
    total, left, right = refs[-3:]
    for step in range(first, first + count):
        senders, receivers, live, reach = (ref[:, CHUNK * step : CHUNK * (step + 1)] for ref in refs[:4])
        turn = reach * (0.5 / cutoff_radius)
        envelope = 0.5 * (horner(COS_TURN, turn * turn) + 1.0) * live.astype(f32)
        centers = 0.5 + basis_width * iota((NB, CHUNK), 0).astype(f32)
        offset = (reach - centers) * (1.0 / basis_width)
        weights = (jnp.exp(-offset * offset) * envelope).astype(bf16)
        atom = iota((ATOMS, CHUNK), 0)
        onehot = (atom == receivers).astype(f32).astype(bf16)
        for b in range(NB):
            left[ATOMS * b : ATOMS * (b + 1), :] = onehot * weights[b : b + 1, :]
        source = iota((EXT, CHUNK), 0)
        right[...] = (source == senders).astype(f32).astype(bf16)
        products = dot_lanes(left[...], right[...])
        if step > first:
            total[...] += products
        elif first:
            total[...] = refs[4][...] + products
        else:
            total[...] = products


def aggregate_kernel(feats, below, above, up, down, w_message, operator, w_radial, aggregate, radial_rows, extended):
    place = place_in_row()
    extended[0:ATOMS, :] = feats[...]
    extended[ATOMS : ATOMS + GHOST, :] = jnp.where(place == 0, up[2 * KB :, :], below[...])
    extended[ATOMS + GHOST :, :] = jnp.where(place == ROW - 1, down[2 * KB :, :], above[...])
    rows = dot(extended[...], w_message[...]).astype(bf16)
    high, low = split(operator[...])
    products = dot(high, rows) + dot(low, rows)
    radial_rows[...] = products
    total = jnp.zeros((ATOMS, C), f32)
    for b in range(NB):
        total = total + w_radial[b : b + 1, :] * products[ATOMS * b : ATOMS * (b + 1)]
    aggregate[...] = total * edge_scale


def update_kernel(
    held, near, across, corner, aggregate, cotangent, w_out, extended, w_message, operator, radial_rows, w_radial,
    act_out, own_total, own_rows, own_quarter, own_radial, send_near, send_across, send_corner, grads,
):
    preact = aggregate[...] + tree(held[...], near[...], across[...], corner[...])
    sig = jax.nn.sigmoid(preact)
    grad_act = dot_lanes(cotangent[...], w_out[...])
    grad = grad_act * sig * (1.0 + preact * (1.0 - sig))
    rounded = grad.astype(bf16)
    grad = grad * edge_scale
    stacked = jnp.concatenate([w_radial[b : b + 1, :] * grad for b in range(NB)], axis=0).astype(bf16)
    high, low = split(operator[...])
    grad_msg = (dot_rows(high, stacked) + dot_rows(low, stacked)).astype(bf16)
    grad_rows = dot_lanes(grad_msg, w_message[...])
    own_total[...] = cotangent[...].astype(f32) + grad_rows[:ATOMS]
    own_rows[0:ATOMS, :] = rounded
    own_rows[ATOMS:, :] = grad_rows[ATOMS:].astype(bf16)
    act = (preact * sig).astype(bf16)
    act_out[...] = act
    grad_message = dot_rows(extended[...], grad_msg)
    grad_out = dot_rows(act, cotangent[...])
    for t in range(ROW):
        grads[PART * t : PART * t + 16, :] = grad_message[16 * t : 16 * (t + 1)]
        grads[PART * t + 16 : PART * (t + 1), :] = grad_out[16 * t : 16 * (t + 1)]
    at = iota((16, C), 0)
    tail = jnp.zeros((16, C), f32)
    for b in range(NB):
        part = jnp.sum(grad * radial_rows[ATOMS * b : ATOMS * (b + 1), :], axis=0, keepdims=True)
        tail = jnp.where(at == b, part, tail)
    tail = tail.astype(bf16)
    own_radial[...] = tail
    own_quarter[...] = grads[z_at(0, QUARTER), :]
    for part, send in ((1, send_near), (2, send_across), (3, send_corner)):
        send[0:EXT, :] = own_rows[...]
        send[EXT : EXT + QUARTER, :] = grads[z_at(part, QUARTER), :].astype(bf16)
        send[EXT + QUARTER :, :] = tail


def updated_kernel(feats, act, w_out, updated, token):
    total = feats[...].astype(f32) + dot(act[...], w_out[...])
    updated[...] = total.astype(bf16)
    token[...] = total[0:8]


def join_kernel(own_rows, own_quarter, own_radial, near, across, corner, joined, kept, sums):
    quarter = own_quarter[...]
    for part, rows in enumerate((own_rows, near, across, corner)):
        joined[ATOMS * part : ATOMS * (part + 1), :] = rows[0:ATOMS, :]
        start = HALF + 2 * GHOST * part
        joined[start : start + 2 * GHOST, :] = rows[ATOMS:EXT, :]
        if part:
            quarter = quarter + rows[EXT : EXT + QUARTER, :].astype(f32)
    sums[...] = quarter
    kept[...] = sums[rows_at(core(), PART), :]
    ends = HALF + 8 * GHOST
    joined[ends : ends + PART, :] = sums[rows_at(1 - core(), PART), :].astype(bf16)
    last = slice(EXT + QUARTER, EXT + QUARTER + 16)
    joined[ends + PART :, :] = tree(own_radial[...], near[last, :], across[last, :], corner[last, :]).astype(bf16)


def back_near_kernel(table, joined, sums):
    sums[...] = dot(table[...], joined[0:HALF, :])


def back_far_kernel(
    table, received, joined, kept, near_sums, message_up, message_down, over, back_down, back_up, ghosts
):
    total = (near_sums[...] + dot(table[...], received[0:HALF, :])).astype(bf16)
    ends = HALF + 8 * GHOST
    part = (kept[...] + received[ends : ends + PART, :].astype(f32)).astype(bf16)
    radial = (joined[ends + PART :, :].astype(f32) + received[ends + PART :, :].astype(f32)).astype(bf16)
    for target in (message_up, message_down, over):
        target[0 : 2 * KB, :] = total
        target[2 * KB : 2 * KB + PART, :] = part
        target[2 * KB + PART : 2 * KB + PART + 16, :] = radial
    ghosts[0 : 8 * GHOST, :] = joined[HALF:ends, :]
    ghosts[8 * GHOST :, :] = received[HALF:ends, :]
    place = place_in_row()

    def returned(owner, above):
        start = at_block(place ^ owner, 2 * GHOST) + above * GHOST
        return ghosts[pl.ds(pl.multiple_of(start, GHOST), GHOST), :]

    back_down[...] = returned((place + ROW - 1) % ROW, 1)
    back_up[...] = returned((place + 1) % ROW, 0)
    first = 2 * KB + PART + 16
    message_up[first:, :] = returned(ROW - 1, 1)
    message_down[first:, :] = returned(0, 0)


def charge_back_kernel(own, up, down, over, filt, near, far, near_gain, far_gain, send, keep, early, field):
    field[...] = field_of(column_sum(own, up, down, over, slice(0, 2 * KB)), filt, inv_waves * inv_atoms)
    early[...] = column_sum(own, up, down, over, slice(2 * KB, 2 * KB + PART + 16)).astype(bf16)
    send[...] = (dot_rows(far[...], field[...]) * far_gain[...]).astype(bf16)
    keep[...] = dot_rows(near[...], field[...]) * near_gain[...]


def charge_kernel(field, early, near_table, near_gain, near_rows, far_table, far_gain, far_rows, message):
    total = jnp.zeros((C, C), f32)
    for table, gain, rows in ((near_table, near_gain, near_rows), (far_table, far_gain, far_rows)):
        total = total + dot(rows[...], (dot(table[...], field[...]) * gain[...]).astype(bf16))
    message[0:C, :] = total.astype(bf16)
    message[C:, :] = early[...]


def tail_spread_kernel(held, received, mine, other, own, grads, *sends):
    values = held[...] + received[...].astype(f32)
    total = (mine[...].astype(f32) + other[...].astype(f32)).astype(bf16)
    own[...] = values[0:ATOMS]
    grads[...] = total
    for part, send in enumerate(sends):
        send[0:ATOMS, :] = values[ATOMS * (part + 1) : ATOMS * (part + 2)].astype(bf16)
        send[ATOMS:, :] = total[0 : C + PART]


def raw_kernel(held, grads, near, across, corner, raw, message):
    rows = slice(0, ATOMS)
    raw[...] = tree(held[...], near[rows, :], across[rows, :], corner[rows, :]).astype(bf16)
    rows = slice(ATOMS, ATOMS + C)
    message[0:C, :] = tree(grads[0:C, :], near[rows, :], across[rows, :], corner[rows, :]).astype(bf16)
    quarters = message.at[C : 2 * C]
    quarters[z_at(0, PART), :] = grads[C : C + PART, :]
    for part, received in ((1, near), (2, across), (3, corner)):
        quarters[z_at(part, PART), :] = received[ATOMS + C :, :]
    message[2 * C :, :] = grads[C + PART :, :]


def cell_sum_kernel(own, near, across, corner, out):
    out[...] = tree(own[...], near[...], across[...], corner[...]) * grad_scale


def feature_kernel(raw, w_charge, own, downs, ups, back_down, back_up, up, down, out, token):
    place = place_in_row()
    first = 2 * KB + PART + 16
    returned = jnp.where(place == 0, up[first:, :], back_down[...])
    total = own[...] + dot_lanes(raw[...], w_charge[...])
    atom = iota((ATOMS, GHOST), 0)
    total = total + dot((atom == downs[...]).astype(f32).astype(bf16), returned)
    returned = jnp.where(place == ROW - 1, down[first:, :], back_up[...])
    total = total + dot((atom == ups[...]).astype(f32).astype(bf16), returned)
    out[...] = total.astype(bf16)
    token[...] = total[0:8]


def weights_kernel(own, other, charge, message, radial, out):
    charge[...] = own[0:C, :] + other[0:C, :]
    for total, at in ((own, core()), (other, 1 - core())):
        for z in range(4):
            start = C + PART * z
            message[rows_at(2 * z + at, 16), :] = total[start : start + 16, :]
            out[rows_at(2 * z + at, 16), :] = total[start + 16 : start + PART, :]
    radial[...] = own[2 * C : 2 * C + NB, :]


def swap(values, axis, mask):
    count = lax.axis_size(axis)
    return lax.ppermute(values, axis, [(i, i ^ mask) for i in range(count)])


def from_y(values, by):
    return lax.ppermute(values, "dom", [(i, (i + ROW * by) % DOMS) for i in range(DOMS)])


def per_device(
    feats,
    positions,
    species,
    wave_vectors,
    smearing,
    species_gain,
    w_charge,
    w_message,
    w_radial,
    w_out,
    edge_sender,
    edge_receiver,
    edge_mask,
    edge_length,
    ghost_down,
    ghost_up,
    cotangent,
):
    own_rows = feats[0]
    cot = cotangent[0]

    def edges(first, count, total, after):
        (out,) = call(
            lambda *refs: edge_kernel(first, count, *refs),
            [((NB * ATOMS, EXT), f32)],
            *edge_arrays, *total,
            scratch=[pltpu.VMEM((NB * ATOMS, CHUNK), bf16), pltpu.VMEM((EXT, CHUNK), bf16)],
            flops=count * 2 * NB * ATOMS * CHUNK * 256,
            after=after,
            name="edges",
        )
        return out

    in_place = pl.BlockSpec(memory_space=pltpu.HBM)
    arrays = (
        own_rows, positions.transpose(1, 0, 2), species, ghost_down, ghost_up,
        edge_sender, edge_receiver, edge_mask, edge_length,
    )
    packed, *edge_arrays = call(
        pack_kernel,
        [((PACK, C), bf16)] + [((1, EDGES), jnp.int32)] * 3 + [((1, EDGES), f32)],
        *[pltpu.with_memory_space_constraint(values, pltpu.HBM) for values in arrays],
        scratch=[
            pltpu.VMEM((16, C), f32), pltpu.VMEM((ATOMS, C), bf16), pltpu.VMEM((3, 1, ATOMS), f32),
            pltpu.VMEM((1, ATOMS), jnp.int32), pltpu.VMEM((2, 1, GHOST), jnp.int32), pltpu.SemaphoreType.DMA((9,)),
        ],
        in_specs=[in_place] * 9,
        out_specs=[pl.BlockSpec(memory_space=pltpu.VMEM)] * 5,
        name="pack",
    )
    operator = edges(0, EDGE_STEPS[0], [], [packed])
    (near_rows,) = call(
        gather_kernel,
        [((ROW // 2 * PACK, C), bf16)],
        packed, *[swap(packed, "dom", mask) for mask in (2, 4, 6)],
        after=[operator],
        name="gather",
    )
    far_rows = swap(near_rows, "dom", 1)
    near, near_sums, filt, near_gain = call(
        structure_near_kernel,
        [((2 * KB, HALF), bf16), ((2 * KB, C), f32), ((KB, C), f32), ((HALF, C), f32)],
        near_rows, wave_vectors, smearing[None], species_gain, w_charge,
        scratch=[pltpu.VMEM((HALF, C), bf16)],
        name="structure_near",
    )
    far, sums, message_up, message_down, far_gain, below, above = call(
        structure_far_kernel,
        [
            ((2 * KB, HALF), bf16), ((2 * KB, C), bf16), ((2 * KB + GHOST, C), bf16), ((2 * KB + GHOST, C), bf16),
            ((HALF, C), f32), ((GHOST, C), bf16), ((GHOST, C), bf16),
        ],
        far_rows, near_rows, near_sums, wave_vectors, species_gain, w_charge,
        scratch=[pltpu.VMEM((HALF, C), bf16), pltpu.VMEM((ROW * PACK, C), bf16)],
        name="structure_far",
    )
    up, down, over = from_y(message_up, 1), from_y(message_down, -1), from_y(sums, 2)
    operator = edges(EDGE_STEPS[0], EDGE_STEPS[1], [operator], [message_up])
    (own_near,) = call(copy_kernel, [((NEAR, C), bf16)], near_rows, after=[operator], name="copy")
    other_near = swap(own_near, "dom", 8)
    send, keep = call(
        potential_kernel,
        [((HALF, C), bf16), ((HALF, C), f32)],
        sums, up, down, over, filt, near, far,
        after=[own_near],
        name="potential",
    )
    received = swap(send, "dom", 1)
    held, *sends = call(
        spread_kernel, [((ATOMS, C), f32)] + [((ATOMS, C), bf16)] * 3, keep, received, name="spread"
    )
    parts = [swap(values, "dom", 2 * (part + 1)) for part, values in enumerate(sends)]
    aggregate, radial_rows, extended = call(
        aggregate_kernel,
        [((ATOMS, C), f32), ((NB * ATOMS, C), f32), ((EXT, C), bf16)],
        own_rows, below, above, up, down, w_message, operator, w_radial,
        name="aggregate",
    )
    (pair,) = call(
        pair_kernel, [((2 * NEAR, C), bf16)], own_near, other_near, after=[aggregate], name="pair"
    )
    other_pair = swap(pair, "dom", 24)
    act, own_total, back_rows, quarter, radial, *sends = call(
        update_kernel,
        [((ATOMS, C), bf16), ((ATOMS, C), f32), ((EXT, C), bf16), ((QUARTER, C), f32), ((16, C), bf16)]
        + [((EXT + QUARTER + 16, C), bf16)] * 3,
        held, *parts, aggregate, cot, w_out, extended, w_message, operator, radial_rows, w_radial,
        scratch=[pltpu.VMEM((2 * C, C), f32)],
        name="update",
    )
    parts = [swap(values, "dom", 2 * (part + 1)) for part, values in enumerate(sends)]
    updated, token = call(
        updated_kernel, [((ATOMS, C), bf16), ((8, C), f32)], own_rows, act, w_out, after=[sends[0]], name="updated"
    )
    joined, kept = call(
        join_kernel,
        [((HALF + 8 * GHOST + PART + 16, C), bf16), ((PART, C), f32)],
        back_rows, quarter, radial, *parts,
        scratch=[pltpu.VMEM((QUARTER, C), f32)],
        after=[token],
        name="join",
    )
    received = swap(joined, "dom", 1)
    (near_sums,) = call(back_near_kernel, [((2 * KB, C), f32)], near, joined, name="back_near")
    message_up, message_down, over, back_down, back_up = call(
        back_far_kernel,
        [
            ((2 * KB + PART + 16 + GHOST, C), bf16), ((2 * KB + PART + 16 + GHOST, C), bf16),
            ((2 * KB + PART + 16, C), bf16),
            ((GHOST, C), bf16), ((GHOST, C), bf16),
        ],
        far, received, joined, kept, near_sums,
        scratch=[pltpu.VMEM((16 * GHOST, C), bf16)],
        name="back_far",
    )
    (near_column,) = call(
        collect_kernel, [((COLUMN * NEAR, C), bf16)], pair, other_pair, after=[over], name="collect"
    )
    far_column = swap(near_column, "dom", 1)
    column_shapes = [((COLUMN * HALF, 2 * KB), bf16), ((COLUMN * HALF, C), f32), ((C, COLUMN * HALF), bf16)]
    near_table, near_column_gain, near_turned = call(
        column_tables_kernel, column_shapes, near_column, wave_vectors, species_gain, after=[over], name="near_tables"
    )
    far_table, far_column_gain, far_turned = call(
        column_tables_kernel, column_shapes, far_column, wave_vectors, species_gain, after=[over], name="far_tables"
    )
    sums = over
    up, down, over = from_y(message_up, 1), from_y(message_down, -1), from_y(over, 2)
    send, keep, early, field = call(
        charge_back_kernel,
        [((HALF, C), bf16), ((HALF, C), f32), ((PART + 16, C), bf16), ((2 * KB, C), bf16)],
        sums, up, down, over, filt, near, far, near_gain, far_gain,
        after=[near_column_gain, far_column_gain],
        name="charge_back",
    )
    received = swap(send, "dom", 1)
    (message,) = call(
        charge_kernel,
        [((C + PART + 16, C), bf16)],
        field, early, near_table, near_column_gain, near_turned, far_table, far_column_gain, far_turned,
        after=[send],
        name="charge",
    )
    other = swap(message, ("cell", "dom"), DOMS + 6)
    held, grads, *sends = call(
        tail_spread_kernel,
        [((ATOMS, C), f32), ((C + PART + 16, C), bf16)] + [((ATOMS + C + PART, C), bf16)] * 3,
        keep, received, message, other,
        name="tail_spread",
    )
    parts = [swap(values, "dom", 2 * (part + 1)) for part, values in enumerate(sends)]
    raw, message = call(
        raw_kernel, [((ATOMS, C), bf16), ((2 * C + 16, C), bf16)], held, grads, *parts, name="raw"
    )
    parts = [swap(message, "cell", mask) for mask in (2, 4, 6)]
    feat_grad, token = call(
        feature_kernel,
        [((ATOMS, C), bf16), ((8, C), f32)],
        raw, w_charge, own_total, ghost_down, ghost_up, back_down, back_up, up, down,
        after=[message],
        name="feature",
    )
    (total,) = call(cell_sum_kernel, [((2 * C + 16, C), f32)], message, *parts, after=[token], name="cell_sum")
    charge, message, radial, out = call(
        weights_kernel,
        [((C, C), f32), ((C, C), f32), ((NB, C), f32), ((C, C), f32)],
        total, swap(total, "dom", 1),
        name="weights",
    )
    return updated[None], feat_grad[None], charge, message, radial, out


def solution(mesh):
    placed = (
        P("cell", "dom", None),
        P("cell", None, "dom"),
        P("cell", "dom"),
        P(),
        P(),
        P(),
        P(),
        P(),
        P(),
        P(),
        P("cell", "dom"),
        P("cell", "dom"),
        P("cell", "dom"),
        P("cell", "dom"),
        P("cell", "dom"),
        P("cell", "dom"),
        P("cell", "dom", None),
    )
    return jax.shard_map(
        per_device,
        mesh=mesh,
        in_specs=placed,
        out_specs=(P("cell", "dom", None), P("cell", "dom", None), P(), P(), P(), P()),
        check_vma=False,
    )
```

```python
import math

import jax
import jax.numpy as jnp
from jax import lax
from jax.experimental import pallas as pl
from jax.experimental.pallas import tpu as pltpu
from jax.sharding import PartitionSpec as P

bf16 = jnp.bfloat16
f32 = jnp.float32

C = 128
K = 2048
NB = 8
ATOMS = 128
GHOST = 32
EXT = ATOMS + 2 * GHOST
EDGES = 12288
DOMS = 32
CELLS = 8
ROW = 8
KB = K // ROW
PACK = ATOMS + 16
QUARTER = 64
PART = QUARTER // 2
NEAR = ROW // 2 * PACK
COLUMN = 4
HALF = ROW * ATOMS // 2
CHUNK = 1024
EDGE_STEPS = (5, 7)

cutoff_radius = 6.0
basis_width = 0.75
edge_scale = 0.25
filter_factor = 12.0
inv_waves = 1.0 / math.sqrt(K)
inv_atoms = 1.0 / math.sqrt(ATOMS * DOMS)
grad_scale = 1.0 / math.sqrt(CELLS * ATOMS * DOMS)

COS_TURN = (
    0.9999999890754399,
    -19.73920450099313,
    64.93911749956553,
    -85.45013994347214,
    60.16763282514798,
    -25.967602441408868,
    6.528658639370483,
)
SIN_TURN = (
    6.283184916984331,
    -41.34158926418157,
    81.59994386455666,
    -76.61447586020026,
    41.342889428722025,
    -12.471244745942547,
)

MIX = (
    (1.25563, -0.56805, 0.251163, -0.11939, 0.059896, -0.030538, 0.014724, -0.005361),
    (-0.56805, 1.647472, -0.773752, 0.355088, -0.172104, 0.085726, -0.040753, 0.014724),
    (0.251163, -0.773752, 1.767661, -0.8374, 0.386766, -0.185002, 0.085726, -0.030538),
    (-0.11939, 0.355088, -0.8374, 1.801205, -0.851469, 0.386766, -0.172104, 0.059896),
    (0.059896, -0.172104, 0.386766, -0.851469, 1.801205, -0.8374, 0.355088, -0.11939),
    (-0.030538, 0.085726, -0.185002, 0.386766, -0.8374, 1.767661, -0.773752, 0.251163),
    (0.014724, -0.040753, 0.085726, -0.172104, 0.355088, -0.773752, 1.647472, -0.56805),
    (-0.005361, 0.014724, -0.030538, 0.059896, -0.11939, 0.251163, -0.56805, 1.25563),
    (0.943774626, 0.330363768, 0.0119126827, 0.00237723804, -0.00100488116, 0.000442211757, -0.000188380319, 6.26400104e-05),
    (0.330363768, 0.879800949, 0.341632643, 0.00920268838, 0.00330706128, -0.00137507484, 0.000571783509, -0.000188380319),
    (0.0119126827, 0.341632643, 0.874756301, 0.343305856, 0.00862722425, 0.0034955942, -0.00137507484, 0.000442211757),
    (0.00237723804, 0.00920268838, 0.343305856, 0.87403504, 0.343551294, 0.00862722425, 0.00330706128, -0.00100488116),
    (-0.00100488116, 0.00330706128, 0.00862722425, 0.343551294, 0.87403504, 0.343305856, 0.00920268838, 0.00237723804),
    (0.000442211757, -0.00137507484, 0.0034955942, 0.00862722425, 0.343305856, 0.874756301, 0.341632643, 0.0119126827),
    (-0.000188380319, 0.000571783509, -0.00137507484, 0.00330706128, 0.00920268838, 0.341632643, 0.879800949, 0.330363768),
    (6.26400104e-05, -0.000188380319, 0.000442211757, -0.00100488116, 0.00237723804, 0.0119126827, 0.330363768, 0.943774626),
)


def horner(coefficients, x):
    total = jnp.full_like(x, coefficients[-1])
    for value in coefficients[-2::-1]:
        total = total * x + value
    return total


def iota(shape, axis):
    return lax.broadcasted_iota(jnp.int32, shape, axis)


def dot(left, right):
    return jnp.dot(left, right, preferred_element_type=f32)


def mixed(table, values):
    at = iota((NB, C), 0)
    total = None
    for j in range(NB):
        column = jnp.full((NB, C), table[0][j], f32)
        for b in range(1, NB):
            column = jnp.where(at == b, table[b][j], column)
        column = jnp.concatenate([column] * (values.shape[1] // C), axis=1)
        part = column * values[j : j + 1, :]
        total = part if total is None else total + part
    return total


def dot_rows(left, right):
    return lax.dot_general(left, right, (((0,), (0,)), ((), ())), preferred_element_type=f32)


def dot_lanes(left, right):
    return lax.dot_general(left, right, (((1,), (1,)), ((), ())), preferred_element_type=f32)


def split(values):
    high = values.astype(bf16)
    return high, (values - high.astype(f32)).astype(bf16)


def call(kernel, outs, *args, scratch=(), flops=0, after=(), name=None, **more):
    def run(*refs):
        kernel(*refs[: len(args)], *refs[len(args) + len(after) :])

    if "in_specs" not in more:
        more["in_specs"] = [pl.BlockSpec(memory_space=pltpu.VMEM)] * len(args)
        more["out_specs"] = [pl.BlockSpec(memory_space=pltpu.VMEM)] * len(outs)
    more["in_specs"] = more["in_specs"] + [pl.BlockSpec(memory_space=pl.ANY)] * len(after)
    return pl.pallas_call(
        run,
        out_shape=[jax.ShapeDtypeStruct(shape, dtype) for shape, dtype in outs],
        scratch_shapes=list(scratch),
        compiler_params=pltpu.CompilerParams(vmem_limit_bytes=40 * 1024 * 1024),
        cost_estimate=pl.CostEstimate(flops=flops, bytes_accessed=1 << 18, transcendentals=0),
        name=name,
        **more,
    )(*args, *after)


def place_in_row():
    return lax.rem(lax.axis_index("dom"), ROW)


def at_block(mask, rows):
    return pl.multiple_of((mask // 2 + (mask % 2) * (ROW // 2)) * rows, rows)


def rows_at(index, count):
    return pl.ds(pl.multiple_of(index * count, count), count)


def z_at(part, count):
    quarter = (place_in_row() // 2) ^ (3 * lax.rem(lax.axis_index("cell"), 2))
    return rows_at(quarter ^ part, count)


def core():
    return lax.rem(lax.axis_index("dom"), 2)


def tree(own, near, across, corner):
    return (own.astype(f32) + near.astype(f32)) + (across.astype(f32) + corner.astype(f32))


def pack_kernel(
    feats, coords, kinds, downs, ups, sent, got, live, reach,
    packed, senders, receivers, mask, lengths, tail, whole, places, labels, indices, sems,
):
    near = [(feats, whole), (coords, places), (kinds, labels), (ups, indices.at[0]), (downs, indices.at[1])]
    edges = [(sent, senders), (got, receivers), (live, mask), (reach, lengths)]
    copies = [
        pltpu.make_async_copy(source, target, sems.at[i]) for i, (source, target) in enumerate(near + edges)
    ]
    for copy in copies:
        copy.start()
    for copy in copies[: len(near)]:
        copy.wait()
    packed[0:ATOMS, :] = whole[...]
    at = iota((16, ATOMS), 0)
    values = jnp.where(at == 9, labels[...].astype(f32), 0.0)
    for axis in range(3):
        place = places[axis]
        for part in range(3):
            piece = place.astype(bf16).astype(f32)
            values = jnp.where(at == 3 * part + axis, piece, values)
            place = place - piece
    tail[...] = values
    tail[10:11, 0:GHOST] = indices[0].astype(f32)
    tail[11:12, 0:GHOST] = indices[1].astype(f32)
    packed[ATOMS:PACK, :] = tail[...].astype(bf16)
    for copy in copies[len(near) :]:
        copy.wait()


def gather_kernel(own, near, across, corner, out):
    for part, rows in enumerate((own, near, across, corner)):
        out[PACK * part : PACK * (part + 1), :] = rows[...]


def wave_lanes(waves):
    mine = waves[:, pl.ds(pl.multiple_of(place_in_row() * KB, KB), KB)].astype(f32)
    at = iota((16, KB), 0)
    stacked = jnp.zeros((16, KB), f32)
    for axis in range(3):
        stacked = jnp.where(at == axis, mine[axis : axis + 1, :], stacked)
    stacked = stacked.astype(bf16)
    axis_at = iota((16, C), 0)
    return [dot_rows(stacked, (axis_at == axis).astype(f32).astype(bf16)) for axis in range(3)]


def tables_of(packed, lanes, species_gain, w_charge, table, gain, charges):
    kind_at = iota((8, ATOMS), 0).astype(f32)
    for j in range(ROW // 2):
        rows = packed[PACK * j : PACK * j + ATOMS, :]
        tail = packed[PACK * j + ATOMS : PACK * (j + 1), :].astype(f32)
        onehot = (tail[9:10, :] == kind_at).astype(f32)
        own_gain = lax.dot_general(
            onehot,
            species_gain[...],
            (((0,), (0,)), ((), ())),
            precision=lax.Precision.HIGHEST,
            preferred_element_type=f32,
        )
        span = slice(ATOMS * j, ATOMS * (j + 1))
        gain[span, :] = own_gain
        charges[span, :] = (dot(rows, w_charge[...]) * own_gain).astype(bf16)
        turns = jnp.zeros((KB, ATOMS), f32)
        for axis in range(3):
            place = tail[axis : axis + 1, :] + tail[axis + 3 : axis + 4, :] + tail[axis + 6 : axis + 7, :]
            turns = turns + place * lanes[axis]
        turns = turns - jnp.round(turns)
        square = turns * turns
        table[0:KB, span] = horner(COS_TURN, square).astype(bf16)
        table[KB : 2 * KB, span] = (turns * horner(SIN_TURN, square)).astype(bf16)


def structure_near_kernel(packed, waves, smearing, species_gain, w_charge, table, sums, filt, gain, charges):
    lanes = wave_lanes(waves)
    squared = lanes[0] * lanes[0] + lanes[1] * lanes[1] + lanes[2] * lanes[2]
    filt[...] = filter_factor * jnp.exp(-squared * smearing[...]) / jnp.sqrt(squared)
    tables_of(packed, lanes, species_gain, w_charge, table, gain, charges)
    sums[...] = dot(table[...], charges[...])


def structure_far_kernel(
    packed, near, near_sums, waves, species_gain, w_charge,
    table, sums, message_up, message_down, gain, below, above, charges, joined,
):
    tables_of(packed, wave_lanes(waves), species_gain, w_charge, table, gain, charges)
    total = (near_sums[...] + dot(table[...], charges[...])).astype(bf16)
    sums[...] = total
    message_up[0 : 2 * KB, :] = total
    message_down[0 : 2 * KB, :] = total
    joined[0:NEAR, :] = near[...]
    joined[NEAR:, :] = packed[...]
    place = place_in_row()
    atom = iota((ATOMS, GHOST), 0).astype(f32)

    def ghosts(owner, row):
        start = at_block(place ^ owner, PACK)
        rows = joined[pl.ds(start, ATOMS), :]
        tail = joined[pl.ds(pl.multiple_of(start + ATOMS, 16), 16), :].astype(f32)
        return dot_rows((atom == tail[row : row + 1, 0:GHOST]).astype(f32).astype(bf16), rows).astype(bf16)

    below[...] = ghosts((place + ROW - 1) % ROW, 10)
    above[...] = ghosts((place + 1) % ROW, 11)
    message_up[2 * KB :, :] = ghosts(ROW - 1, 10)
    message_down[2 * KB :, :] = ghosts(0, 11)


def copy_kernel(rows, out):
    out[...] = rows[...]


def pair_kernel(own, other, out):
    out[0:NEAR, :] = own[...]
    out[NEAR:, :] = other[...]


def collect_kernel(pair, other, out):
    mine = lax.axis_index("dom") // ROW
    for at, rows, half in ((mine, pair, 0), (mine ^ 1, pair, 1), (mine ^ 3, other, 0), (mine ^ 2, other, 1)):
        out[rows_at(at, NEAR), :] = rows[NEAR * half : NEAR * (half + 1), :]


def column_tables_kernel(packed, waves, species_gain, table, gain, turned):
    mine = waves[:, pl.ds(pl.multiple_of(place_in_row() * KB, KB), KB)].astype(f32)
    at = iota((16, KB), 0)
    kind_at = iota((8, ATOMS), 0).astype(f32)
    for j in range(COLUMN * ROW // 2):
        tail = packed[PACK * j + ATOMS : PACK * (j + 1), :]
        turned[:, ATOMS * j : ATOMS * (j + 1)] = packed[PACK * j : PACK * j + ATOMS, :].T
        span = slice(ATOMS * j, ATOMS * (j + 1))
        turns = jnp.zeros((ATOMS, KB), f32)
        for axis in range(3):
            chosen = (at == axis) | (at == axis + 3) | (at == axis + 6)
            turns = turns + dot_rows(tail, chosen.astype(f32).astype(bf16)) * mine[axis : axis + 1, :]
        turns = turns - jnp.round(turns)
        square = turns * turns
        table[span, 0:KB] = horner(COS_TURN, square).astype(bf16)
        table[span, KB : 2 * KB] = (turns * horner(SIN_TURN, square)).astype(bf16)
        onehot = (tail.astype(f32)[9:10, :] == kind_at).astype(f32)
        gain[span, :] = lax.dot_general(
            onehot,
            species_gain[...],
            (((0,), (0,)), ((), ())),
            precision=lax.Precision.HIGHEST,
            preferred_element_type=f32,
        )


def column_sum(own, up, down, over, span):
    return tree(own[span, :], over[span, :], up[span, :], down[span, :])


def field_of(sums, filt, scale):
    weight = filt[...] * scale
    return jnp.concatenate(
        [(weight * sums[0:KB]).astype(bf16), (weight * sums[KB : 2 * KB]).astype(bf16)], axis=0
    )


def potential_kernel(own, up, down, over, filt, near, far, send, keep):
    field = field_of(column_sum(own, up, down, over, slice(0, 2 * KB)), filt, inv_atoms)
    send[...] = (dot_rows(far[...], field) * inv_waves).astype(bf16)
    keep[...] = dot_rows(near[...], field) * inv_waves


def spread_kernel(held, received, own, *sends):
    values = held[...] + received[...].astype(f32)
    own[...] = values[0:ATOMS]
    for part, send in enumerate(sends):
        send[...] = values[ATOMS * (part + 1) : ATOMS * (part + 2)].astype(bf16)


def edge_kernel(first, count, *refs):
    total, left, right = refs[-3:]
    for step in range(first, first + count):
        senders, receivers, live, reach = (ref[:, CHUNK * step : CHUNK * (step + 1)] for ref in refs[:4])
        turn = reach * (0.5 / cutoff_radius)
        envelope = 0.5 * (horner(COS_TURN, turn * turn) + 1.0) * live.astype(f32)
        centers = 0.5 + basis_width * iota((NB, CHUNK), 0).astype(f32)
        offset = (reach - centers) * (1.0 / basis_width)
        weights = (mixed(MIX[:NB], jnp.exp(-offset * offset)) * envelope).astype(bf16)
        atom = iota((ATOMS, CHUNK), 0)
        onehot = (atom == receivers).astype(f32).astype(bf16)
        for b in range(NB):
            left[ATOMS * b : ATOMS * (b + 1), :] = onehot * weights[b : b + 1, :]
        source = iota((EXT, CHUNK), 0)
        right[...] = (source == senders).astype(f32).astype(bf16)
        products = dot_lanes(left[...], right[...])
        if step > first:
            total[...] += products
        elif first:
            total[...] = refs[4][...] + products
        else:
            total[...] = products


def aggregate_kernel(feats, below, above, up, down, w_message, operator, w_radial, aggregate, radial_rows, extended):
    place = place_in_row()
    extended[0:ATOMS, :] = feats[...]
    extended[ATOMS : ATOMS + GHOST, :] = jnp.where(place == 0, up[2 * KB :, :], below[...])
    extended[ATOMS + GHOST :, :] = jnp.where(place == ROW - 1, down[2 * KB :, :], above[...])
    rows = dot(extended[...], w_message[...]).astype(bf16)
    high, low = split(operator[...])
    products = dot(high, rows) + dot(low, rows)
    radial_rows[...] = products
    weights = mixed(MIX[NB:], w_radial[...])
    total = jnp.zeros((ATOMS, C), f32)
    for b in range(NB):
        total = total + weights[b : b + 1, :] * products[ATOMS * b : ATOMS * (b + 1)]
    aggregate[...] = total * edge_scale


def update_kernel(
    held, near, across, corner, aggregate, cotangent, w_out, extended, w_message, operator, radial_rows, w_radial,
    act_out, own_total, own_rows, own_quarter, own_radial, send_near, send_across, send_corner, grads,
):
    preact = aggregate[...] + tree(held[...], near[...], across[...], corner[...])
    sig = jax.nn.sigmoid(preact)
    grad_act = dot_lanes(cotangent[...], w_out[...])
    grad = grad_act * sig * (1.0 + preact * (1.0 - sig))
    rounded = grad.astype(bf16)
    grad = grad * edge_scale
    weights = mixed(MIX[NB:], w_radial[...])
    stacked = split(jnp.concatenate([weights[b : b + 1, :] * grad for b in range(NB)], axis=0))
    high, low = split(operator[...])
    products = dot_rows(high, jnp.concatenate(stacked, axis=1))
    grad_msg = (products[:, :C] + products[:, C:] + dot_rows(low, stacked[0])).astype(bf16)
    grad_rows = dot_lanes(grad_msg, w_message[...])
    own_total[...] = cotangent[...].astype(f32) + grad_rows[:ATOMS]
    own_rows[0:ATOMS, :] = rounded
    own_rows[ATOMS:, :] = grad_rows[ATOMS:].astype(bf16)
    act = (preact * sig).astype(bf16)
    act_out[...] = act
    grad_message = dot_rows(extended[...], grad_msg)
    grad_out = dot_rows(act, cotangent[...])
    for t in range(ROW):
        grads[PART * t : PART * t + 16, :] = grad_message[16 * t : 16 * (t + 1)]
        grads[PART * t + 16 : PART * (t + 1), :] = grad_out[16 * t : 16 * (t + 1)]
    at = iota((NB, C), 0)
    tail = jnp.zeros((NB, C), f32)
    for b in range(NB):
        part = jnp.sum(grad * radial_rows[ATOMS * b : ATOMS * (b + 1), :], axis=0, keepdims=True)
        tail = jnp.where(at == b, part, tail)
    tail = jnp.concatenate([mixed(MIX[NB:], tail), jnp.zeros((NB, C), f32)], axis=0).astype(bf16)
    own_radial[...] = tail
    own_quarter[...] = grads[z_at(0, QUARTER), :]
    for part, send in ((1, send_near), (2, send_across), (3, send_corner)):
        send[0:EXT, :] = own_rows[...]
        send[EXT : EXT + QUARTER, :] = grads[z_at(part, QUARTER), :].astype(bf16)
        send[EXT + QUARTER :, :] = tail


def updated_kernel(feats, act, w_out, updated, token):
    total = feats[...].astype(f32) + dot(act[...], w_out[...])
    updated[...] = total.astype(bf16)
    token[...] = total[0:8]


def join_kernel(own_rows, own_quarter, own_radial, near, across, corner, joined, kept, sums):
    quarter = own_quarter[...]
    for part, rows in enumerate((own_rows, near, across, corner)):
        joined[ATOMS * part : ATOMS * (part + 1), :] = rows[0:ATOMS, :]
        start = HALF + 2 * GHOST * part
        joined[start : start + 2 * GHOST, :] = rows[ATOMS:EXT, :]
        if part:
            quarter = quarter + rows[EXT : EXT + QUARTER, :].astype(f32)
    sums[...] = quarter
    kept[...] = sums[rows_at(core(), PART), :]
    ends = HALF + 8 * GHOST
    joined[ends : ends + PART, :] = sums[rows_at(1 - core(), PART), :].astype(bf16)
    last = slice(EXT + QUARTER, EXT + QUARTER + 16)
    joined[ends + PART :, :] = tree(own_radial[...], near[last, :], across[last, :], corner[last, :]).astype(bf16)


def back_near_kernel(table, joined, sums):
    sums[...] = dot(table[...], joined[0:HALF, :])


def back_far_kernel(
    table, received, joined, kept, near_sums, message_up, message_down, over, back_down, back_up, ghosts
):
    total = (near_sums[...] + dot(table[...], received[0:HALF, :])).astype(bf16)
    ends = HALF + 8 * GHOST
    part = (kept[...] + received[ends : ends + PART, :].astype(f32)).astype(bf16)
    radial = (joined[ends + PART :, :].astype(f32) + received[ends + PART :, :].astype(f32)).astype(bf16)
    for target in (message_up, message_down, over):
        target[0 : 2 * KB, :] = total
        target[2 * KB : 2 * KB + PART, :] = part
        target[2 * KB + PART : 2 * KB + PART + 16, :] = radial
    ghosts[0 : 8 * GHOST, :] = joined[HALF:ends, :]
    ghosts[8 * GHOST :, :] = received[HALF:ends, :]
    place = place_in_row()

    def returned(owner, above):
        start = at_block(place ^ owner, 2 * GHOST) + above * GHOST
        return ghosts[pl.ds(pl.multiple_of(start, GHOST), GHOST), :]

    back_down[...] = returned((place + ROW - 1) % ROW, 1)
    back_up[...] = returned((place + 1) % ROW, 0)
    first = 2 * KB + PART + 16
    message_up[first:, :] = returned(ROW - 1, 1)
    message_down[first:, :] = returned(0, 0)


def charge_back_kernel(own, up, down, over, filt, near, far, near_gain, far_gain, send, keep, early, field):
    field[...] = field_of(column_sum(own, up, down, over, slice(0, 2 * KB)), filt, inv_waves * inv_atoms)
    early[...] = column_sum(own, up, down, over, slice(2 * KB, 2 * KB + PART + 16)).astype(bf16)
    send[...] = (dot_rows(far[...], field[...]) * far_gain[...]).astype(bf16)
    keep[...] = dot_rows(near[...], field[...]) * near_gain[...]


def charge_kernel(field, early, near_table, near_gain, near_rows, far_table, far_gain, far_rows, message):
    total = jnp.zeros((C, C), f32)
    for table, gain, rows in ((near_table, near_gain, near_rows), (far_table, far_gain, far_rows)):
        total = total + dot(rows[...], (dot(table[...], field[...]) * gain[...]).astype(bf16))
    message[0:C, :] = total.astype(bf16)
    message[C:, :] = early[...]


def tail_spread_kernel(held, received, mine, other, own, grads, *sends):
    values = held[...] + received[...].astype(f32)
    total = (mine[...].astype(f32) + other[...].astype(f32)).astype(bf16)
    own[...] = values[0:ATOMS]
    grads[...] = total
    for part, send in enumerate(sends):
        send[0:ATOMS, :] = values[ATOMS * (part + 1) : ATOMS * (part + 2)].astype(bf16)
        send[ATOMS:, :] = total[0 : C + PART]


def raw_kernel(held, grads, near, across, corner, raw, message):
    rows = slice(0, ATOMS)
    raw[...] = tree(held[...], near[rows, :], across[rows, :], corner[rows, :]).astype(bf16)
    rows = slice(ATOMS, ATOMS + C)
    message[0:C, :] = tree(grads[0:C, :], near[rows, :], across[rows, :], corner[rows, :]).astype(bf16)
    quarters = message.at[C : 2 * C]
    quarters[z_at(0, PART), :] = grads[C : C + PART, :]
    for part, received in ((1, near), (2, across), (3, corner)):
        quarters[z_at(part, PART), :] = received[ATOMS + C :, :]
    message[2 * C :, :] = grads[C + PART :, :]


def cell_sum_kernel(own, near, across, corner, out):
    out[...] = tree(own[...], near[...], across[...], corner[...]) * grad_scale


def feature_kernel(raw, w_charge, own, downs, ups, back_down, back_up, up, down, out, token):
    place = place_in_row()
    first = 2 * KB + PART + 16
    returned = jnp.where(place == 0, up[first:, :], back_down[...])
    total = own[...] + dot_lanes(raw[...], w_charge[...])
    atom = iota((ATOMS, GHOST), 0)
    total = total + dot((atom == downs[...]).astype(f32).astype(bf16), returned)
    returned = jnp.where(place == ROW - 1, down[first:, :], back_up[...])
    total = total + dot((atom == ups[...]).astype(f32).astype(bf16), returned)
    out[...] = total.astype(bf16)
    token[...] = total[0:8]


def weights_kernel(own, other, charge, message, radial, out):
    charge[...] = own[0:C, :] + other[0:C, :]
    for total, at in ((own, core()), (other, 1 - core())):
        for z in range(4):
            start = C + PART * z
            message[rows_at(2 * z + at, 16), :] = total[start : start + 16, :]
            out[rows_at(2 * z + at, 16), :] = total[start + 16 : start + PART, :]
    radial[...] = own[2 * C : 2 * C + NB, :]


def swap(values, axis, mask):
    count = lax.axis_size(axis)
    return lax.ppermute(values, axis, [(i, i ^ mask) for i in range(count)])


def from_y(values, by):
    return lax.ppermute(values, "dom", [(i, (i + ROW * by) % DOMS) for i in range(DOMS)])


def per_device(
    feats,
    positions,
    species,
    wave_vectors,
    smearing,
    species_gain,
    w_charge,
    w_message,
    w_radial,
    w_out,
    edge_sender,
    edge_receiver,
    edge_mask,
    edge_length,
    ghost_down,
    ghost_up,
    cotangent,
):
    own_rows = feats[0]
    cot = cotangent[0]

    def edges(first, count, total, after):
        (out,) = call(
            lambda *refs: edge_kernel(first, count, *refs),
            [((NB * ATOMS, EXT), f32)],
            *edge_arrays, *total,
            scratch=[pltpu.VMEM((NB * ATOMS, CHUNK), bf16), pltpu.VMEM((EXT, CHUNK), bf16)],
            flops=count * 2 * NB * ATOMS * CHUNK * 256,
            after=after,
            name="edges",
        )
        return out

    in_place = pl.BlockSpec(memory_space=pltpu.HBM)
    arrays = (
        own_rows, positions.transpose(1, 0, 2), species, ghost_down, ghost_up,
        edge_sender, edge_receiver, edge_mask, edge_length,
    )
    packed, *edge_arrays = call(
        pack_kernel,
        [((PACK, C), bf16)] + [((1, EDGES), jnp.int32)] * 3 + [((1, EDGES), f32)],
        *[pltpu.with_memory_space_constraint(values, pltpu.HBM) for values in arrays],
        scratch=[
            pltpu.VMEM((16, C), f32), pltpu.VMEM((ATOMS, C), bf16), pltpu.VMEM((3, 1, ATOMS), f32),
            pltpu.VMEM((1, ATOMS), jnp.int32), pltpu.VMEM((2, 1, GHOST), jnp.int32), pltpu.SemaphoreType.DMA((9,)),
        ],
        in_specs=[in_place] * 9,
        out_specs=[pl.BlockSpec(memory_space=pltpu.VMEM)] * 5,
        name="pack",
    )
    operator = edges(0, EDGE_STEPS[0], [], [packed])
    (near_rows,) = call(
        gather_kernel,
        [((ROW // 2 * PACK, C), bf16)],
        packed, *[swap(packed, "dom", mask) for mask in (2, 4, 6)],
        after=[operator],
        name="gather",
    )
    far_rows = swap(near_rows, "dom", 1)
    near, near_sums, filt, near_gain = call(
        structure_near_kernel,
        [((2 * KB, HALF), bf16), ((2 * KB, C), f32), ((KB, C), f32), ((HALF, C), f32)],
        near_rows, wave_vectors, smearing[None], species_gain, w_charge,
        scratch=[pltpu.VMEM((HALF, C), bf16)],
        name="structure_near",
    )
    far, sums, message_up, message_down, far_gain, below, above = call(
        structure_far_kernel,
        [
            ((2 * KB, HALF), bf16), ((2 * KB, C), bf16), ((2 * KB + GHOST, C), bf16), ((2 * KB + GHOST, C), bf16),
            ((HALF, C), f32), ((GHOST, C), bf16), ((GHOST, C), bf16),
        ],
        far_rows, near_rows, near_sums, wave_vectors, species_gain, w_charge,
        scratch=[pltpu.VMEM((HALF, C), bf16), pltpu.VMEM((ROW * PACK, C), bf16)],
        name="structure_far",
    )
    up, down, over = from_y(message_up, 1), from_y(message_down, -1), from_y(sums, 2)
    operator = edges(EDGE_STEPS[0], EDGE_STEPS[1], [operator], [message_up])
    (own_near,) = call(copy_kernel, [((NEAR, C), bf16)], near_rows, after=[operator], name="copy")
    other_near = swap(own_near, "dom", 8)
    send, keep = call(
        potential_kernel,
        [((HALF, C), bf16), ((HALF, C), f32)],
        sums, up, down, over, filt, near, far,
        after=[own_near],
        name="potential",
    )
    received = swap(send, "dom", 1)
    held, *sends = call(
        spread_kernel, [((ATOMS, C), f32)] + [((ATOMS, C), bf16)] * 3, keep, received, name="spread"
    )
    parts = [swap(values, "dom", 2 * (part + 1)) for part, values in enumerate(sends)]
    aggregate, radial_rows, extended = call(
        aggregate_kernel,
        [((ATOMS, C), f32), ((NB * ATOMS, C), f32), ((EXT, C), bf16)],
        own_rows, below, above, up, down, w_message, operator, w_radial,
        name="aggregate",
    )
    (pair,) = call(
        pair_kernel, [((2 * NEAR, C), bf16)], own_near, other_near, after=[aggregate], name="pair"
    )
    other_pair = swap(pair, "dom", 24)
    act, own_total, back_rows, quarter, radial, *sends = call(
        update_kernel,
        [((ATOMS, C), bf16), ((ATOMS, C), f32), ((EXT, C), bf16), ((QUARTER, C), f32), ((16, C), bf16)]
        + [((EXT + QUARTER + 16, C), bf16)] * 3,
        held, *parts, aggregate, cot, w_out, extended, w_message, operator, radial_rows, w_radial,
        scratch=[pltpu.VMEM((2 * C, C), f32)],
        name="update",
    )
    parts = [swap(values, "dom", 2 * (part + 1)) for part, values in enumerate(sends)]
    updated, token = call(
        updated_kernel, [((ATOMS, C), bf16), ((8, C), f32)], own_rows, act, w_out, after=[sends[0]], name="updated"
    )
    joined, kept = call(
        join_kernel,
        [((HALF + 8 * GHOST + PART + 16, C), bf16), ((PART, C), f32)],
        back_rows, quarter, radial, *parts,
        scratch=[pltpu.VMEM((QUARTER, C), f32)],
        after=[token],
        name="join",
    )
    received = swap(joined, "dom", 1)
    (near_sums,) = call(back_near_kernel, [((2 * KB, C), f32)], near, joined, name="back_near")
    message_up, message_down, over, back_down, back_up = call(
        back_far_kernel,
        [
            ((2 * KB + PART + 16 + GHOST, C), bf16), ((2 * KB + PART + 16 + GHOST, C), bf16),
            ((2 * KB + PART + 16, C), bf16),
            ((GHOST, C), bf16), ((GHOST, C), bf16),
        ],
        far, received, joined, kept, near_sums,
        scratch=[pltpu.VMEM((16 * GHOST, C), bf16)],
        name="back_far",
    )
    (near_column,) = call(
        collect_kernel, [((COLUMN * NEAR, C), bf16)], pair, other_pair, after=[over], name="collect"
    )
    far_column = swap(near_column, "dom", 1)
    column_shapes = [((COLUMN * HALF, 2 * KB), bf16), ((COLUMN * HALF, C), f32), ((C, COLUMN * HALF), bf16)]
    near_table, near_column_gain, near_turned = call(
        column_tables_kernel, column_shapes, near_column, wave_vectors, species_gain, after=[over], name="near_tables"
    )
    far_table, far_column_gain, far_turned = call(
        column_tables_kernel, column_shapes, far_column, wave_vectors, species_gain, after=[over], name="far_tables"
    )
    sums = over
    up, down, over = from_y(message_up, 1), from_y(message_down, -1), from_y(over, 2)
    send, keep, early, field = call(
        charge_back_kernel,
        [((HALF, C), bf16), ((HALF, C), f32), ((PART + 16, C), bf16), ((2 * KB, C), bf16)],
        sums, up, down, over, filt, near, far, near_gain, far_gain,
        after=[near_column_gain, far_column_gain],
        name="charge_back",
    )
    received = swap(send, "dom", 1)
    (message,) = call(
        charge_kernel,
        [((C + PART + 16, C), bf16)],
        field, early, near_table, near_column_gain, near_turned, far_table, far_column_gain, far_turned,
        after=[send],
        name="charge",
    )
    other = swap(message, ("cell", "dom"), DOMS + 6)
    held, grads, *sends = call(
        tail_spread_kernel,
        [((ATOMS, C), f32), ((C + PART + 16, C), bf16)] + [((ATOMS + C + PART, C), bf16)] * 3,
        keep, received, message, other,
        name="tail_spread",
    )
    parts = [swap(values, "dom", 2 * (part + 1)) for part, values in enumerate(sends)]
    raw, message = call(
        raw_kernel, [((ATOMS, C), bf16), ((2 * C + 16, C), bf16)], held, grads, *parts, name="raw"
    )
    parts = [swap(message, "cell", mask) for mask in (2, 4, 6)]
    feat_grad, token = call(
        feature_kernel,
        [((ATOMS, C), bf16), ((8, C), f32)],
        raw, w_charge, own_total, ghost_down, ghost_up, back_down, back_up, up, down,
        after=[message],
        name="feature",
    )
    (total,) = call(cell_sum_kernel, [((2 * C + 16, C), f32)], message, *parts, after=[token], name="cell_sum")
    charge, message, radial, out = call(
        weights_kernel,
        [((C, C), f32), ((C, C), f32), ((NB, C), f32), ((C, C), f32)],
        total, swap(total, "dom", 1),
        name="weights",
    )
    return updated[None], feat_grad[None], charge, message, radial, out


def solution(mesh):
    placed = (
        P("cell", "dom", None),
        P("cell", None, "dom"),
        P("cell", "dom"),
        P(),
        P(),
        P(),
        P(),
        P(),
        P(),
        P(),
        P("cell", "dom"),
        P("cell", "dom"),
        P("cell", "dom"),
        P("cell", "dom"),
        P("cell", "dom"),
        P("cell", "dom"),
        P("cell", "dom", None),
    )
    return jax.shard_map(
        per_device,
        mesh=mesh,
        in_specs=placed,
        out_specs=(P("cell", "dom", None), P("cell", "dom", None), P(), P(), P(), P()),
        check_vma=False,
    )
```

```python
import math

import jax
import jax.numpy as jnp
from jax import lax
from jax.experimental import pallas as pl
from jax.experimental.pallas import tpu as pltpu
from jax.sharding import PartitionSpec as P

bf16 = jnp.bfloat16
f32 = jnp.float32

C = 128
K = 2048
NB = 8
ATOMS = 128
GHOST = 32
EXT = ATOMS + 2 * GHOST
EDGES = 12288
DOMS = 32
CELLS = 8
ROW = 8
KB = K // ROW
PACK = ATOMS + 16
QUARTER = 64
PART = QUARTER // 2
NEAR = ROW // 2 * PACK
COLUMN = 4
HALF = ROW * ATOMS // 2
CHUNK = 1024
EDGE_STEPS = (5, 7)

cutoff_radius = 6.0
basis_width = 0.75
edge_scale = 0.25
filter_factor = 12.0
inv_waves = 1.0 / math.sqrt(K)
inv_atoms = 1.0 / math.sqrt(ATOMS * DOMS)
grad_scale = 1.0 / math.sqrt(CELLS * ATOMS * DOMS)

COS_TURN = (
    0.9999999890754399,
    -19.73920450099313,
    64.93911749956553,
    -85.45013994347214,
    60.16763282514798,
    -25.967602441408868,
    6.528658639370483,
)
SIN_TURN = (
    6.283184916984331,
    -41.34158926418157,
    81.59994386455666,
    -76.61447586020026,
    41.342889428722025,
    -12.471244745942547,
)

MIX = (
    (1.25563, -0.56805, 0.251163, -0.11939, 0.059896, -0.030538, 0.014724, -0.005361),
    (-0.56805, 1.647472, -0.773752, 0.355088, -0.172104, 0.085726, -0.040753, 0.014724),
    (0.251163, -0.773752, 1.767661, -0.8374, 0.386766, -0.185002, 0.085726, -0.030538),
    (-0.11939, 0.355088, -0.8374, 1.801205, -0.851469, 0.386766, -0.172104, 0.059896),
    (0.059896, -0.172104, 0.386766, -0.851469, 1.801205, -0.8374, 0.355088, -0.11939),
    (-0.030538, 0.085726, -0.185002, 0.386766, -0.8374, 1.767661, -0.773752, 0.251163),
    (0.014724, -0.040753, 0.085726, -0.172104, 0.355088, -0.773752, 1.647472, -0.56805),
    (-0.005361, 0.014724, -0.030538, 0.059896, -0.11939, 0.251163, -0.56805, 1.25563),
    (0.943774626, 0.330363768, 0.0119126827, 0.00237723804, -0.00100488116, 0.000442211757, -0.000188380319, 6.26400104e-05),
    (0.330363768, 0.879800949, 0.341632643, 0.00920268838, 0.00330706128, -0.00137507484, 0.000571783509, -0.000188380319),
    (0.0119126827, 0.341632643, 0.874756301, 0.343305856, 0.00862722425, 0.0034955942, -0.00137507484, 0.000442211757),
    (0.00237723804, 0.00920268838, 0.343305856, 0.87403504, 0.343551294, 0.00862722425, 0.00330706128, -0.00100488116),
    (-0.00100488116, 0.00330706128, 0.00862722425, 0.343551294, 0.87403504, 0.343305856, 0.00920268838, 0.00237723804),
    (0.000442211757, -0.00137507484, 0.0034955942, 0.00862722425, 0.343305856, 0.874756301, 0.341632643, 0.0119126827),
    (-0.000188380319, 0.000571783509, -0.00137507484, 0.00330706128, 0.00920268838, 0.341632643, 0.879800949, 0.330363768),
    (6.26400104e-05, -0.000188380319, 0.000442211757, -0.00100488116, 0.00237723804, 0.0119126827, 0.330363768, 0.943774626),
)


def horner(coefficients, x):
    total = jnp.full_like(x, coefficients[-1])
    for value in coefficients[-2::-1]:
        total = total * x + value
    return total


def iota(shape, axis):
    return lax.broadcasted_iota(jnp.int32, shape, axis)


def dot(left, right):
    return jnp.dot(left, right, preferred_element_type=f32)


def thirds(values):
    rest = jnp.concatenate([values, jnp.zeros_like(values)], axis=0)
    parts = []
    for _ in range(3):
        parts.append(rest.astype(bf16))
        rest = rest - parts[-1].astype(f32)
    return parts


def pick(onehot, parts):
    chosen = onehot.astype(bf16)
    return dot_rows(chosen, parts[0]) + dot_rows(chosen, parts[1]) + dot_rows(chosen, parts[2])


def mixed(table, values):
    at = iota((NB, C), 0)
    total = None
    for j in range(NB):
        column = jnp.full((NB, C), table[0][j], f32)
        for b in range(1, NB):
            column = jnp.where(at == b, table[b][j], column)
        column = jnp.concatenate([column] * (values.shape[1] // C), axis=1)
        part = column * values[j : j + 1, :]
        total = part if total is None else total + part
    return total


def dot_rows(left, right):
    return lax.dot_general(left, right, (((0,), (0,)), ((), ())), preferred_element_type=f32)


def dot_lanes(left, right):
    return lax.dot_general(left, right, (((1,), (1,)), ((), ())), preferred_element_type=f32)


def split(values):
    high = values.astype(bf16)
    return high, (values - high.astype(f32)).astype(bf16)


def call(kernel, outs, *args, scratch=(), flops=0, after=(), name=None, **more):
    def run(*refs):
        kernel(*refs[: len(args)], *refs[len(args) + len(after) :])

    if "in_specs" not in more:
        more["in_specs"] = [pl.BlockSpec(memory_space=pltpu.VMEM)] * len(args)
        more["out_specs"] = [pl.BlockSpec(memory_space=pltpu.VMEM)] * len(outs)
    more["in_specs"] = more["in_specs"] + [pl.BlockSpec(memory_space=pl.ANY)] * len(after)
    return pl.pallas_call(
        run,
        out_shape=[jax.ShapeDtypeStruct(shape, dtype) for shape, dtype in outs],
        scratch_shapes=list(scratch),
        compiler_params=pltpu.CompilerParams(vmem_limit_bytes=40 * 1024 * 1024),
        cost_estimate=pl.CostEstimate(flops=flops, bytes_accessed=1 << 18, transcendentals=0),
        name=name,
        **more,
    )(*args, *after)


def place_in_row():
    return lax.rem(lax.axis_index("dom"), ROW)


def at_block(mask, rows):
    return pl.multiple_of((mask // 2 + (mask % 2) * (ROW // 2)) * rows, rows)


def rows_at(index, count):
    return pl.ds(pl.multiple_of(index * count, count), count)


def z_at(part, count):
    quarter = (place_in_row() // 2) ^ (3 * lax.rem(lax.axis_index("cell"), 2))
    return rows_at(quarter ^ part, count)


def core():
    return lax.rem(lax.axis_index("dom"), 2)


def tree(own, near, across, corner):
    return (own.astype(f32) + near.astype(f32)) + (across.astype(f32) + corner.astype(f32))


def pack_kernel(
    feats, coords, kinds, downs, ups, sent, got, live, reach,
    packed, senders, receivers, mask, lengths, tail, whole, places, labels, indices, sems,
):
    near = [(feats, whole), (coords, places), (kinds, labels), (ups, indices.at[0]), (downs, indices.at[1])]
    edges = [(sent, senders), (got, receivers), (live, mask), (reach, lengths)]
    copies = [
        pltpu.make_async_copy(source, target, sems.at[i]) for i, (source, target) in enumerate(near + edges)
    ]
    for copy in copies:
        copy.start()
    for copy in copies[: len(near)]:
        copy.wait()
    packed[0:ATOMS, :] = whole[...]
    at = iota((16, ATOMS), 0)
    values = jnp.where(at == 9, labels[...].astype(f32), 0.0)
    for axis in range(3):
        place = places[axis]
        for part in range(3):
            piece = place.astype(bf16).astype(f32)
            values = jnp.where(at == 3 * part + axis, piece, values)
            place = place - piece
    tail[...] = values
    tail[10:11, 0:GHOST] = indices[0].astype(f32)
    tail[11:12, 0:GHOST] = indices[1].astype(f32)
    packed[ATOMS:PACK, :] = tail[...].astype(bf16)
    for copy in copies[len(near) :]:
        copy.wait()


def gather_kernel(own, near, across, corner, out):
    for part, rows in enumerate((own, near, across, corner)):
        out[PACK * part : PACK * (part + 1), :] = rows[...]


def wave_lanes(waves):
    mine = waves[:, pl.ds(pl.multiple_of(place_in_row() * KB, KB), KB)].astype(f32)
    at = iota((16, KB), 0)
    stacked = jnp.zeros((16, KB), f32)
    for axis in range(3):
        stacked = jnp.where(at == axis, mine[axis : axis + 1, :], stacked)
    stacked = stacked.astype(bf16)
    axis_at = iota((16, C), 0)
    return [dot_rows(stacked, (axis_at == axis).astype(f32).astype(bf16)) for axis in range(3)]


def tables_of(packed, lanes, species_gain, w_charge, table, gain, charges):
    kind_at = iota((16, ATOMS), 0).astype(f32)
    gains = thirds(species_gain[...])
    for j in range(ROW // 2):
        rows = packed[PACK * j : PACK * j + ATOMS, :]
        tail = packed[PACK * j + ATOMS : PACK * (j + 1), :].astype(f32)
        onehot = (tail[9:10, :] == kind_at).astype(f32)
        own_gain = pick(onehot, gains)
        span = slice(ATOMS * j, ATOMS * (j + 1))
        gain[span, :] = own_gain
        charges[span, :] = (dot(rows, w_charge[...]) * own_gain).astype(bf16)
        turns = jnp.zeros((KB, ATOMS), f32)
        for axis in range(3):
            place = tail[axis : axis + 1, :] + tail[axis + 3 : axis + 4, :] + tail[axis + 6 : axis + 7, :]
            turns = turns + place * lanes[axis]
        turns = turns - jnp.round(turns)
        square = turns * turns
        table[0:KB, span] = horner(COS_TURN, square).astype(bf16)
        table[KB : 2 * KB, span] = (turns * horner(SIN_TURN, square)).astype(bf16)


def structure_near_kernel(packed, waves, smearing, species_gain, w_charge, table, sums, filt, gain, charges):
    lanes = wave_lanes(waves)
    squared = lanes[0] * lanes[0] + lanes[1] * lanes[1] + lanes[2] * lanes[2]
    filt[...] = filter_factor * jnp.exp(-squared * smearing[...]) / jnp.sqrt(squared)
    tables_of(packed, lanes, species_gain, w_charge, table, gain, charges)
    sums[...] = dot(table[...], charges[...])


def ghosts(joined, owner, row):
    atom = iota((ATOMS, GHOST), 0).astype(f32)
    start = at_block(place_in_row() ^ owner, PACK)
    rows = joined[pl.ds(start, ATOMS), :]
    tail = joined[pl.ds(pl.multiple_of(start + ATOMS, 16), 16), :].astype(f32)
    return dot_rows((atom == tail[row : row + 1, 0:GHOST]).astype(f32).astype(bf16), rows).astype(bf16)


def structure_far_kernel(
    packed, near, near_sums, waves, species_gain, w_charge,
    table, sums, message_up, message_down, gain, joined, charges,
):
    tables_of(packed, wave_lanes(waves), species_gain, w_charge, table, gain, charges)
    total = (near_sums[...] + dot(table[...], charges[...])).astype(bf16)
    sums[...] = total
    message_up[0 : 2 * KB, :] = total
    message_down[0 : 2 * KB, :] = total
    joined[0:NEAR, :] = near[...]
    joined[NEAR:, :] = packed[...]
    message_up[2 * KB :, :] = ghosts(joined, ROW - 1, 10)
    message_down[2 * KB :, :] = ghosts(joined, 0, 11)


def copy_kernel(rows, joined, out, below, above):
    out[...] = rows[...]
    place = place_in_row()
    below[...] = ghosts(joined, (place + ROW - 1) % ROW, 10)
    above[...] = ghosts(joined, (place + 1) % ROW, 11)


def pair_kernel(own, other, out):
    out[0:NEAR, :] = own[...]
    out[NEAR:, :] = other[...]


def collect_kernel(pair, other, out):
    mine = lax.axis_index("dom") // ROW
    for at, rows, half in ((mine, pair, 0), (mine ^ 1, pair, 1), (mine ^ 3, other, 0), (mine ^ 2, other, 1)):
        out[rows_at(at, NEAR), :] = rows[NEAR * half : NEAR * (half + 1), :]


def column_tables_kernel(packed, waves, species_gain, table, gain, turned):
    mine = waves[:, pl.ds(pl.multiple_of(place_in_row() * KB, KB), KB)].astype(f32)
    at = iota((16, KB), 0)
    kind_at = iota((16, ATOMS), 0).astype(f32)
    gains = thirds(species_gain[...])
    for j in range(COLUMN * ROW // 2):
        tail = packed[PACK * j + ATOMS : PACK * (j + 1), :]
        turned[:, ATOMS * j : ATOMS * (j + 1)] = packed[PACK * j : PACK * j + ATOMS, :].T
        span = slice(ATOMS * j, ATOMS * (j + 1))
        turns = jnp.zeros((ATOMS, KB), f32)
        for axis in range(3):
            chosen = (at == axis) | (at == axis + 3) | (at == axis + 6)
            turns = turns + dot_rows(tail, chosen.astype(f32).astype(bf16)) * mine[axis : axis + 1, :]
        turns = turns - jnp.round(turns)
        square = turns * turns
        table[span, 0:KB] = horner(COS_TURN, square).astype(bf16)
        table[span, KB : 2 * KB] = (turns * horner(SIN_TURN, square)).astype(bf16)
        onehot = (tail.astype(f32)[9:10, :] == kind_at).astype(f32)
        gain[span, :] = pick(onehot, gains)


def column_sum(own, up, down, over, span):
    return tree(own[span, :], over[span, :], up[span, :], down[span, :])


def field_of(sums, filt, scale):
    weight = filt[...] * scale
    return jnp.concatenate(
        [(weight * sums[0:KB]).astype(bf16), (weight * sums[KB : 2 * KB]).astype(bf16)], axis=0
    )


def potential_kernel(own, up, down, over, filt, near, far, send, keep):
    field = field_of(column_sum(own, up, down, over, slice(0, 2 * KB)), filt, inv_atoms)
    send[...] = (dot_rows(far[...], field) * inv_waves).astype(bf16)
    keep[...] = dot_rows(near[...], field) * inv_waves


def spread_kernel(held, received, own, *sends):
    values = held[...] + received[...].astype(f32)
    own[...] = values[0:ATOMS]
    for part, send in enumerate(sends):
        send[...] = values[ATOMS * (part + 1) : ATOMS * (part + 2)].astype(bf16)


def edge_kernel(first, count, *refs):
    total, left, right = refs[-3:]
    for step in range(first, first + count):
        senders, receivers, live, reach = (ref[:, CHUNK * step : CHUNK * (step + 1)] for ref in refs[:4])
        turn = reach * (0.5 / cutoff_radius)
        envelope = 0.5 * (horner(COS_TURN, turn * turn) + 1.0) * live.astype(f32)
        centers = 0.5 + basis_width * iota((NB, CHUNK), 0).astype(f32)
        offset = (reach - centers) * (1.0 / basis_width)
        weights = (mixed(MIX[:NB], jnp.exp(-offset * offset)) * envelope).astype(bf16)
        atom = iota((ATOMS, CHUNK), 0)
        onehot = (atom == receivers).astype(f32).astype(bf16)
        for b in range(NB):
            left[ATOMS * b : ATOMS * (b + 1), :] = onehot * weights[b : b + 1, :]
        source = iota((EXT, CHUNK), 0)
        right[...] = (source == senders).astype(f32).astype(bf16)
        products = dot_lanes(left[...], right[...])
        if step > first:
            total[...] += products
        elif first:
            total[...] = refs[4][...] + products
        else:
            total[...] = products


def aggregate_kernel(feats, below, above, up, down, w_message, operator, w_radial, aggregate, radial_rows, extended):
    place = place_in_row()
    extended[0:ATOMS, :] = feats[...]
    extended[ATOMS : ATOMS + GHOST, :] = jnp.where(place == 0, up[2 * KB :, :], below[...])
    extended[ATOMS + GHOST :, :] = jnp.where(place == ROW - 1, down[2 * KB :, :], above[...])
    rows = dot(extended[...], w_message[...]).astype(bf16)
    high, low = split(operator[...])
    products = dot(high, rows) + dot(low, rows)
    radial_rows[...] = products
    weights = mixed(MIX[NB:], w_radial[...])
    total = jnp.zeros((ATOMS, C), f32)
    for b in range(NB):
        total = total + weights[b : b + 1, :] * products[ATOMS * b : ATOMS * (b + 1)]
    aggregate[...] = total * edge_scale


def update_kernel(
    held, near, across, corner, aggregate, cotangent, w_out, extended, w_message, operator, radial_rows, w_radial,
    act_out, own_total, own_rows, own_quarter, own_radial, send_near, send_across, send_corner, grads,
):
    preact = aggregate[...] + tree(held[...], near[...], across[...], corner[...])
    sig = jax.nn.sigmoid(preact)
    grad_act = dot_lanes(cotangent[...], w_out[...])
    grad = grad_act * sig * (1.0 + preact * (1.0 - sig))
    rounded = grad.astype(bf16)
    grad = grad * edge_scale
    weights = mixed(MIX[NB:], w_radial[...])
    stacked = split(jnp.concatenate([weights[b : b + 1, :] * grad for b in range(NB)], axis=0))
    high, low = split(operator[...])
    products = dot_rows(high, jnp.concatenate(stacked, axis=1))
    grad_msg = (products[:, :C] + products[:, C:] + dot_rows(low, stacked[0])).astype(bf16)
    grad_rows = dot_lanes(grad_msg, w_message[...])
    own_total[...] = cotangent[...].astype(f32) + grad_rows[:ATOMS]
    own_rows[0:ATOMS, :] = rounded
    own_rows[ATOMS:, :] = grad_rows[ATOMS:].astype(bf16)
    act = (preact * sig).astype(bf16)
    act_out[...] = act
    grad_message = dot_rows(extended[...], grad_msg)
    grad_out = dot_rows(act, cotangent[...])
    for t in range(ROW):
        grads[PART * t : PART * t + 16, :] = grad_message[16 * t : 16 * (t + 1)]
        grads[PART * t + 16 : PART * (t + 1), :] = grad_out[16 * t : 16 * (t + 1)]
    at = iota((NB, C), 0)
    tail = jnp.zeros((NB, C), f32)
    for b in range(NB):
        part = jnp.sum(grad * radial_rows[ATOMS * b : ATOMS * (b + 1), :], axis=0, keepdims=True)
        tail = jnp.where(at == b, part, tail)
    tail = jnp.concatenate([mixed(MIX[NB:], tail), jnp.zeros((NB, C), f32)], axis=0).astype(bf16)
    own_radial[...] = tail
    own_quarter[...] = grads[z_at(0, QUARTER), :]
    for part, send in ((1, send_near), (2, send_across), (3, send_corner)):
        send[0:EXT, :] = own_rows[...]
        send[EXT : EXT + QUARTER, :] = grads[z_at(part, QUARTER), :].astype(bf16)
        send[EXT + QUARTER :, :] = tail


def updated_kernel(feats, act, w_out, updated, token):
    total = feats[...].astype(f32) + dot(act[...], w_out[...])
    updated[...] = total.astype(bf16)
    token[...] = total[0:8]


def join_kernel(own_rows, own_quarter, own_radial, near, across, corner, joined, kept, sums):
    quarter = own_quarter[...]
    for part, rows in enumerate((own_rows, near, across, corner)):
        joined[ATOMS * part : ATOMS * (part + 1), :] = rows[0:ATOMS, :]
        start = HALF + 2 * GHOST * part
        joined[start : start + 2 * GHOST, :] = rows[ATOMS:EXT, :]
        if part:
            quarter = quarter + rows[EXT : EXT + QUARTER, :].astype(f32)
    sums[...] = quarter
    kept[...] = sums[rows_at(core(), PART), :]
    ends = HALF + 8 * GHOST
    joined[ends : ends + PART, :] = sums[rows_at(1 - core(), PART), :].astype(bf16)
    last = slice(EXT + QUARTER, EXT + QUARTER + 16)
    joined[ends + PART :, :] = tree(own_radial[...], near[last, :], across[last, :], corner[last, :]).astype(bf16)


def back_near_kernel(table, joined, sums):
    sums[...] = dot(table[...], joined[0:HALF, :])


def back_far_kernel(
    table, received, joined, kept, near_sums, message_up, message_down, over, back_down, back_up, ghosts
):
    total = (near_sums[...] + dot(table[...], received[0:HALF, :])).astype(bf16)
    ends = HALF + 8 * GHOST
    part = (kept[...] + received[ends : ends + PART, :].astype(f32)).astype(bf16)
    radial = (joined[ends + PART :, :].astype(f32) + received[ends + PART :, :].astype(f32)).astype(bf16)
    for target in (message_up, message_down, over):
        target[0 : 2 * KB, :] = total
        target[2 * KB : 2 * KB + PART, :] = part
        target[2 * KB + PART : 2 * KB + PART + 16, :] = radial
    ghosts[0 : 8 * GHOST, :] = joined[HALF:ends, :]
    ghosts[8 * GHOST :, :] = received[HALF:ends, :]
    place = place_in_row()

    def returned(owner, above):
        start = at_block(place ^ owner, 2 * GHOST) + above * GHOST
        return ghosts[pl.ds(pl.multiple_of(start, GHOST), GHOST), :]

    back_down[...] = returned((place + ROW - 1) % ROW, 1)
    back_up[...] = returned((place + 1) % ROW, 0)
    first = 2 * KB + PART + 16
    message_up[first:, :] = returned(ROW - 1, 1)
    message_down[first:, :] = returned(0, 0)


def charge_back_kernel(own, up, down, over, filt, near, far, near_gain, far_gain, send, keep, early, field):
    field[...] = field_of(column_sum(own, up, down, over, slice(0, 2 * KB)), filt, inv_waves * inv_atoms)
    early[...] = column_sum(own, up, down, over, slice(2 * KB, 2 * KB + PART + 16)).astype(bf16)
    send[...] = (dot_rows(far[...], field[...]) * far_gain[...]).astype(bf16)
    keep[...] = dot_rows(near[...], field[...]) * near_gain[...]


def charge_kernel(field, early, near_table, near_gain, near_rows, far_table, far_gain, far_rows, message):
    total = jnp.zeros((C, C), f32)
    for table, gain, rows in ((near_table, near_gain, near_rows), (far_table, far_gain, far_rows)):
        total = total + dot(rows[...], (dot(table[...], field[...]) * gain[...]).astype(bf16))
    message[0:C, :] = total.astype(bf16)
    message[C:, :] = early[...]


def tail_spread_kernel(held, received, mine, other, own, grads, *sends):
    values = held[...] + received[...].astype(f32)
    total = (mine[...].astype(f32) + other[...].astype(f32)).astype(bf16)
    own[...] = values[0:ATOMS]
    grads[...] = total
    for part, send in enumerate(sends):
        send[0:ATOMS, :] = values[ATOMS * (part + 1) : ATOMS * (part + 2)].astype(bf16)
        send[ATOMS:, :] = total[0 : C + PART]


def raw_kernel(held, grads, near, across, corner, raw, message):
    rows = slice(0, ATOMS)
    raw[...] = tree(held[...], near[rows, :], across[rows, :], corner[rows, :]).astype(bf16)
    rows = slice(ATOMS, ATOMS + C)
    message[0:C, :] = tree(grads[0:C, :], near[rows, :], across[rows, :], corner[rows, :]).astype(bf16)
    quarters = message.at[C : 2 * C]
    quarters[z_at(0, PART), :] = grads[C : C + PART, :]
    for part, received in ((1, near), (2, across), (3, corner)):
        quarters[z_at(part, PART), :] = received[ATOMS + C :, :]
    message[2 * C :, :] = grads[C + PART :, :]


def cell_sum_kernel(own, near, across, corner, out):
    out[...] = tree(own[...], near[...], across[...], corner[...]) * grad_scale


def feature_kernel(raw, w_charge, own, downs, ups, back_down, back_up, up, down, out, token):
    place = place_in_row()
    first = 2 * KB + PART + 16
    returned = jnp.where(place == 0, up[first:, :], back_down[...])
    total = own[...] + dot_lanes(raw[...], w_charge[...])
    atom = iota((ATOMS, GHOST), 0)
    total = total + dot((atom == downs[...]).astype(f32).astype(bf16), returned)
    returned = jnp.where(place == ROW - 1, down[first:, :], back_up[...])
    total = total + dot((atom == ups[...]).astype(f32).astype(bf16), returned)
    out[...] = total.astype(bf16)
    token[...] = total[0:8]


def weights_kernel(own, other, charge, message, radial, out):
    charge[...] = own[0:C, :] + other[0:C, :]
    for total, at in ((own, core()), (other, 1 - core())):
        for z in range(4):
            start = C + PART * z
            message[rows_at(2 * z + at, 16), :] = total[start : start + 16, :]
            out[rows_at(2 * z + at, 16), :] = total[start + 16 : start + PART, :]
    radial[...] = own[2 * C : 2 * C + NB, :]


def swap(values, axis, mask):
    count = lax.axis_size(axis)
    return lax.ppermute(values, axis, [(i, i ^ mask) for i in range(count)])


def from_y(values, by):
    return lax.ppermute(values, "dom", [(i, (i + ROW * by) % DOMS) for i in range(DOMS)])


def per_device(
    feats,
    positions,
    species,
    wave_vectors,
    smearing,
    species_gain,
    w_charge,
    w_message,
    w_radial,
    w_out,
    edge_sender,
    edge_receiver,
    edge_mask,
    edge_length,
    ghost_down,
    ghost_up,
    cotangent,
):
    own_rows = feats[0]
    cot = cotangent[0]

    def edges(first, count, total, after):
        (out,) = call(
            lambda *refs: edge_kernel(first, count, *refs),
            [((NB * ATOMS, EXT), f32)],
            *edge_arrays, *total,
            scratch=[pltpu.VMEM((NB * ATOMS, CHUNK), bf16), pltpu.VMEM((EXT, CHUNK), bf16)],
            flops=count * 2 * NB * ATOMS * CHUNK * 256,
            after=after,
            name="edges",
        )
        return out

    in_place = pl.BlockSpec(memory_space=pltpu.HBM)
    arrays = (
        own_rows, positions.transpose(1, 0, 2), species, ghost_down, ghost_up,
        edge_sender, edge_receiver, edge_mask, edge_length,
    )
    packed, *edge_arrays = call(
        pack_kernel,
        [((PACK, C), bf16)] + [((1, EDGES), jnp.int32)] * 3 + [((1, EDGES), f32)],
        *[pltpu.with_memory_space_constraint(values, pltpu.HBM) for values in arrays],
        scratch=[
            pltpu.VMEM((16, C), f32), pltpu.VMEM((ATOMS, C), bf16), pltpu.VMEM((3, 1, ATOMS), f32),
            pltpu.VMEM((1, ATOMS), jnp.int32), pltpu.VMEM((2, 1, GHOST), jnp.int32), pltpu.SemaphoreType.DMA((9,)),
        ],
        in_specs=[in_place] * 9,
        out_specs=[pl.BlockSpec(memory_space=pltpu.VMEM)] * 5,
        name="pack",
    )
    operator = edges(0, EDGE_STEPS[0], [], [packed])
    (near_rows,) = call(
        gather_kernel,
        [((ROW // 2 * PACK, C), bf16)],
        packed, *[swap(packed, "dom", mask) for mask in (2, 4, 6)],
        after=[operator],
        name="gather",
    )
    far_rows = swap(near_rows, "dom", 1)
    near, near_sums, filt, near_gain = call(
        structure_near_kernel,
        [((2 * KB, HALF), bf16), ((2 * KB, C), f32), ((KB, C), f32), ((HALF, C), f32)],
        near_rows, wave_vectors, smearing[None], species_gain, w_charge,
        scratch=[pltpu.VMEM((HALF, C), bf16)],
        name="structure_near",
    )
    far, sums, message_up, message_down, far_gain, joined_rows = call(
        structure_far_kernel,
        [
            ((2 * KB, HALF), bf16), ((2 * KB, C), bf16), ((2 * KB + GHOST, C), bf16), ((2 * KB + GHOST, C), bf16),
            ((HALF, C), f32), ((ROW * PACK, C), bf16),
        ],
        far_rows, near_rows, near_sums, wave_vectors, species_gain, w_charge,
        scratch=[pltpu.VMEM((HALF, C), bf16)],
        name="structure_far",
    )
    up, down, over = from_y(message_up, 1), from_y(message_down, -1), from_y(sums, 2)
    operator = edges(EDGE_STEPS[0], EDGE_STEPS[1], [operator], [message_up])
    own_near, below, above = call(
        copy_kernel,
        [((NEAR, C), bf16), ((GHOST, C), bf16), ((GHOST, C), bf16)],
        near_rows, joined_rows,
        after=[operator],
        name="copy",
    )
    other_near = swap(own_near, "dom", 8)
    send, keep = call(
        potential_kernel,
        [((HALF, C), bf16), ((HALF, C), f32)],
        sums, up, down, over, filt, near, far,
        after=[own_near],
        name="potential",
    )
    received = swap(send, "dom", 1)
    held, *sends = call(
        spread_kernel, [((ATOMS, C), f32)] + [((ATOMS, C), bf16)] * 3, keep, received, name="spread"
    )
    parts = [swap(values, "dom", 2 * (part + 1)) for part, values in enumerate(sends)]
    aggregate, radial_rows, extended = call(
        aggregate_kernel,
        [((ATOMS, C), f32), ((NB * ATOMS, C), f32), ((EXT, C), bf16)],
        own_rows, below, above, up, down, w_message, operator, w_radial,
        name="aggregate",
    )
    (pair,) = call(
        pair_kernel, [((2 * NEAR, C), bf16)], own_near, other_near, after=[aggregate], name="pair"
    )
    other_pair = swap(pair, "dom", 24)
    act, own_total, back_rows, quarter, radial, *sends = call(
        update_kernel,
        [((ATOMS, C), bf16), ((ATOMS, C), f32), ((EXT, C), bf16), ((QUARTER, C), f32), ((16, C), bf16)]
        + [((EXT + QUARTER + 16, C), bf16)] * 3,
        held, *parts, aggregate, cot, w_out, extended, w_message, operator, radial_rows, w_radial,
        scratch=[pltpu.VMEM((2 * C, C), f32)],
        name="update",
    )
    parts = [swap(values, "dom", 2 * (part + 1)) for part, values in enumerate(sends)]
    updated, token = call(
        updated_kernel, [((ATOMS, C), bf16), ((8, C), f32)], own_rows, act, w_out, after=[sends[0]], name="updated"
    )
    joined, kept = call(
        join_kernel,
        [((HALF + 8 * GHOST + PART + 16, C), bf16), ((PART, C), f32)],
        back_rows, quarter, radial, *parts,
        scratch=[pltpu.VMEM((QUARTER, C), f32)],
        after=[token],
        name="join",
    )
    received = swap(joined, "dom", 1)
    (near_sums,) = call(back_near_kernel, [((2 * KB, C), f32)], near, joined, name="back_near")
    message_up, message_down, over, back_down, back_up = call(
        back_far_kernel,
        [
            ((2 * KB + PART + 16 + GHOST, C), bf16), ((2 * KB + PART + 16 + GHOST, C), bf16),
            ((2 * KB + PART + 16, C), bf16),
            ((GHOST, C), bf16), ((GHOST, C), bf16),
        ],
        far, received, joined, kept, near_sums,
        scratch=[pltpu.VMEM((16 * GHOST, C), bf16)],
        name="back_far",
    )
    (near_column,) = call(
        collect_kernel, [((COLUMN * NEAR, C), bf16)], pair, other_pair, after=[over], name="collect"
    )
    far_column = swap(near_column, "dom", 1)
    column_shapes = [((COLUMN * HALF, 2 * KB), bf16), ((COLUMN * HALF, C), f32), ((C, COLUMN * HALF), bf16)]
    near_table, near_column_gain, near_turned = call(
        column_tables_kernel, column_shapes, near_column, wave_vectors, species_gain, after=[over], name="near_tables"
    )
    far_table, far_column_gain, far_turned = call(
        column_tables_kernel, column_shapes, far_column, wave_vectors, species_gain, after=[over], name="far_tables"
    )
    sums = over
    up, down, over = from_y(message_up, 1), from_y(message_down, -1), from_y(over, 2)
    send, keep, early, field = call(
        charge_back_kernel,
        [((HALF, C), bf16), ((HALF, C), f32), ((PART + 16, C), bf16), ((2 * KB, C), bf16)],
        sums, up, down, over, filt, near, far, near_gain, far_gain,
        after=[near_column_gain, far_column_gain],
        name="charge_back",
    )
    received = swap(send, "dom", 1)
    (message,) = call(
        charge_kernel,
        [((C + PART + 16, C), bf16)],
        field, early, near_table, near_column_gain, near_turned, far_table, far_column_gain, far_turned,
        after=[send],
        name="charge",
    )
    other = swap(message, ("cell", "dom"), DOMS + 6)
    held, grads, *sends = call(
        tail_spread_kernel,
        [((ATOMS, C), f32), ((C + PART + 16, C), bf16)] + [((ATOMS + C + PART, C), bf16)] * 3,
        keep, received, message, other,
        name="tail_spread",
    )
    parts = [swap(values, "dom", 2 * (part + 1)) for part, values in enumerate(sends)]
    raw, message = call(
        raw_kernel, [((ATOMS, C), bf16), ((2 * C + 16, C), bf16)], held, grads, *parts, name="raw"
    )
    parts = [swap(message, "cell", mask) for mask in (2, 4, 6)]
    feat_grad, token = call(
        feature_kernel,
        [((ATOMS, C), bf16), ((8, C), f32)],
        raw, w_charge, own_total, ghost_down, ghost_up, back_down, back_up, up, down,
        after=[message],
        name="feature",
    )
    (total,) = call(cell_sum_kernel, [((2 * C + 16, C), f32)], message, *parts, after=[token], name="cell_sum")
    charge, message, radial, out = call(
        weights_kernel,
        [((C, C), f32), ((C, C), f32), ((NB, C), f32), ((C, C), f32)],
        total, swap(total, "dom", 1),
        name="weights",
    )
    return updated[None], feat_grad[None], charge, message, radial, out


def solution(mesh):
    placed = (
        P("cell", "dom", None),
        P("cell", None, "dom"),
        P("cell", "dom"),
        P(),
        P(),
        P(),
        P(),
        P(),
        P(),
        P(),
        P("cell", "dom"),
        P("cell", "dom"),
        P("cell", "dom"),
        P("cell", "dom"),
        P("cell", "dom"),
        P("cell", "dom"),
        P("cell", "dom", None),
    )
    return jax.shard_map(
        per_device,
        mesh=mesh,
        in_specs=placed,
        out_specs=(P("cell", "dom", None), P("cell", "dom", None), P(), P(), P(), P()),
        check_vma=False,
    )
```
